32 devices in a mesh: grp: 2 (over y), pair: 4 (over z), orb: 4 (over x, core).
Axes of the slice: x: 2, y: 2, z: 4, core: 2. Of those that a mesh axis runs over, the one named last changes fastest.
Arguments:
- integrals: bfloat16 [64, 8, 4096], P(('grp', 'pair', 'orb')), parts along dimension 0, may hold values from -6 to 6
- mu_block: int32 [64], P(('grp', 'pair', 'orb')), parts along dimension 0, may hold values from 0 to 31, as said below
- nu_block: int32 [64], P(('grp', 'pair', 'orb')), parts along dimension 0, may hold values from 0 to 31
- counts: int32 [32], P(('grp', 'pair', 'orb')), parts along dimension 0, may hold values from 1 to 2
- coeff: bfloat16 [4096, 512], P(('grp', 'pair', 'orb')), parts along dimension 0, may hold values from -0.125 to 0.125
Outputs:
- transformed: float32 [1024, 8, 512], P(('grp', 'orb'), 'pair'), parts along dimension 0
The draws below stay inside these ranges and needn't reach their ends.
There are 2 independent parts, one for each index of `grp`. The reference program is written for one: setup_inputs(seed, part) draws one part's arguments, and reference() takes and returns one part's arrays. A program takes and returns all parts, laid end to end along the dimension named above; each array names one. Nothing has to cross between parts.
Inputs may be any that keep to these rules, and one draw needn't show every extreme that they name: mu_block and nu_block together name distinct pairs of shell blocks. `counts`: slots of a device beyond its count hold arbitrary values, which must be ignored.
All inputs are finite; a program needn't handle non-finite values.
Results may differ from the reference program's by a relative error of at most 0.0029.
Values may be sent and summed in bfloat16 or wider, within the bound.
No kernel may reach another device: no remote copies, remote signals or barrier semaphores. Data moves between devices by JAX's collectives and lax.ppermute only.
A program may use at most 64 MiB of HBM per device.

```python
import jax
import jax.numpy as jnp
from jax import lax

SB = 64
NB = 2048
NI = 512
NBLK_DEV = 2
NSB = 32
KTOT = 8
TILES = 32
N_PAIR = 4
N_ORB = 4


def pair_list(key):
    return jax.random.permutation(key, NSB * NSB)[:TILES].astype(jnp.int32)


def draw_mu_block(key, part):
    listed = pair_list(key)
    return listed // NSB


def draw_nu_block(key, part):
    listed = pair_list(key)
    return listed % NSB


def touch_ends(array, key, smallest, top_value):
    longest = array.shape.index(max(array.shape))
    spots = []
    for shift in (0, 1):
        where = [jax.random.randint(jax.random.fold_in(key, axis), (), 0, length) for axis, length in enumerate(array.shape)]
        where[longest] = (where[longest] + shift) % array.shape[longest]
        spots.append(tuple(where))
    return array.at[spots[0]].set(smallest).at[spots[1]].set(top_value)


def block_scale(key, extent, cuts, smallest, top_value):
    def one(position, blocks):
        draws = jax.random.uniform(jax.random.fold_in(jax.random.fold_in(key, 6), position), (blocks,), jnp.float32, smallest / len(cuts), top_value / len(cuts))
        return jnp.repeat(jnp.exp(draws), extent[position] // blocks).reshape((-1,) + (1,) * (len(extent) - position - 1))

    factor_of = one(*cuts[0])
    for cut in cuts[1:]:
        factor_of = factor_of * one(*cut)
    return factor_of


def centred(stream_key, shape, deviation, reach, shards=(), held_as=jnp.bfloat16):
    level = block_scale(stream_key, shape, shards, -0.22, 0.18) if shards else 1.0
    drawn = jax.random.normal(stream_key, shape, jnp.float32) * deviation * level
    return jnp.minimum(jnp.maximum(drawn, -reach), reach).astype(held_as)


def setup_inputs(seed: int = 0, part: int = 0) -> dict:
    seeds = jax.random.split(jax.random.key(seed), 6)
    part_splits = jax.random.split(jax.random.fold_in(seeds[5], part), 6)
    integrals = centred(part_splits[0], (TILES, KTOT, SB * SB), 1.0, 6.0, ((0, 16),))
    mu_block = draw_mu_block(jax.random.fold_in(jax.random.fold_in(seeds[5], part), 71), part)
    nu_block = draw_nu_block(jax.random.fold_in(jax.random.fold_in(seeds[5], part), 71), part)
    counts = touch_ends(jax.random.randint(part_splits[3], (N_PAIR * N_ORB,), 1, NBLK_DEV + 1), jax.random.fold_in(part_splits[3], 1), 1, NBLK_DEV).astype(jnp.int32)
    coeff = centred(part_splits[4], (NB, NI), NB ** -0.5, 0.125, ((0, 16),))
    return {"integrals": integrals, "mu_block": mu_block, "nu_block": nu_block, "counts": counts, "coeff": coeff}


def reference(integrals, mu_block, nu_block, counts, coeff):
    slots = jnp.arange(TILES, dtype=jnp.int32)
    valid = (slots % NBLK_DEV < jnp.repeat(counts, NBLK_DEV)).astype(jnp.float32)
    blocks = coeff.astype(jnp.float32).reshape(NSB, SB, NI)

    def add_tile(summed, item):
        tile, mu_id, nu_id, keep = item
        rows = blocks[nu_id]
        square = tile.astype(jnp.float32).reshape(KTOT, SB, SB)
        half = jnp.einsum("kmn,ni->mki", square, rows)
        rounded = lax.optimization_barrier(half.astype(jnp.bfloat16))
        half_f = rounded.astype(jnp.float32) * keep
        return summed.at[mu_id].add(half_f), None

    start = jnp.zeros((NSB, SB, KTOT, NI), jnp.float32)
    summed, unused = lax.scan(add_tile, start, (integrals, mu_block, nu_block, valid))
    return jnp.einsum("bma,bmki->aki", blocks, summed, precision=lax.Precision.HIGHEST)
```

```python
import functools

import jax
import jax.numpy as jnp
from jax import lax
from jax.experimental import pallas as pl
from jax.experimental.pallas import tpu as pltpu
from jax.sharding import PartitionSpec as P

SB = 64
LANES = 128
CHUNK = 16


def transform_kernel(c_rows, x_devs, n_c, n_x, *refs):
    where, mu, nu, keep = refs[:4]
    c_in, x_in = refs[4 : 4 + n_c], refs[4 + n_c : 4 + n_c + n_x]
    out, c_all, x_all, half, left, sems = refs[4 + n_c + n_x :]
    copies = []
    for q, piece in enumerate(c_in):
        rows = pl.ds(pl.multiple_of(where[q] * c_rows, c_rows), c_rows)
        copies.append(pltpu.make_async_copy(piece, c_all.at[rows], sems.at[q]))
    for q, piece in enumerate(x_in):
        place = pl.ds(where[n_c + q] * x_devs, x_devs)
        copies.append(pltpu.make_async_copy(piece, x_all.at[place], sems.at[n_c + q]))
    for copy in copies:
        copy.start()
    for copy in copies:
        copy.wait()

    mine = pl.ds(pl.multiple_of(where[n_c + n_x] * LANES, LANES), LANES)
    lane = lax.broadcasted_iota(jnp.int32, (2 * SB, LANES), 1)
    devices = x_all.shape[0]
    chunks = devices // CHUNK

    def rows_of(block):
        return pl.ds(pl.multiple_of(block * SB, SB), SB)

    def chunk_step(chunk, carry):
        for d in range(CHUNK):
            device = chunk * CHUNK + d
            first, second = 2 * device, 2 * device + 1
            tile = x_all[device]
            one = jnp.where(lane < SB * keep[first], tile, jnp.zeros_like(tile))
            two = jnp.where(lane >= LANES - SB * keep[second], tile, jnp.zeros_like(tile))
            one = jnp.where(lane < SB, one, jnp.zeros_like(tile))
            two = jnp.where(lane >= SB, two, jnp.zeros_like(tile))
            rows = jnp.concatenate([c_all[rows_of(nu[first])], c_all[rows_of(nu[second])]], 0)
            stacked = jnp.concatenate([one[:SB], two[:SB], one[SB:], two[SB:]], 0)
            moved = jnp.dot(stacked, rows, preferred_element_type=jnp.float32)
            moved = moved.astype(jnp.bfloat16)
            at = pl.ds(d * 2 * SB, 2 * SB)
            half[0, at] = moved[: 2 * SB]
            half[1, at] = moved[2 * SB :]
            left[at, :] = jnp.concatenate([c_all[rows_of(mu[first]), mine], c_all[rows_of(mu[second]), mine]], 0)
        for k in range(2):
            part = lax.dot_general(
                left[...], half[k], (((0,), (0,)), ((), ())), preferred_element_type=jnp.float32
            )
            for j in range(part.shape[1] // LANES):
                at = pl.ds(2 * j + k, part.shape[0], stride=2 * (part.shape[1] // LANES))
                value = part[:, j * LANES : (j + 1) * LANES]
                if chunks == 1:
                    out[at, :] = value
                else:
                    out[at, :] = jnp.where(chunk == 0, value, value + out[at, :])
        return carry

    if chunks == 1:
        chunk_step(0, 0)
    else:
        out[...] = jnp.zeros_like(out)
        lax.fori_loop(0, chunks, chunk_step, 0)


def transform(c_pieces, c_at, x_pieces, x_at, mine, mu, nu, keep):
    c_rows, orbitals = c_pieces[0].shape
    x_devs = x_pieces[0].shape[0]
    n_c, n_x = len(c_pieces), len(x_pieces)
    devices = x_devs * n_x
    where = jnp.stack(c_at + x_at + [mine]).astype(jnp.int32)
    smem = pl.BlockSpec(memory_space=pltpu.SMEM)
    hbm = pl.BlockSpec(memory_space=pl.ANY)
    wide = CHUNK * 2 * SB
    out = pl.pallas_call(
        functools.partial(transform_kernel, c_rows, x_devs, n_c, n_x),
        out_shape=jax.ShapeDtypeStruct((2 * orbitals // 4 // LANES * orbitals, LANES), jnp.float32),
        in_specs=[smem] * 4 + [hbm] * (n_c + n_x),
        out_specs=pl.BlockSpec(memory_space=pltpu.VMEM),
        scratch_shapes=[
            pltpu.VMEM((c_rows * n_c, orbitals), jnp.bfloat16),
            pltpu.VMEM((devices, LANES, LANES), jnp.bfloat16),
            pltpu.VMEM((2, wide, orbitals), jnp.bfloat16),
            pltpu.VMEM((wide, LANES), jnp.bfloat16),
            pltpu.SemaphoreType.DMA((n_c + n_x,)),
        ],
        compiler_params=pltpu.CompilerParams(vmem_limit_bytes=40 << 20),
        name="transform",
    )(where, mu, nu, keep, *c_pieces, *x_pieces)
    return out


def shift(array, axis, size, step):
    return lax.ppermute(array, axis, [(i, (i + step) % size) for i in range(size)])


def flip(array, axis, size, bit):
    return lax.ppermute(array, axis, [(i, i ^ bit) for i in range(size)])


def body(n_pair, n_orb, integrals, mu_block, nu_block, counts, coeff):
    p, o = lax.axis_index("pair"), lax.axis_index("orb")
    slots = integrals.shape[0]
    columns = integrals.shape[1] // n_pair
    everyone = ("pair", "orb")

    tiles = integrals.reshape(slots, n_pair, columns, SB, SB).transpose(1, 2, 3, 0, 4)
    tiles = tiles.reshape(n_pair, columns * SB, slots * SB)
    kept = (jnp.arange(slots, dtype=jnp.int32) < counts[0]).astype(jnp.int32)
    index = jnp.stack([jnp.where(kept > 0, mu_block, 0), jnp.where(kept > 0, nu_block, 0), kept])
    index = index.reshape(1, 3 * slots)

    arrived = None
    if n_pair * n_orb <= 16:
        lines = [coeff] + [shift(coeff, "pair", n_pair, s) for s in range(1, n_pair)]
        c_pieces, c_at = [], []
        for s, line in enumerate(lines):
            source = (p - s) % n_pair
            across = flip(line, "orb", n_orb, 2)
            for far, piece in ((0, line), (2, across)):
                c_pieces += [piece, flip(piece, "orb", n_orb, 1)]
                c_at += [source * n_orb + (o ^ far), source * n_orb + (o ^ far ^ 1)]
        line = lax.all_to_all(tiles, "pair", split_axis=0, concat_axis=0, tiled=True)
        across = flip(line, "orb", n_orb, 2)
        x_pieces = [line, flip(line, "orb", n_orb, 1), across, flip(across, "orb", n_orb, 1)]
        x_at = [o, o ^ 1, o ^ 2, o ^ 3]
        spread = jnp.broadcast_to(index, (n_pair * n_orb, 3 * slots))
        table = lax.all_to_all(spread, everyone, split_axis=0, concat_axis=0, tiled=True)
    else:
        c_pieces, c_at = [lax.all_gather(coeff, everyone, axis=0, tiled=True)], [p * 0]
        line = lax.all_to_all(tiles, "pair", split_axis=0, concat_axis=0, tiled=True)
        whole = lax.all_gather(line, "orb", axis=0, tiled=True)
        x_pieces, x_at = [whole], [p * 0]
        table = lax.all_gather(index, everyone, axis=0, tiled=True)
    table = table.reshape(n_pair, n_orb, 3, slots).transpose(2, 1, 0, 3).reshape(3, -1)
    out = transform(c_pieces, c_at, x_pieces, x_at, o, table[0], table[1], table[2])
    orbitals = coeff.shape[1]
    out = out.reshape(orbitals // n_orb, orbitals // LANES, columns, LANES)
    return out.transpose(0, 2, 1, 3).reshape(orbitals // n_orb, columns, orbitals)


def solution(mesh):
    placed = (
        P(("grp", "pair", "orb"), None, None),
        P(("grp", "pair", "orb")),
        P(("grp", "pair", "orb")),
        P(("grp", "pair", "orb")),
        P(("grp", "pair", "orb"), None),
    )
    return jax.shard_map(
        functools.partial(body, mesh.shape["pair"], mesh.shape["orb"]),
        mesh=mesh,
        in_specs=placed,
        out_specs=P(("grp", "orb"), "pair", None),
        check_vma=False,
    )
```

```python
import functools

import jax
import jax.numpy as jnp
from jax import lax
from jax.experimental import pallas as pl
from jax.experimental.pallas import tpu as pltpu
from jax.sharding import PartitionSpec as P

SB = 64
LANES = 128
TAG = 16
CHUNK = 16


def pack_kernel(n_pair, integrals, mu, nu, counts, coeff, *refs):
    outs, spread, woven = refs[:n_pair], refs[n_pair], refs[n_pair + 1]
    p = lax.axis_index("pair")
    slots, kets, flat = integrals.shape
    wide = flat // LANES
    columns = kets // n_pair
    rows, orbitals = coeff.shape
    blocks = orbitals // LANES
    for t in range(slots):
        for j in range(wide):
            at = pl.ds((t * wide + j) * kets, kets)
            spread[at, :] = integrals[t, :, j * LANES : (j + 1) * LANES].astype(jnp.float32)
    lane = lax.broadcasted_iota(jnp.int32, (wide, LANES), 1)
    low, kept = lane < SB, lane < SB * counts[0]
    lane = lax.broadcasted_iota(jnp.int32, (TAG, LANES), 1)
    tag = jnp.zeros((TAG, LANES), jnp.int32)
    for t in range(slots):
        tag = jnp.where((lane == 2 * t) & (t < counts[0]), mu[t], tag)
        tag = jnp.where((lane == 2 * t + 1) & (t < counts[0]), nu[t], tag)
    tag = tag.astype(jnp.float32).astype(jnp.bfloat16)
    for s in range(n_pair):
        dest = lax.rem(p + s, n_pair)
        for k in range(columns):
            column = dest * columns + k
            one = spread[pl.ds(column, wide, stride=kets), :]
            two = spread[pl.ds(wide * kets + column, wide, stride=kets), :]
            even = jnp.where(low, one, pltpu.roll(two, SB, axis=1))
            odd = jnp.where(low, pltpu.roll(one, SB, axis=1), two)
            start = (s * columns + k) * SB
            woven[pl.ds(start, wide, stride=2), :] = jnp.where(kept, even, 0.0)
            woven[pl.ds(start + 1, wide, stride=2), :] = jnp.where(kept, odd, 0.0)
        for j in range(blocks):
            outs[s][pl.ds(j * rows, rows), :] = coeff[:, j * LANES : (j + 1) * LANES]
        tile = woven[pl.ds(s * columns * SB, columns * SB), :]
        outs[s][pl.ds(blocks * rows, columns * SB), :] = tile.astype(jnp.bfloat16)
        outs[s][pl.ds(blocks * rows + columns * SB, TAG), :] = tag


def pack(n_pair, integrals, mu, nu, counts, coeff):
    slots, kets, flat = integrals.shape
    rows, orbitals = coeff.shape
    total = orbitals // LANES * rows + kets // n_pair * SB + TAG
    smem = pl.BlockSpec(memory_space=pltpu.SMEM)
    vmem = pl.BlockSpec(memory_space=pltpu.VMEM)
    return pl.pallas_call(
        functools.partial(pack_kernel, n_pair),
        out_shape=[jax.ShapeDtypeStruct((total, LANES), jnp.bfloat16)] * n_pair,
        in_specs=[vmem, smem, smem, smem, vmem],
        out_specs=[vmem] * n_pair,
        scratch_shapes=[
            pltpu.VMEM((slots * kets * flat // LANES, LANES), jnp.float32),
            pltpu.VMEM((kets * SB, LANES), jnp.float32),
        ],
        compiler_params=pltpu.CompilerParams(vmem_limit_bytes=16 << 20),
        name="pack",
    )(integrals, mu, nu, counts, coeff)


def transform_kernel(n_pair, n_orb, steps, sides, n_in, *refs):
    pieces = refs[:n_in]
    out, c_all, x_all, tags, codes, index, half, left, sems = refs[n_in:]
    p, o = lax.axis_index("pair"), lax.axis_index("orb")
    devices = x_all.shape[0]
    orbitals = c_all.shape[1]
    blocks = orbitals // LANES
    first_copies, copies = [], []
    if steps:
        rows = c_all.shape[0] // devices
        tile_at = blocks * rows
        for q, piece in enumerate(pieces):
            source = lax.rem(p + n_pair - steps[q], n_pair) * n_orb + (o ^ sides[q])
            place = pl.ds(pl.multiple_of(source * rows, rows), rows)
            for j in range(blocks):
                copies.append(
                    pltpu.make_async_copy(
                        piece.at[pl.ds(j * rows, rows), :],
                        c_all.at[place, pl.ds(j * LANES, LANES)],
                        sems.at[q, j],
                    )
                )
            copies.append(
                pltpu.make_async_copy(piece.at[pl.ds(tile_at, 2 * SB), :], x_all.at[q], sems.at[q, blocks])
            )
            first_copies.append(
                pltpu.make_async_copy(piece.at[pl.ds(tile_at + 2 * SB, TAG), :], tags.at[q], sems.at[q, blocks + 1])
            )
    else:
        whole, coeff = pieces
        copies = [
            pltpu.make_async_copy(coeff, c_all, sems.at[0, 0]),
            pltpu.make_async_copy(whole.at[:, pl.ds(0, 2 * SB), :], x_all, sems.at[0, 1]),
        ]
        first_copies = [pltpu.make_async_copy(whole.at[:, pl.ds(2 * SB, TAG), :], tags, sems.at[0, 2])]
    for copy in first_copies + copies:
        copy.start()
    for copy in first_copies:
        copy.wait()
    codes[...] = tags[:, 0, :].astype(jnp.float32).astype(jnp.int32)
    to_scalars = pltpu.make_async_copy(codes, index, sems.at[0, blocks + 2])
    to_scalars.start()
    to_scalars.wait()
    for copy in copies:
        copy.wait()

    mine = pl.ds(pl.multiple_of(o * LANES, LANES), LANES)
    low = lax.broadcasted_iota(jnp.int32, (2 * SB, LANES), 1) < SB
    chunks = devices // CHUNK

    def rows_of(block):
        return pl.ds(pl.multiple_of(block * SB, SB), SB)

    def chunk_step(chunk, carry):
        for d in range(CHUNK):
            device = chunk * CHUNK + d
            tile = x_all[device]
            one = jnp.where(low, tile, jnp.zeros_like(tile))
            two = jnp.where(low, jnp.zeros_like(tile), tile)
            mu_one, nu_one, mu_two, nu_two = (index[device, n] for n in range(4))
            rows = jnp.concatenate([c_all[rows_of(nu_one)], c_all[rows_of(nu_two)]], 0)
            stacked = jnp.concatenate([one[:SB], two[:SB], one[SB:], two[SB:]], 0)
            moved = jnp.dot(stacked, rows, preferred_element_type=jnp.float32)
            moved = moved.astype(jnp.bfloat16)
            at = pl.ds(d * 2 * SB, 2 * SB)
            half[at, :orbitals] = moved[: 2 * SB]
            half[at, orbitals:] = moved[2 * SB :]
            left[at, :] = jnp.concatenate([c_all[rows_of(mu_one), mine], c_all[rows_of(mu_two), mine]], 0)
        part = lax.dot_general(
            left[...], half[...], (((0,), (0,)), ((), ())), preferred_element_type=jnp.float32
        )
        for k in range(2):
            for j in range(blocks):
                at = pl.ds(2 * j + k, LANES, stride=2 * blocks)
                begin = k * orbitals + j * LANES
                value = part[:, begin : begin + LANES]
                out[at, :] = value if chunks == 1 else out[at, :] + value
        return carry

    if chunks == 1:
        chunk_step(0, 0)
    else:
        out[...] = jnp.zeros_like(out)
        lax.fori_loop(0, chunks, chunk_step, 0)


def transform(n_pair, n_orb, steps, sides, pieces, rows_all, orbitals):
    devices = n_pair * n_orb
    wide = CHUNK * 2 * SB
    return pl.pallas_call(
        functools.partial(transform_kernel, n_pair, n_orb, steps, sides, len(pieces)),
        out_shape=jax.ShapeDtypeStruct((2 * orbitals // LANES * LANES, LANES), jnp.float32),
        in_specs=[pl.BlockSpec(memory_space=pl.ANY)] * len(pieces),
        out_specs=pl.BlockSpec(memory_space=pltpu.VMEM),
        scratch_shapes=[
            pltpu.VMEM((rows_all, orbitals), jnp.bfloat16),
            pltpu.VMEM((devices, 2 * SB, LANES), jnp.bfloat16),
            pltpu.VMEM((devices, TAG, LANES), jnp.bfloat16),
            pltpu.VMEM((devices, LANES), jnp.int32),
            pltpu.SMEM((devices, LANES), jnp.int32),
            pltpu.VMEM((wide, 2 * orbitals), jnp.bfloat16),
            pltpu.VMEM((wide, LANES), jnp.bfloat16),
            pltpu.SemaphoreType.DMA((len(pieces), orbitals // LANES + 3)),
        ],
        compiler_params=pltpu.CompilerParams(vmem_limit_bytes=40 << 20),
        name="transform",
    )(*pieces)


def shift(array, axis, size, step):
    return lax.ppermute(array, axis, [(i, (i + step) % size) for i in range(size)])


def flip(array, axis, size, bit):
    return lax.ppermute(array, axis, [(i, i ^ bit) for i in range(size)])


def body(n_pair, n_orb, integrals, mu_block, nu_block, counts, coeff):
    slots, kets, flat = integrals.shape
    columns = kets // n_pair
    orbitals = coeff.shape[1]
    everyone = ("pair", "orb")
    if n_pair * n_orb <= 16:
        packed = pack(n_pair, integrals, mu_block, nu_block, counts, coeff)
        pieces, steps, sides = [], [], []
        for s in range(n_pair):
            line = shift(packed[s], "pair", n_pair, s) if s else packed[0]
            across = flip(line, "orb", n_orb, 2)
            pieces += [line, flip(line, "orb", n_orb, 1), across, flip(across, "orb", n_orb, 1)]
            steps += [s] * 4
            sides += [0, 1, 2, 3]
    else:
        kept = jnp.arange(slots, dtype=jnp.int32) < counts[0]
        tiles = jnp.where(kept[:, None, None], integrals, jnp.zeros_like(integrals))
        tiles = tiles.reshape(slots, n_pair, columns, SB, SB).transpose(1, 2, 3, 0, 4)
        tiles = tiles.reshape(n_pair, columns * SB, slots * SB)
        tag = jnp.where(kept[:, None], jnp.stack([mu_block, nu_block], 1), 0).reshape(-1)
        tag = jnp.zeros((n_pair, TAG, LANES), jnp.bfloat16).at[:, :, : 2 * slots].set(tag.astype(jnp.bfloat16))
        packed = jnp.concatenate([tiles, tag], 1)
        line = lax.all_to_all(packed, "pair", split_axis=0, concat_axis=0, tiled=True)
        pieces = [lax.all_gather(line, "orb", axis=0, tiled=True), lax.all_gather(coeff, everyone, axis=0, tiled=True)]
        steps, sides = None, None
    out = transform(n_pair, n_orb, steps, sides, pieces, coeff.shape[0] * n_pair * n_orb, orbitals)
    out = out.reshape(orbitals // n_orb, orbitals // LANES, columns, LANES)
    return out.transpose(0, 2, 1, 3).reshape(orbitals // n_orb, columns, orbitals)


def solution(mesh):
    placed = (
        P(("grp", "pair", "orb"), None, None),
        P(("grp", "pair", "orb")),
        P(("grp", "pair", "orb")),
        P(("grp", "pair", "orb")),
        P(("grp", "pair", "orb"), None),
    )
    return jax.shard_map(
        functools.partial(body, mesh.shape["pair"], mesh.shape["orb"]),
        mesh=mesh,
        in_specs=placed,
        out_specs=P(("grp", "orb"), "pair", None),
        check_vma=False,
    )
```

```python
import functools

import jax
import jax.numpy as jnp
from jax import lax
from jax.experimental import pallas as pl
from jax.experimental.pallas import tpu as pltpu
from jax.sharding import PartitionSpec as P

SB = 64
LANES = 128
GROUP = 16
CHUNK = 16


def pack_kernel(n_pair, integrals, mu, nu, counts, coeff, *refs):
    outs = refs[:n_pair]
    tiles, shard, mu_in, nu_in, spread, woven, sems = refs[n_pair:]
    copies = [
        pltpu.make_async_copy(source, target, sems.at[n])
        for n, (source, target) in enumerate(
            ((integrals, tiles), (coeff, shard), (mu, mu_in), (nu, nu_in))
        )
    ]
    for copy in copies:
        copy.start()
    p = lax.axis_index("pair")
    slots, kets, flat = tiles.shape
    wide = flat // LANES
    columns = kets // n_pair
    rows, orbitals = shard.shape
    blocks = orbitals // LANES
    copies[0].wait()
    for t in range(slots):
        for j in range(wide):
            at = pl.ds((t * wide + j) * kets, kets)
            spread[at, :] = tiles[t, :, j * LANES : (j + 1) * LANES].astype(jnp.float32)
    for copy in copies[2:]:
        copy.wait()
    count = counts[0]
    lane = lax.broadcasted_iota(jnp.int32, (wide, LANES), 1)
    low, kept = lane < SB, lane < SB * count
    lane = lax.broadcasted_iota(jnp.int32, (GROUP, LANES), 1)
    tag = jnp.zeros((GROUP, LANES), jnp.int32)
    for t in range(slots):
        tag = jnp.where((lane == 2 * t) & (t < count), mu_in[t], tag)
        tag = jnp.where((lane == 2 * t + 1) & (t < count), nu_in[t], tag)
    tag = tag.astype(jnp.float32).astype(jnp.bfloat16)
    tile_at = rows // GROUP * blocks
    for s in range(n_pair):
        dest = lax.rem(p + s, n_pair)
        for k in range(columns):
            column = dest * columns + k
            one = spread[pl.ds(column, wide, stride=kets), :]
            two = spread[pl.ds(wide * kets + column, wide, stride=kets), :]
            even = jnp.where(low, one, pltpu.roll(two, SB, axis=1))
            odd = jnp.where(low, pltpu.roll(one, SB, axis=1), two)
            begin = (s * columns + k) * SB
            woven[pl.ds(begin, wide, stride=2), :] = jnp.where(kept, even, 0.0)
            woven[pl.ds(begin + 1, wide, stride=2), :] = jnp.where(kept, odd, 0.0)
        tiled = columns * SB // GROUP
        for g in range(tiled):
            rows_at = pl.ds((s * tiled + g) * GROUP, GROUP)
            outs[s][tile_at + g] = woven[rows_at, :].astype(jnp.bfloat16)
        outs[s][tile_at + tiled] = tag
    copies[1].wait()
    for g in range(rows // GROUP):
        for j in range(blocks):
            group = shard[g * GROUP : (g + 1) * GROUP, j * LANES : (j + 1) * LANES]
            for s in range(n_pair):
                outs[s][g * blocks + j] = group


def pack(n_pair, integrals, mu, nu, counts, coeff):
    slots, kets, flat = integrals.shape
    rows, orbitals = coeff.shape
    groups = rows // GROUP * (orbitals // LANES) + kets // n_pair * SB // GROUP + 1
    hbm = pl.BlockSpec(memory_space=pltpu.HBM)
    return pl.pallas_call(
        functools.partial(pack_kernel, n_pair),
        out_shape=[jax.ShapeDtypeStruct((groups, GROUP, LANES), jnp.bfloat16)] * n_pair,
        in_specs=[hbm, hbm, hbm, pl.BlockSpec(memory_space=pltpu.SMEM), hbm],
        out_specs=[pl.BlockSpec(memory_space=pltpu.VMEM)] * n_pair,
        scratch_shapes=[
            pltpu.VMEM(integrals.shape, jnp.bfloat16),
            pltpu.VMEM(coeff.shape, jnp.bfloat16),
            pltpu.SMEM(mu.shape, jnp.int32),
            pltpu.SMEM(nu.shape, jnp.int32),
            pltpu.VMEM((slots * kets * flat // LANES, LANES), jnp.float32),
            pltpu.VMEM((kets * SB, LANES), jnp.float32),
            pltpu.SemaphoreType.DMA((4,)),
        ],
        compiler_params=pltpu.CompilerParams(vmem_limit_bytes=60 << 20),
        name="pack",
    )(integrals, mu, nu, counts, coeff)


def transform_kernel(n_pair, n_orb, steps, sides, blocks, n_in, *refs):
    pieces = refs[:n_in]
    out, *held = refs[n_in:-6]
    codes, index, half, left, sems, tag_sem = refs[-6:]
    p, o = lax.axis_index("pair"), lax.axis_index("orb")
    devices = codes.shape[0]
    orbitals = blocks * LANES
    tiled = 2 * SB // GROUP
    in_block = SB // GROUP * blocks
    if steps:
        (together,) = held
        per = together.shape[0] // devices
        copies = []
        for q, piece in enumerate(pieces):
            source = lax.rem(p + n_pair - steps[q], n_pair) * n_orb + (o ^ sides[q])
            copies.append(pltpu.make_async_copy(piece, together.at[pl.ds(source * per, per)], sems.at[q]))
        tiles, spacing, tile_at = together, per, per - tiled - 1
        coeffs, per_dev = together, tile_at // in_block

        def block_at(block):
            return lax.div(block, per_dev) * per + lax.rem(block, per_dev) * in_block
    else:
        tiles, coeffs = held
        spacing, tile_at = tiled + 1, 0
        copies = [pltpu.make_async_copy(piece, target, sems.at[q]) for q, (piece, target) in enumerate(zip(pieces, held))]

        def block_at(block):
            return block * in_block

    for copy in copies:
        copy.start()
    for copy in copies:
        copy.wait()
    for d in range(devices):
        codes[d : d + 1, :] = tiles[d * spacing + tile_at + tiled][:1].astype(jnp.float32).astype(jnp.int32)
    to_scalars = pltpu.make_async_copy(codes, index, tag_sem)
    to_scalars.start()
    to_scalars.wait()

    low = lax.broadcasted_iota(jnp.int32, (SB, LANES), 1) < SB
    chunks = devices // CHUNK

    def block_rows(block):
        at = block_at(block)
        return jnp.concatenate(
            [
                jnp.concatenate([coeffs[at + g * blocks + j] for j in range(blocks)], 1)
                for g in range(SB // GROUP)
            ],
            0,
        )

    def block_mine(block):
        at = block_at(block) + o
        return jnp.concatenate([coeffs[at + g * blocks] for g in range(SB // GROUP)], 0)

    def chunk_step(chunk, carry):
        for d in range(CHUNK):
            device = chunk * CHUNK + d
            at = device * spacing + tile_at
            stacked = []
            for k in range(2):
                begin = at + k * (SB // GROUP)
                tile = jnp.concatenate([tiles[begin + g] for g in range(SB // GROUP)], 0)
                stacked += [jnp.where(low, tile, jnp.zeros_like(tile)), jnp.where(low, jnp.zeros_like(tile), tile)]
            mu_one, nu_one, mu_two, nu_two = (index[device, n] for n in range(4))
            rows = jnp.concatenate([block_rows(nu_one), block_rows(nu_two)], 0)
            moved = jnp.dot(jnp.concatenate(stacked, 0), rows, preferred_element_type=jnp.float32)
            moved = moved.astype(jnp.bfloat16)
            at = pl.ds(d * 2 * SB, 2 * SB)
            half[at, :orbitals] = moved[: 2 * SB]
            half[at, orbitals:] = moved[2 * SB :]
            left[at, :] = jnp.concatenate([block_mine(mu_one), block_mine(mu_two)], 0)
        part = lax.dot_general(
            left[...], half[...], (((0,), (0,)), ((), ())), preferred_element_type=jnp.float32
        )
        for k in range(2):
            for j in range(blocks):
                at = pl.ds(2 * j + k, LANES, stride=2 * blocks)
                begin = k * orbitals + j * LANES
                value = part[:, begin : begin + LANES]
                out[at, :] = value if chunks == 1 else out[at, :] + value
        return carry

    if chunks == 1:
        chunk_step(0, 0)
    else:
        out[...] = jnp.zeros_like(out)
        lax.fori_loop(0, chunks, chunk_step, 0)


def transform(n_pair, n_orb, steps, sides, pieces, orbitals):
    devices = n_pair * n_orb
    wide = CHUNK * 2 * SB
    if steps:
        held = [(sum(piece.shape[0] for piece in pieces), GROUP, LANES)]
    else:
        held = [piece.shape for piece in pieces]
    return pl.pallas_call(
        functools.partial(transform_kernel, n_pair, n_orb, steps, sides, orbitals // LANES, len(pieces)),
        out_shape=jax.ShapeDtypeStruct((2 * orbitals // LANES * LANES, LANES), jnp.float32),
        in_specs=[pl.BlockSpec(memory_space=pl.ANY)] * len(pieces),
        out_specs=pl.BlockSpec(memory_space=pltpu.VMEM),
        scratch_shapes=[pltpu.VMEM(shape, jnp.bfloat16) for shape in held]
        + [
            pltpu.VMEM((devices, LANES), jnp.int32),
            pltpu.SMEM((devices, LANES), jnp.int32),
            pltpu.VMEM((wide, 2 * orbitals), jnp.bfloat16),
            pltpu.VMEM((wide, LANES), jnp.bfloat16),
            pltpu.SemaphoreType.DMA((len(pieces),)),
            pltpu.SemaphoreType.DMA,
        ],
        compiler_params=pltpu.CompilerParams(vmem_limit_bytes=40 << 20),
        name="transform",
    )(*pieces)


def shift(array, axis, size, step):
    return lax.ppermute(array, axis, [(i, (i + step) % size) for i in range(size)])


def flip(array, axis, size, bit):
    return lax.ppermute(array, axis, [(i, i ^ bit) for i in range(size)])


def body(n_pair, n_orb, integrals, mu_block, nu_block, counts, coeff):
    slots, kets, flat = integrals.shape
    columns = kets // n_pair
    orbitals = coeff.shape[1]
    everyone = ("pair", "orb")
    if n_pair * n_orb == CHUNK and n_pair == 4:
        packed = pack(n_pair, integrals, mu_block, nu_block, counts, coeff)
        first = shift(packed[1], "pair", n_pair, 1)
        third = shift(packed[3], "pair", n_pair, 3)
        held_back, first = lax.optimization_barrier((packed[2], first))
        second = shift(held_back, "pair", n_pair, 2)
        pieces, steps, sides = [], [], []
        for s, line in enumerate([packed[0], first, second, third]):
            across = flip(line, "orb", n_orb, 2)
            pieces += [line, flip(line, "orb", n_orb, 1), across, flip(across, "orb", n_orb, 1)]
            steps += [s] * 4
            sides += [0, 1, 2, 3]
    else:
        kept = jnp.arange(slots, dtype=jnp.int32) < counts[0]
        tiles = jnp.where(kept[:, None, None], integrals, jnp.zeros_like(integrals))
        tiles = tiles.reshape(slots, n_pair, columns, SB, SB).transpose(1, 2, 3, 0, 4)
        tiles = tiles.reshape(n_pair, columns * SB, slots * SB)
        tag = jnp.where(kept[:, None], jnp.stack([mu_block, nu_block], 1), 0).reshape(-1)
        tag = jnp.zeros((n_pair, GROUP, LANES), jnp.bfloat16).at[:, :, : 2 * slots].set(tag.astype(jnp.bfloat16))
        packed = jnp.concatenate([tiles, tag], 1)
        line = lax.all_to_all(packed, "pair", split_axis=0, concat_axis=0, tiled=True)
        whole = lax.all_gather(line, "orb", axis=0, tiled=True)
        rows = lax.all_gather(coeff, everyone, axis=0, tiled=True)
        rows = rows.reshape(rows.shape[0] // GROUP, GROUP, orbitals // LANES, LANES).transpose(0, 2, 1, 3)
        pieces = [whole.reshape(-1, GROUP, LANES), rows.reshape(-1, GROUP, LANES)]
        steps, sides = None, None
    out = transform(n_pair, n_orb, steps, sides, pieces, orbitals)
    out = out.reshape(orbitals // n_orb, orbitals // LANES, columns, LANES)
    return out.transpose(0, 2, 1, 3).reshape(orbitals // n_orb, columns, orbitals)


def solution(mesh):
    placed = (
        P(("grp", "pair", "orb"), None, None),
        P(("grp", "pair", "orb")),
        P(("grp", "pair", "orb")),
        P(("grp", "pair", "orb")),
        P(("grp", "pair", "orb"), None),
    )
    return jax.shard_map(
        functools.partial(body, mesh.shape["pair"], mesh.shape["orb"]),
        mesh=mesh,
        in_specs=placed,
        out_specs=P(("grp", "orb"), "pair", None),
        check_vma=False,
    )
```

```python
import functools

import jax
import jax.numpy as jnp
from jax import lax
from jax.experimental import pallas as pl
from jax.experimental.pallas import tpu as pltpu
from jax.sharding import PartitionSpec as P

SB = 64
LANES = 128
GROUP = 16
CHUNK = 16


def pack_kernel(n_pair, integrals, mu, nu, counts, out, tiles, mu_in, nu_in, spread, woven, sems):
    copies = [
        pltpu.make_async_copy(source, target, sems.at[n])
        for n, (source, target) in enumerate(((integrals, tiles), (mu, mu_in), (nu, nu_in)))
    ]
    for copy in copies:
        copy.start()
    slots, kets, flat = tiles.shape
    wide = flat // LANES
    columns = kets // n_pair
    for copy in copies[1:]:
        copy.wait()
    count = counts[0]
    lane = lax.broadcasted_iota(jnp.int32, (wide, LANES), 1)
    low, kept = lane < SB, lane < SB * count
    lane = lax.broadcasted_iota(jnp.int32, (GROUP, LANES), 1)
    tag = jnp.zeros((GROUP, LANES), jnp.int32)
    for t in range(slots):
        tag = jnp.where((lane == 2 * t) & (t < count), mu_in[t], tag)
        tag = jnp.where((lane == 2 * t + 1) & (t < count), nu_in[t], tag)
    tag = tag.astype(jnp.float32).astype(jnp.bfloat16)
    copies[0].wait()
    for t in range(slots):
        for j in range(wide):
            at = pl.ds((t * wide + j) * kets, kets)
            spread[at, :] = tiles[t, :, j * LANES : (j + 1) * LANES].astype(jnp.float32)
    tiled = columns * SB // GROUP
    for dest in range(n_pair):
        for k in range(columns):
            column = dest * columns + k
            one = spread[pl.ds(column, wide, stride=kets), :]
            two = spread[pl.ds(wide * kets + column, wide, stride=kets), :]
            even = jnp.where(low, one, pltpu.roll(two, SB, axis=1))
            odd = jnp.where(low, pltpu.roll(one, SB, axis=1), two)
            begin = column * SB
            woven[pl.ds(begin, wide, stride=2), :] = jnp.where(kept, even, 0.0)
            woven[pl.ds(begin + 1, wide, stride=2), :] = jnp.where(kept, odd, 0.0)
        for g in range(tiled):
            rows_at = pl.ds((dest * tiled + g) * GROUP, GROUP)
            out[dest, g] = woven[rows_at, :].astype(jnp.bfloat16)
        out[dest, tiled] = tag


def pack(n_pair, integrals, mu, nu, counts):
    slots, kets, flat = integrals.shape
    groups = kets // n_pair * SB // GROUP + 1
    hbm, smem = pl.BlockSpec(memory_space=pltpu.HBM), pl.BlockSpec(memory_space=pltpu.SMEM)
    return pl.pallas_call(
        functools.partial(pack_kernel, n_pair),
        out_shape=jax.ShapeDtypeStruct((n_pair, groups, GROUP, LANES), jnp.bfloat16),
        in_specs=[hbm, hbm, hbm, smem],
        out_specs=pl.BlockSpec(memory_space=pltpu.VMEM),
        scratch_shapes=[
            pltpu.VMEM(integrals.shape, jnp.bfloat16),
            pltpu.SMEM(mu.shape, jnp.int32),
            pltpu.SMEM(nu.shape, jnp.int32),
            pltpu.VMEM((slots * kets * flat // LANES, LANES), jnp.float32),
            pltpu.VMEM((kets * SB, LANES), jnp.float32),
            pltpu.SemaphoreType.DMA((3,)),
        ],
        compiler_params=pltpu.CompilerParams(vmem_limit_bytes=60 << 20),
        name="pack",
    )(integrals, mu, nu, counts)


def transform_kernel(source_of, n_c, n_x, *refs):
    c_in, x_in = refs[:n_c], refs[n_c : n_c + n_x]
    out, c_all, x_all, tags, codes, index, half, left, sems = refs[n_c + n_x :]
    o = lax.axis_index("orb")
    devices = codes.shape[0]
    orbitals = c_all.shape[1]
    blocks = orbitals // LANES
    tiled = 2 * SB // GROUP
    early, late = [], []
    per = devices // n_x
    for q, piece in enumerate(x_in):
        place = pl.ds(q * per, per)
        early.append(pltpu.make_async_copy(piece.at[:, tiled], tags.at[place], sems.at[q]))
        late.append(pltpu.make_async_copy(piece.at[:, pl.ds(0, tiled)], x_all.at[place], sems.at[n_x + q]))
    for q, piece in enumerate(c_in):
        rows = c_all.shape[0] // n_c
        place = pl.ds(pl.multiple_of(source_of(q) * rows, rows), rows)
        late.append(pltpu.make_async_copy(piece, c_all.at[place], sems.at[2 * n_x + q]))
    for copy in early + late:
        copy.start()
    for copy in early:
        copy.wait()
    codes[...] = tags[:, 0, :].astype(jnp.float32).astype(jnp.int32)
    to_scalars = pltpu.make_async_copy(codes, index, sems.at[2 * n_x + n_c])
    to_scalars.start()
    to_scalars.wait()
    for copy in late:
        copy.wait()

    mine = pl.ds(pl.multiple_of(o * LANES, LANES), LANES)
    low = lax.broadcasted_iota(jnp.int32, (SB, LANES), 1) < SB
    chunks = devices // CHUNK

    def rows_of(block):
        return pl.ds(pl.multiple_of(block * SB, SB), SB)

    def chunk_step(chunk, carry):
        for d in range(CHUNK):
            device = chunk * CHUNK + d
            stacked = []
            for k in range(2):
                tile = jnp.concatenate([x_all[device, k * (tiled // 2) + g] for g in range(tiled // 2)], 0)
                stacked += [jnp.where(low, tile, jnp.zeros_like(tile)), jnp.where(low, jnp.zeros_like(tile), tile)]
            mu_one, nu_one, mu_two, nu_two = (index[device, n] for n in range(4))
            rows = jnp.concatenate([c_all[rows_of(nu_one)], c_all[rows_of(nu_two)]], 0)
            moved = jnp.dot(jnp.concatenate(stacked, 0), rows, preferred_element_type=jnp.float32)
            moved = moved.astype(jnp.bfloat16)
            at = pl.ds(d * 2 * SB, 2 * SB)
            half[at, :orbitals] = moved[: 2 * SB]
            half[at, orbitals:] = moved[2 * SB :]
            left[at, :] = jnp.concatenate([c_all[rows_of(mu_one), mine], c_all[rows_of(mu_two), mine]], 0)
        part = lax.dot_general(
            left[...], half[...], (((0,), (0,)), ((), ())), preferred_element_type=jnp.float32
        )
        for k in range(2):
            for j in range(blocks):
                at = pl.ds(2 * j + k, LANES, stride=2 * blocks)
                begin = k * orbitals + j * LANES
                value = part[:, begin : begin + LANES]
                out[at, :] = value if chunks == 1 else out[at, :] + value
        return carry

    if chunks == 1:
        chunk_step(0, 0)
    else:
        out[...] = jnp.zeros_like(out)
        lax.fori_loop(0, chunks, chunk_step, 0)


def transform(source_of, c_pieces, x_pieces):
    orbitals = c_pieces[0].shape[1]
    devices = sum(piece.shape[0] for piece in x_pieces)
    n_c, n_x = len(c_pieces), len(x_pieces)
    wide = CHUNK * 2 * SB
    return pl.pallas_call(
        functools.partial(transform_kernel, source_of, n_c, n_x),
        out_shape=jax.ShapeDtypeStruct((2 * orbitals // LANES * LANES, LANES), jnp.float32),
        in_specs=[pl.BlockSpec(memory_space=pl.ANY)] * (n_c + n_x),
        out_specs=pl.BlockSpec(memory_space=pltpu.VMEM),
        scratch_shapes=[
            pltpu.VMEM((c_pieces[0].shape[0] * n_c, orbitals), jnp.bfloat16),
            pltpu.VMEM((devices, 2 * SB // GROUP, GROUP, LANES), jnp.bfloat16),
            pltpu.VMEM((devices, GROUP, LANES), jnp.bfloat16),
            pltpu.VMEM((devices, LANES), jnp.int32),
            pltpu.SMEM((devices, LANES), jnp.int32),
            pltpu.VMEM((wide, 2 * orbitals), jnp.bfloat16),
            pltpu.VMEM((wide, LANES), jnp.bfloat16),
            pltpu.SemaphoreType.DMA((n_c + 2 * n_x + 1,)),
        ],
        compiler_params=pltpu.CompilerParams(vmem_limit_bytes=40 << 20),
        name="transform",
    )(*c_pieces, *x_pieces)


def flip(array, axis, size, bit):
    return lax.ppermute(array, axis, [(i, i ^ bit) for i in range(size)])


def around(n_pair, n_orb, core, step):
    length = 2 * n_pair
    far = n_orb // 2
    stops = [p * n_orb + core for p in range(n_pair)] + [p * n_orb + far + core for p in reversed(range(n_pair))]
    return [(stops[r], stops[(r + step) % length]) for r in range(length)]


def ring_source(n_pair, n_orb, step, flipped):
    p, o = lax.axis_index("pair"), lax.axis_index("orb")
    length = 2 * n_pair
    column = lax.div(o, 2)
    place = jnp.where(column == 0, p, length - 1 - p)
    place = lax.rem(place + length - step, length)
    second = (place >= n_pair).astype(jnp.int32)
    source = jnp.where(second == 1, length - 1 - place, place)
    return source * n_orb + 2 * second + (lax.rem(o, 2) ^ flipped)


def body(n_pair, n_orb, integrals, mu_block, nu_block, counts, coeff):
    slots, kets, flat = integrals.shape
    columns = kets // n_pair
    orbitals = coeff.shape[1]
    everyone = ("pair", "orb")
    if n_orb == 4 and n_pair <= 4:
        forward = around(n_pair, n_orb, 0, 1) + around(n_pair, n_orb, 1, 1)
        backward = [(b, a) for a, b in forward]
        held = {0: coeff}
        for step in range(1, n_pair + 1):
            held[step] = lax.ppermute(held[step - 1], everyone, forward)
            if step < n_pair:
                held[-step] = lax.ppermute(held[1 - step], everyone, backward)
        packed = pack(n_pair, integrals, mu_block, nu_block, counts)
        line = lax.all_to_all(packed, "pair", split_axis=0, concat_axis=0, tiled=True)
        across = flip(line, "orb", n_orb, 2)
        x_pieces = [line, flip(line, "orb", n_orb, 1), across, flip(across, "orb", n_orb, 1)]
        c_pieces, came = [], []
        for step, piece in held.items():
            c_pieces += [piece, flip(piece, "orb", n_orb, 1)]
            came += [(step % (2 * n_pair), 0), (step % (2 * n_pair), 1)]

        def source_of(q):
            return ring_source(n_pair, n_orb, *came[q])
    else:
        kept = jnp.arange(slots, dtype=jnp.int32) < counts[0]
        tiles = jnp.where(kept[:, None, None], integrals, jnp.zeros_like(integrals))
        tiles = tiles.reshape(slots, n_pair, columns, SB, SB).transpose(1, 2, 3, 0, 4)
        tiles = tiles.reshape(n_pair, columns * SB, slots * SB)
        tag = jnp.where(kept[:, None], jnp.stack([mu_block, nu_block], 1), 0).reshape(-1)
        tag = jnp.zeros((n_pair, GROUP, LANES), jnp.bfloat16).at[:, :, : 2 * slots].set(tag.astype(jnp.bfloat16))
        packed = jnp.concatenate([tiles, tag], 1).reshape(n_pair, -1, GROUP, LANES)
        line = lax.all_to_all(packed, "pair", split_axis=0, concat_axis=0, tiled=True)
        x_pieces = [lax.all_gather(line, "orb", axis=0, tiled=True)]
        c_pieces = [lax.all_gather(coeff, everyone, axis=0, tiled=True)]

        def source_of(q):
            return q
    out = transform(source_of, c_pieces, x_pieces)
    out = out.reshape(orbitals // n_orb, orbitals // LANES, columns, LANES)
    return out.transpose(0, 2, 1, 3).reshape(orbitals // n_orb, columns, orbitals)


def solution(mesh):
    placed = (
        P(("grp", "pair", "orb"), None, None),
        P(("grp", "pair", "orb")),
        P(("grp", "pair", "orb")),
        P(("grp", "pair", "orb")),
        P(("grp", "pair", "orb"), None),
    )
    return jax.shard_map(
        functools.partial(body, mesh.shape["pair"], mesh.shape["orb"]),
        mesh=mesh,
        in_specs=placed,
        out_specs=P(("grp", "orb"), "pair", None),
        check_vma=False,
    )
```

```python
import functools

import jax
import jax.numpy as jnp
from jax import lax
from jax.experimental import pallas as pl
from jax.experimental.pallas import tpu as pltpu
from jax.sharding import PartitionSpec as P

SB = 64
LANES = 128
TAG = 16
CHUNK = 16


def pack_kernel(n_pair, integrals, mu, nu, counts, *refs):
    outs = refs[:n_pair]
    tiles, mu_in, nu_in, spread, woven, sems = refs[n_pair:]
    p = lax.axis_index("pair")
    copies = [
        pltpu.make_async_copy(source, target, sems.at[n])
        for n, (source, target) in enumerate(((integrals, tiles), (mu, mu_in), (nu, nu_in)))
    ]
    for copy in copies:
        copy.start()
    slots, kets, flat = tiles.shape
    wide = flat // LANES
    columns = kets // n_pair
    for copy in copies[1:]:
        copy.wait()
    count = counts[0]
    lane = lax.broadcasted_iota(jnp.int32, (wide, LANES), 1)
    low, kept = lane < SB, lane < SB * count
    lane = lax.broadcasted_iota(jnp.int32, (TAG, LANES), 1)
    tag = jnp.zeros((TAG, LANES), jnp.int32)
    for t in range(slots):
        tag = jnp.where((lane == 2 * t) & (t < count), mu_in[t], tag)
        tag = jnp.where((lane == 2 * t + 1) & (t < count), nu_in[t], tag)
    tag = tag.astype(jnp.float32).astype(jnp.bfloat16)
    copies[0].wait()
    for t in range(slots):
        for j in range(wide):
            at = pl.ds((t * wide + j) * kets, kets)
            spread[at, :] = tiles[t, :, j * LANES : (j + 1) * LANES].astype(jnp.float32)
    for s in range(n_pair):
        dest = lax.rem(p + s, n_pair)
        for k in range(columns):
            column = dest * columns + k
            one = spread[pl.ds(column, wide, stride=kets), :]
            two = spread[pl.ds(wide * kets + column, wide, stride=kets), :]
            even = jnp.where(low, one, pltpu.roll(two, SB, axis=1))
            odd = jnp.where(low, pltpu.roll(one, SB, axis=1), two)
            begin = (s * columns + k) * SB
            woven[pl.ds(begin, wide, stride=2), :] = jnp.where(kept, even, 0.0)
            woven[pl.ds(begin + 1, wide, stride=2), :] = jnp.where(kept, odd, 0.0)
        rows = columns * SB
        outs[s][0, :rows] = woven[pl.ds(s * rows, rows), :].astype(jnp.bfloat16)
        outs[s][0, rows:] = tag


def pack(n_pair, integrals, mu, nu, counts):
    slots, kets, flat = integrals.shape
    rows = kets // n_pair * SB + TAG
    hbm, smem = pl.BlockSpec(memory_space=pltpu.HBM), pl.BlockSpec(memory_space=pltpu.SMEM)
    return pl.pallas_call(
        functools.partial(pack_kernel, n_pair),
        out_shape=[jax.ShapeDtypeStruct((1, rows, LANES), jnp.bfloat16)] * n_pair,
        in_specs=[hbm, hbm, hbm, smem],
        out_specs=[pl.BlockSpec(memory_space=pltpu.VMEM)] * n_pair,
        scratch_shapes=[
            pltpu.VMEM(integrals.shape, jnp.bfloat16),
            pltpu.SMEM(mu.shape, jnp.int32),
            pltpu.SMEM(nu.shape, jnp.int32),
            pltpu.VMEM((slots * kets * flat // LANES, LANES), jnp.float32),
            pltpu.VMEM((kets * SB, LANES), jnp.float32),
            pltpu.SemaphoreType.DMA((3,)),
        ],
        compiler_params=pltpu.CompilerParams(vmem_limit_bytes=60 << 20),
        name="pack",
    )(integrals, mu, nu, counts)


def transform_kernel(source_of, n_c, n_x, *refs):
    c_in, x_in = refs[:n_c], refs[n_c : n_c + n_x]
    out, c_all, x_all, tags, codes, index, half, left, sems = refs[n_c + n_x :]
    o = lax.axis_index("orb")
    devices = codes.shape[0]
    orbitals = c_all.shape[1]
    blocks = orbitals // LANES
    early, late = [], []
    per = devices // n_x
    for q, piece in enumerate(x_in):
        place = pl.ds(q * per, per)
        early.append(pltpu.make_async_copy(piece.at[:, pl.ds(2 * SB, TAG)], tags.at[place], sems.at[q]))
        late.append(pltpu.make_async_copy(piece.at[:, pl.ds(0, 2 * SB)], x_all.at[place], sems.at[n_x + q]))
    for q, piece in enumerate(c_in):
        rows = c_all.shape[0] // n_c
        place = pl.ds(pl.multiple_of(source_of(q) * rows, rows), rows)
        late.append(pltpu.make_async_copy(piece, c_all.at[place], sems.at[2 * n_x + q]))
    for copy in early + late:
        copy.start()
    for copy in early:
        copy.wait()
    codes[...] = tags[:, 0, :].astype(jnp.float32).astype(jnp.int32)
    to_scalars = pltpu.make_async_copy(codes, index, sems.at[2 * n_x + n_c])
    to_scalars.start()
    to_scalars.wait()
    for copy in late:
        copy.wait()

    mine = pl.ds(pl.multiple_of(o * LANES, LANES), LANES)
    low = lax.broadcasted_iota(jnp.int32, (SB, LANES), 1) < SB
    chunks = devices // CHUNK

    def rows_of(block):
        return pl.ds(pl.multiple_of(block * SB, SB), SB)

    def chunk_step(chunk, carry):
        for d in range(CHUNK):
            device = chunk * CHUNK + d
            stacked = []
            for k in range(2):
                tile = x_all[device, k * SB : (k + 1) * SB, :]
                stacked += [jnp.where(low, tile, jnp.zeros_like(tile)), jnp.where(low, jnp.zeros_like(tile), tile)]
            mu_one, nu_one, mu_two, nu_two = (index[device, n] for n in range(4))
            rows = jnp.concatenate([c_all[rows_of(nu_one)], c_all[rows_of(nu_two)]], 0)
            moved = jnp.dot(jnp.concatenate(stacked, 0), rows, preferred_element_type=jnp.float32)
            moved = moved.astype(jnp.bfloat16)
            at = pl.ds(d * 2 * SB, 2 * SB)
            half[at, :orbitals] = moved[: 2 * SB]
            half[at, orbitals:] = moved[2 * SB :]
            left[at, :] = jnp.concatenate([c_all[rows_of(mu_one), mine], c_all[rows_of(mu_two), mine]], 0)
        part = lax.dot_general(
            left[...], half[...], (((0,), (0,)), ((), ())), preferred_element_type=jnp.float32
        )
        for k in range(2):
            for j in range(blocks):
                at = pl.ds(2 * j + k, LANES, stride=2 * blocks)
                begin = k * orbitals + j * LANES
                value = part[:, begin : begin + LANES]
                out[at, :] = value if chunks == 1 else out[at, :] + value
        return carry

    if chunks == 1:
        chunk_step(0, 0)
    else:
        out[...] = jnp.zeros_like(out)
        lax.fori_loop(0, chunks, chunk_step, 0)


def transform(source_of, c_pieces, x_pieces):
    orbitals = c_pieces[0].shape[1]
    devices = sum(piece.shape[0] for piece in x_pieces)
    n_c, n_x = len(c_pieces), len(x_pieces)
    wide = CHUNK * 2 * SB
    return pl.pallas_call(
        functools.partial(transform_kernel, source_of, n_c, n_x),
        out_shape=jax.ShapeDtypeStruct((2 * orbitals // LANES * LANES, LANES), jnp.float32),
        in_specs=[pl.BlockSpec(memory_space=pl.ANY)] * (n_c + n_x),
        out_specs=pl.BlockSpec(memory_space=pltpu.VMEM),
        scratch_shapes=[
            pltpu.VMEM((c_pieces[0].shape[0] * n_c, orbitals), jnp.bfloat16),
            pltpu.VMEM((devices, 2 * SB, LANES), jnp.bfloat16),
            pltpu.VMEM((devices, TAG, LANES), jnp.bfloat16),
            pltpu.VMEM((devices, LANES), jnp.int32),
            pltpu.SMEM((devices, LANES), jnp.int32),
            pltpu.VMEM((wide, 2 * orbitals), jnp.bfloat16),
            pltpu.VMEM((wide, LANES), jnp.bfloat16),
            pltpu.SemaphoreType.DMA((n_c + 2 * n_x + 1,)),
        ],
        compiler_params=pltpu.CompilerParams(vmem_limit_bytes=40 << 20),
        name="transform",
    )(*c_pieces, *x_pieces)


def shift(array, axis, size, step):
    return lax.ppermute(array, axis, [(i, (i + step) % size) for i in range(size)])


def flip(array, axis, size, bit):
    return lax.ppermute(array, axis, [(i, i ^ bit) for i in range(size)])


def around(n_pair, n_orb):
    length = 2 * n_pair
    ups = [p * n_orb for p in range(n_pair)]
    stops = ups + [stop + n_orb // 2 for stop in reversed(ups)]
    ring = [(stops[r], stops[(r + 1) % length]) for r in range(length)]
    return ring + [(b + 1, a + 1) for a, b in ring]


def ring_source(n_pair, n_orb, step, flipped):
    p, o = lax.axis_index("pair"), lax.axis_index("orb")
    length = 2 * n_pair
    core = lax.rem(o, 2) ^ flipped
    place = jnp.where(o < 2, p, length - 1 - p)
    place = lax.rem(place + jnp.where(core == 0, length - step, length + step), length)
    down = place >= n_pair
    return jnp.where(down, (length - 1 - place) * n_orb + 2, place * n_orb) + core


def body(n_pair, n_orb, integrals, mu_block, nu_block, counts, coeff):
    slots, kets, flat = integrals.shape
    columns = kets // n_pair
    orbitals = coeff.shape[1]
    everyone = ("pair", "orb")
    if n_orb == 4 and n_pair <= 4:
        forward = around(n_pair, n_orb)
        backward = [(b, a) for a, b in forward]
        held = {0: coeff}
        for step in range(1, n_pair + 1):
            held[step] = lax.ppermute(held[step - 1], everyone, forward)
            if step < n_pair:
                held[-step] = lax.ppermute(held[1 - step], everyone, backward)
        packed = pack(n_pair, integrals, mu_block, nu_block, counts)
        line = jnp.concatenate([packed[0]] + [shift(packed[s], "pair", n_pair, s) for s in range(1, n_pair)], 0)
        across = flip(line, "orb", n_orb, 2)
        x_pieces = [line, flip(line, "orb", n_orb, 1), across, flip(across, "orb", n_orb, 1)]
        c_pieces, came = [], []
        for step, piece in held.items():
            c_pieces += [piece, flip(piece, "orb", n_orb, 1)]
            came += [(step, 0), (step, 1)]

        def source_of(q):
            return ring_source(n_pair, n_orb, *came[q])
    else:
        kept = jnp.arange(slots, dtype=jnp.int32) < counts[0]
        tiles = jnp.where(kept[:, None, None], integrals, jnp.zeros_like(integrals))
        tiles = tiles.reshape(slots, n_pair, columns, SB, SB).transpose(1, 2, 3, 0, 4)
        tiles = tiles.reshape(n_pair, columns * SB, slots * SB)
        tag = jnp.where(kept[:, None], jnp.stack([mu_block, nu_block], 1), 0).reshape(-1)
        tag = jnp.zeros((n_pair, TAG, LANES), jnp.bfloat16).at[:, :, : 2 * slots].set(tag.astype(jnp.bfloat16))
        packed = jnp.concatenate([tiles, tag], 1)
        line = lax.all_to_all(packed, "pair", split_axis=0, concat_axis=0, tiled=True)
        x_pieces = [lax.all_gather(line, "orb", axis=0, tiled=True)]
        c_pieces = [lax.all_gather(coeff, everyone, axis=0, tiled=True)]

        def source_of(q):
            return q
    out = transform(source_of, c_pieces, x_pieces)
    out = out.reshape(orbitals // n_orb, orbitals // LANES, columns, LANES)
    return out.transpose(0, 2, 1, 3).reshape(orbitals // n_orb, columns, orbitals)


def solution(mesh):
    placed = (
        P(("grp", "pair", "orb"), None, None),
        P(("grp", "pair", "orb")),
        P(("grp", "pair", "orb")),
        P(("grp", "pair", "orb")),
        P(("grp", "pair", "orb"), None),
    )
    return jax.shard_map(
        functools.partial(body, mesh.shape["pair"], mesh.shape["orb"]),
        mesh=mesh,
        in_specs=placed,
        out_specs=P(("grp", "orb"), "pair", None),
        check_vma=False,
    )
```

```python
import functools

import jax
import jax.numpy as jnp
from jax import lax
from jax.experimental import pallas as pl
from jax.experimental.pallas import tpu as pltpu
from jax.sharding import PartitionSpec as P

SB = 64
LANES = 128
TAG = 16
CHUNK = 16


def pack_kernel(n_pair, integrals, mu, nu, counts, *refs):
    outs = refs[:n_pair]
    tiles, mu_in, nu_in, spread, woven, sems = refs[n_pair:]
    p = lax.axis_index("pair")
    copies = [
        pltpu.make_async_copy(source, target, sems.at[n])
        for n, (source, target) in enumerate(((integrals, tiles), (mu, mu_in), (nu, nu_in)))
    ]
    for copy in copies:
        copy.start()
    slots, kets, flat = tiles.shape
    wide = flat // LANES
    columns = kets // n_pair
    for copy in copies[1:]:
        copy.wait()
    count = counts[0]
    lane = lax.broadcasted_iota(jnp.int32, (wide, LANES), 1)
    low, kept = lane < SB, lane < SB * count
    lane = lax.broadcasted_iota(jnp.int32, (TAG, LANES), 1)
    tag = jnp.zeros((TAG, LANES), jnp.int32)
    for t in range(slots):
        tag = jnp.where((lane == 2 * t) & (t < count), mu_in[t], tag)
        tag = jnp.where((lane == 2 * t + 1) & (t < count), nu_in[t], tag)
    tag = tag.astype(jnp.float32).astype(jnp.bfloat16)
    copies[0].wait()
    for t in range(slots):
        for j in range(wide):
            at = pl.ds((t * wide + j) * kets, kets)
            spread[at, :] = tiles[t, :, j * LANES : (j + 1) * LANES].astype(jnp.float32)
    for s in range(n_pair):
        dest = lax.rem(p + s, n_pair)
        for k in range(columns):
            column = dest * columns + k
            one = spread[pl.ds(column, wide, stride=kets), :]
            two = spread[pl.ds(wide * kets + column, wide, stride=kets), :]
            even = jnp.where(low, one, pltpu.roll(two, SB, axis=1))
            odd = jnp.where(low, pltpu.roll(one, SB, axis=1), two)
            begin = (s * columns + k) * SB
            woven[pl.ds(begin, wide, stride=2), :] = jnp.where(kept, even, 0.0)
            woven[pl.ds(begin + 1, wide, stride=2), :] = jnp.where(kept, odd, 0.0)
        rows = columns * SB
        outs[s][0, :rows] = woven[pl.ds(s * rows, rows), :].astype(jnp.bfloat16)
        outs[s][0, rows:] = tag


def pack(n_pair, integrals, mu, nu, counts):
    slots, kets, flat = integrals.shape
    rows = kets // n_pair * SB + TAG
    hbm, smem = pl.BlockSpec(memory_space=pltpu.HBM), pl.BlockSpec(memory_space=pltpu.SMEM)
    return pl.pallas_call(
        functools.partial(pack_kernel, n_pair),
        out_shape=[jax.ShapeDtypeStruct((1, rows, LANES), jnp.bfloat16)] * n_pair,
        in_specs=[hbm, hbm, hbm, smem],
        out_specs=[pl.BlockSpec(memory_space=pltpu.VMEM)] * n_pair,
        scratch_shapes=[
            pltpu.VMEM(integrals.shape, jnp.bfloat16),
            pltpu.SMEM(mu.shape, jnp.int32),
            pltpu.SMEM(nu.shape, jnp.int32),
            pltpu.VMEM((slots * kets * flat // LANES, LANES), jnp.float32),
            pltpu.VMEM((kets * SB, LANES), jnp.float32),
            pltpu.SemaphoreType.DMA((3,)),
        ],
        compiler_params=pltpu.CompilerParams(vmem_limit_bytes=60 << 20),
        name="pack",
    )(integrals, mu, nu, counts)


def transform_kernel(place_of, n_c, n_x, *refs):
    c_in, x_in = refs[:n_c], refs[n_c : n_c + n_x]
    out, c_all, codes, index, half, left, sem = refs[n_c + n_x :]
    o = lax.axis_index("orb")
    devices = codes.shape[0]
    orbitals = c_in[0].shape[1]
    blocks = orbitals // LANES
    per = devices // n_x
    for q, piece in enumerate(x_in):
        tag = piece[:, 2 * SB :, :][:, 0, :]
        codes[q * per : (q + 1) * per, :] = tag.astype(jnp.float32).astype(jnp.int32)
    to_scalars = pltpu.make_async_copy(codes, index, sem)
    to_scalars.start()
    if n_c == 1:
        (c_all,) = c_in
    else:
        for q, piece in enumerate(c_in):
            for at, row in place_of(q):
                rows = c_all.shape[0] // devices
                c_all[pl.ds(pl.multiple_of(row * rows, rows), rows), :] = piece[at * rows : (at + 1) * rows, :]
    to_scalars.wait()

    mine = pl.ds(pl.multiple_of(o * LANES, LANES), LANES)
    low = lax.broadcasted_iota(jnp.int32, (SB, LANES), 1) < SB
    chunks = devices // CHUNK

    def rows_of(block):
        return pl.ds(pl.multiple_of(block * SB, SB), SB)

    def chunk_step(chunk, carry):
        for d in range(CHUNK):
            device = chunk * CHUNK + d
            stacked = []
            for k in range(2):
                piece, at = (x_in[d // per], d % per) if chunks == 1 else (x_in[0], device)
                tile = piece[at, k * SB : (k + 1) * SB, :]
                stacked += [jnp.where(low, tile, jnp.zeros_like(tile)), jnp.where(low, jnp.zeros_like(tile), tile)]
            mu_one, nu_one, mu_two, nu_two = (index[device, n] for n in range(4))
            rows = jnp.concatenate([c_all[rows_of(nu_one)], c_all[rows_of(nu_two)]], 0)
            moved = jnp.dot(jnp.concatenate(stacked, 0), rows, preferred_element_type=jnp.float32)
            moved = moved.astype(jnp.bfloat16)
            at = pl.ds(d * 2 * SB, 2 * SB)
            half[at, :orbitals] = moved[: 2 * SB]
            half[at, orbitals:] = moved[2 * SB :]
            left[at, :] = jnp.concatenate([c_all[rows_of(mu_one), mine], c_all[rows_of(mu_two), mine]], 0)
        part = lax.dot_general(
            left[...], half[...], (((0,), (0,)), ((), ())), preferred_element_type=jnp.float32
        )
        for k in range(2):
            for j in range(blocks):
                at = pl.ds(2 * j + k, LANES, stride=2 * blocks)
                begin = k * orbitals + j * LANES
                value = part[:, begin : begin + LANES]
                out[at, :] = value if chunks == 1 else out[at, :] + value
        return carry

    if chunks == 1:
        chunk_step(0, 0)
    else:
        out[...] = jnp.zeros_like(out)
        lax.fori_loop(0, chunks, chunk_step, 0)


def transform(place_of, c_pieces, x_pieces):
    orbitals = c_pieces[0].shape[1]
    devices = sum(piece.shape[0] for piece in x_pieces)
    n_c, n_x = len(c_pieces), len(x_pieces)
    wide = CHUNK * 2 * SB
    joined = sum(piece.shape[0] for piece in c_pieces) if n_c > 1 else TAG
    return pl.pallas_call(
        functools.partial(transform_kernel, place_of, n_c, n_x),
        out_shape=jax.ShapeDtypeStruct((2 * orbitals // LANES * LANES, LANES), jnp.float32),
        in_specs=[pl.BlockSpec(memory_space=pltpu.VMEM)] * (n_c + n_x),
        out_specs=pl.BlockSpec(memory_space=pltpu.VMEM),
        scratch_shapes=[
            pltpu.VMEM((joined, orbitals), jnp.bfloat16),
            pltpu.VMEM((devices, LANES), jnp.int32),
            pltpu.SMEM((devices, LANES), jnp.int32),
            pltpu.VMEM((wide, 2 * orbitals), jnp.bfloat16),
            pltpu.VMEM((wide, LANES), jnp.bfloat16),
            pltpu.SemaphoreType.DMA,
        ],
        compiler_params=pltpu.CompilerParams(vmem_limit_bytes=40 << 20),
        name="transform",
    )(*c_pieces, *x_pieces)


def together(*arrays):
    return lax.optimization_barrier(arrays)


def shift(array, axis, size, step):
    return lax.ppermute(array, axis, [(i, (i + step) % size) for i in range(size)])


def flip(array, axis, size, bit):
    return lax.ppermute(array, axis, [(i, i ^ bit) for i in range(size)])


def around(n_pair, n_orb):
    length = 2 * n_pair
    ups = [p * n_orb for p in range(n_pair)]
    stops = ups + [stop + n_orb // 2 for stop in reversed(ups)]
    ring = [(stops[r], stops[(r + 1) % length]) for r in range(length)]
    return ring + [(b + 1, a + 1) for a, b in ring]


def ring_source(n_pair, n_orb, step, flipped):
    p, o = lax.axis_index("pair"), lax.axis_index("orb")
    length = 2 * n_pair
    core = lax.rem(o, 2) ^ flipped
    place = jnp.where(o < 2, p, length - 1 - p)
    place = lax.rem(place + jnp.where(core == 0, length - step, length + step), length)
    down = place >= n_pair
    return jnp.where(down, (length - 1 - place) * n_orb + 2, place * n_orb), core


def body(n_pair, n_orb, integrals, mu_block, nu_block, counts, coeff):
    slots, kets, flat = integrals.shape
    columns = kets // n_pair
    orbitals = coeff.shape[1]
    everyone = ("pair", "orb")
    if n_orb == 4 and n_pair == 4:
        ring = around(n_pair, n_orb)
        swapped = flip(coeff, "orb", n_orb, 1)
        half = coeff.shape[0]
        start = jnp.concatenate([coeff, swapped], 0)
        first = lax.ppermute(start, everyone, ring)
        first, packed = together(first, pack(n_pair, integrals, mu_block, nu_block, counts))
        second = lax.ppermute(first, everyone, ring)
        moved = [shift(packed[s], "pair", n_pair, s) for s in (1, 2)]
        second, moved, last = together(second, moved, packed[3])
        third = lax.ppermute(second, everyone, ring)
        moved.append(shift(last, "pair", n_pair, 3))
        third, moved = together(third, moved)
        fourth = lax.ppermute(third[:half], everyone, ring)
        line = jnp.concatenate([packed[0]] + moved, 0)
        across = flip(line, "orb", n_orb, 2)
        x_pieces = [line, flip(line, "orb", n_orb, 1), across, flip(across, "orb", n_orb, 1)]
        held = [start, first, second, third, fourth]
        c_pieces, came = [coeff, swapped], [(0, 0, 0), (0, 0, 1)]
        for step in range(1, n_pair + 1):
            c_pieces += [held[step], flip(held[step], "orb", n_orb, 1)]
            came += [(step, 0, 0), (step, 1, 0)]

        def place_of(q):
            step, flipped, other = came[q]
            chip, core = ring_source(n_pair, n_orb, step, flipped)
            if 0 < step < n_pair:
                return [(0, chip + core), (1, chip + 1 - core)]
            return [(0, chip + (core ^ other))]
    else:
        kept = jnp.arange(slots, dtype=jnp.int32) < counts[0]
        tiles = jnp.where(kept[:, None, None], integrals, jnp.zeros_like(integrals))
        tiles = tiles.reshape(slots, n_pair, columns, SB, SB).transpose(1, 2, 3, 0, 4)
        tiles = tiles.reshape(n_pair, columns * SB, slots * SB)
        tag = jnp.where(kept[:, None], jnp.stack([mu_block, nu_block], 1), 0).reshape(-1)
        tag = jnp.zeros((n_pair, TAG, LANES), jnp.bfloat16).at[:, :, : 2 * slots].set(tag.astype(jnp.bfloat16))
        packed = jnp.concatenate([tiles, tag], 1)
        line = lax.all_to_all(packed, "pair", split_axis=0, concat_axis=0, tiled=True)
        x_pieces = [lax.all_gather(line, "orb", axis=0, tiled=True)]
        c_pieces = [lax.all_gather(coeff, everyone, axis=0, tiled=True)]

        place_of = None
    out = transform(place_of, c_pieces, x_pieces)
    out = out.reshape(orbitals // n_orb, orbitals // LANES, columns, LANES)
    return out.transpose(0, 2, 1, 3).reshape(orbitals // n_orb, columns, orbitals)


def solution(mesh):
    placed = (
        P(("grp", "pair", "orb"), None, None),
        P(("grp", "pair", "orb")),
        P(("grp", "pair", "orb")),
        P(("grp", "pair", "orb")),
        P(("grp", "pair", "orb"), None),
    )
    return jax.shard_map(
        functools.partial(body, mesh.shape["pair"], mesh.shape["orb"]),
        mesh=mesh,
        in_specs=placed,
        out_specs=P(("grp", "orb"), "pair", None),
        check_vma=False,
    )
```

```python
import functools

import jax
import jax.numpy as jnp
from jax import lax
from jax.experimental import pallas as pl
from jax.experimental.pallas import tpu as pltpu
from jax.sharding import PartitionSpec as P

SB = 64
LANES = 128
TAG = 16
CHUNK = 16


def pack_kernel(n_pair, integrals, mu, nu, counts, *refs):
    outs = refs[:n_pair]
    tiles, mu_in, nu_in, spread, woven, sems = refs[n_pair:]
    p = lax.axis_index("pair")
    copies = [
        pltpu.make_async_copy(source, target, sems.at[n])
        for n, (source, target) in enumerate(((integrals, tiles), (mu, mu_in), (nu, nu_in)))
    ]
    for copy in copies:
        copy.start()
    slots, kets, flat = tiles.shape
    wide = flat // LANES
    columns = kets // n_pair
    for copy in copies[1:]:
        copy.wait()
    count = counts[0]
    lane = lax.broadcasted_iota(jnp.int32, (wide, LANES), 1)
    low, kept = lane < SB, lane < SB * count
    lane = lax.broadcasted_iota(jnp.int32, (TAG, LANES), 1)
    tag = jnp.zeros((TAG, LANES), jnp.int32)
    for t in range(slots):
        tag = jnp.where((lane == 2 * t) & (t < count), mu_in[t], tag)
        tag = jnp.where((lane == 2 * t + 1) & (t < count), nu_in[t], tag)
    tag = tag.astype(jnp.float32).astype(jnp.bfloat16)
    copies[0].wait()
    for t in range(slots):
        for j in range(wide):
            at = pl.ds((t * wide + j) * kets, kets)
            spread[at, :] = tiles[t, :, j * LANES : (j + 1) * LANES].astype(jnp.float32)
    for s in range(n_pair):
        dest = lax.rem(p + s, n_pair)
        for k in range(columns):
            column = dest * columns + k
            one = spread[pl.ds(column, wide, stride=kets), :]
            two = spread[pl.ds(wide * kets + column, wide, stride=kets), :]
            even = jnp.where(low, one, pltpu.roll(two, SB, axis=1))
            odd = jnp.where(low, pltpu.roll(one, SB, axis=1), two)
            begin = (s * columns + k) * SB
            woven[pl.ds(begin, wide, stride=2), :] = jnp.where(kept, even, 0.0)
            woven[pl.ds(begin + 1, wide, stride=2), :] = jnp.where(kept, odd, 0.0)
        rows = columns * SB
        outs[s][0, :rows] = woven[pl.ds(s * rows, rows), :].astype(jnp.bfloat16)
        outs[s][0, rows:] = tag


def pack(n_pair, integrals, mu, nu, counts):
    slots, kets, flat = integrals.shape
    rows = kets // n_pair * SB + TAG
    hbm, smem = pl.BlockSpec(memory_space=pltpu.HBM), pl.BlockSpec(memory_space=pltpu.SMEM)
    return pl.pallas_call(
        functools.partial(pack_kernel, n_pair),
        out_shape=[pltpu.VMEM((1, rows, LANES), jnp.bfloat16)] * n_pair,
        in_specs=[hbm, hbm, hbm, smem],
        out_specs=[pl.BlockSpec(memory_space=pltpu.VMEM)] * n_pair,
        scratch_shapes=[
            pltpu.VMEM(integrals.shape, jnp.bfloat16),
            pltpu.SMEM(mu.shape, jnp.int32),
            pltpu.SMEM(nu.shape, jnp.int32),
            pltpu.VMEM((slots * kets * flat // LANES, LANES), jnp.float32),
            pltpu.VMEM((kets * SB, LANES), jnp.float32),
            pltpu.SemaphoreType.DMA((3,)),
        ],
        compiler_params=pltpu.CompilerParams(vmem_limit_bytes=56 << 20),
        name="pack",
    )(integrals, mu, nu, counts)


def transform_kernel(place_of, n_c, n_x, *refs):
    c_in, x_in = refs[:n_c], refs[n_c : n_c + n_x]
    out, c_all, codes, index, half, left, sem = refs[n_c + n_x :]
    o = lax.axis_index("orb")
    devices = codes.shape[0]
    orbitals = c_in[0].shape[1]
    blocks = orbitals // LANES
    per = devices // n_x
    for q, piece in enumerate(x_in):
        tag = piece[:, 2 * SB :, :][:, 0, :]
        codes[q * per : (q + 1) * per, :] = tag.astype(jnp.float32).astype(jnp.int32)
    to_scalars = pltpu.make_async_copy(codes, index, sem)
    to_scalars.start()
    if n_c == 1:
        (c_all,) = c_in
    else:
        for q, piece in enumerate(c_in):
            for at, row in place_of(q):
                rows = c_all.shape[0] // devices
                c_all[pl.ds(pl.multiple_of(row * rows, rows), rows), :] = piece[at * rows : (at + 1) * rows, :]
    to_scalars.wait()

    mine = pl.ds(pl.multiple_of(o * LANES, LANES), LANES)
    low = lax.broadcasted_iota(jnp.int32, (SB, LANES), 1) < SB
    chunks = devices // CHUNK

    def rows_of(block):
        return pl.ds(pl.multiple_of(block * SB, SB), SB)

    def chunk_step(chunk, carry):
        for d in range(CHUNK):
            device = chunk * CHUNK + d
            stacked = []
            for k in range(2):
                piece, at = (x_in[d // per], d % per) if chunks == 1 else (x_in[0], device)
                tile = piece[at, k * SB : (k + 1) * SB, :]
                stacked += [jnp.where(low, tile, jnp.zeros_like(tile)), jnp.where(low, jnp.zeros_like(tile), tile)]
            mu_one, nu_one, mu_two, nu_two = (index[device, n] for n in range(4))
            rows = jnp.concatenate([c_all[rows_of(nu_one)], c_all[rows_of(nu_two)]], 0)
            moved = jnp.dot(jnp.concatenate(stacked, 0), rows, preferred_element_type=jnp.float32)
            moved = moved.astype(jnp.bfloat16)
            at = pl.ds(d * 2 * SB, 2 * SB)
            half[at, :orbitals] = moved[: 2 * SB]
            half[at, orbitals:] = moved[2 * SB :]
            left[at, :] = jnp.concatenate([c_all[rows_of(mu_one), mine], c_all[rows_of(mu_two), mine]], 0)
        part = lax.dot_general(
            left[...], half[...], (((0,), (0,)), ((), ())), preferred_element_type=jnp.float32
        )
        for k in range(2):
            for j in range(blocks):
                at = pl.ds(2 * j + k, LANES, stride=2 * blocks)
                begin = k * orbitals + j * LANES
                value = part[:, begin : begin + LANES]
                out[at, :] = value if chunks == 1 else out[at, :] + value
        return carry

    if chunks == 1:
        chunk_step(0, 0)
    else:
        out[...] = jnp.zeros_like(out)
        lax.fori_loop(0, chunks, chunk_step, 0)


def transform(place_of, c_pieces, x_pieces):
    orbitals = c_pieces[0].shape[1]
    devices = sum(piece.shape[0] for piece in x_pieces)
    n_c, n_x = len(c_pieces), len(x_pieces)
    wide = CHUNK * 2 * SB
    joined = sum(piece.shape[0] for piece in c_pieces) if n_c > 1 else TAG
    return pl.pallas_call(
        functools.partial(transform_kernel, place_of, n_c, n_x),
        out_shape=jax.ShapeDtypeStruct((2 * orbitals // LANES * LANES, LANES), jnp.float32),
        in_specs=[pl.BlockSpec(memory_space=pltpu.VMEM)] * (n_c + n_x),
        out_specs=pl.BlockSpec(memory_space=pltpu.VMEM),
        scratch_shapes=[
            pltpu.VMEM((joined, orbitals), jnp.bfloat16),
            pltpu.VMEM((devices, LANES), jnp.int32),
            pltpu.SMEM((devices, LANES), jnp.int32),
            pltpu.VMEM((wide, 2 * orbitals), jnp.bfloat16),
            pltpu.VMEM((wide, LANES), jnp.bfloat16),
            pltpu.SemaphoreType.DMA,
        ],
        compiler_params=pltpu.CompilerParams(vmem_limit_bytes=40 << 20),
        name="transform",
    )(*c_pieces, *x_pieces)


def together(*arrays):
    return lax.optimization_barrier(arrays)


def shift(array, axis, size, step):
    return lax.ppermute(array, axis, [(i, (i + step) % size) for i in range(size)])


def flip(array, axis, size, bit):
    return lax.ppermute(array, axis, [(i, i ^ bit) for i in range(size)])


def around(n_pair, n_orb):
    length = 2 * n_pair
    ups = [p * n_orb for p in range(n_pair)]
    stops = ups + [stop + n_orb // 2 for stop in reversed(ups)]
    ring = [(stops[r], stops[(r + 1) % length]) for r in range(length)]
    return ring + [(a + 1, b + 1) for a, b in ring]


def ring_source(n_pair, n_orb, step, flipped):
    p, o = lax.axis_index("pair"), lax.axis_index("orb")
    length = 2 * n_pair
    place = jnp.where(o < 2, p, length - 1 - p)
    place = lax.rem(place + length - step, length)
    down = place >= n_pair
    return jnp.where(down, (length - 1 - place) * n_orb + 2, place * n_orb) + (lax.rem(o, 2) ^ flipped)


def body(n_pair, n_orb, integrals, mu_block, nu_block, counts, coeff):
    slots, kets, flat = integrals.shape
    columns = kets // n_pair
    orbitals = coeff.shape[1]
    everyone = ("pair", "orb")
    if n_orb == 4 and n_pair == 4:
        ring = around(n_pair, n_orb)
        back = [(b, a) for a, b in ring]
        held = {0: coeff}
        held[1] = lax.ppermute(held[0], everyone, ring)
        held[-1] = lax.ppermute(held[0], everyone, back)
        packed = pack(n_pair, integrals, mu_block, nu_block, counts)
        held[1], packed = together(held[1], packed)
        held[2] = lax.ppermute(held[1], everyone, ring)
        held[-2] = lax.ppermute(held[-1], everyone, back)
        moved = {1: shift(packed[1], "pair", n_pair, 1)}
        held[2], later = together(held[2], packed[3])
        moved[3] = shift(later, "pair", n_pair, 3)
        held[3] = lax.ppermute(held[2], everyone, ring)
        held[-3] = lax.ppermute(held[-2], everyone, back)
        held[2], later = together(held[2], packed[2])
        moved[2] = shift(later, "pair", n_pair, 2)
        held[4] = lax.ppermute(held[3], everyone, ring)
        line = jnp.concatenate([packed[0]] + [moved[s] for s in range(1, n_pair)], 0)
        across = flip(line, "orb", n_orb, 2)
        x_pieces = [line, flip(line, "orb", n_orb, 1), across, flip(across, "orb", n_orb, 1)]
        c_pieces, came = [], []
        for step, piece in held.items():
            c_pieces += [piece, flip(piece, "orb", n_orb, 1)]
            came += [(step, 0), (step, 1)]

        def place_of(q):
            return [(0, ring_source(n_pair, n_orb, *came[q]))]
    else:
        kept = jnp.arange(slots, dtype=jnp.int32) < counts[0]
        tiles = jnp.where(kept[:, None, None], integrals, jnp.zeros_like(integrals))
        tiles = tiles.reshape(slots, n_pair, columns, SB, SB).transpose(1, 2, 3, 0, 4)
        tiles = tiles.reshape(n_pair, columns * SB, slots * SB)
        tag = jnp.where(kept[:, None], jnp.stack([mu_block, nu_block], 1), 0).reshape(-1)
        tag = jnp.zeros((n_pair, TAG, LANES), jnp.bfloat16).at[:, :, : 2 * slots].set(tag.astype(jnp.bfloat16))
        packed = jnp.concatenate([tiles, tag], 1)
        line = lax.all_to_all(packed, "pair", split_axis=0, concat_axis=0, tiled=True)
        x_pieces = [lax.all_gather(line, "orb", axis=0, tiled=True)]
        c_pieces = [lax.all_gather(coeff, everyone, axis=0, tiled=True)]

        place_of = None
    out = transform(place_of, c_pieces, x_pieces)
    out = out.reshape(orbitals // n_orb, orbitals // LANES, columns, LANES)
    return out.transpose(0, 2, 1, 3).reshape(orbitals // n_orb, columns, orbitals)


def solution(mesh):
    placed = (
        P(("grp", "pair", "orb"), None, None),
        P(("grp", "pair", "orb")),
        P(("grp", "pair", "orb")),
        P(("grp", "pair", "orb")),
        P(("grp", "pair", "orb"), None),
    )
    return jax.shard_map(
        functools.partial(body, mesh.shape["pair"], mesh.shape["orb"]),
        mesh=mesh,
        in_specs=placed,
        out_specs=P(("grp", "orb"), "pair", None),
        check_vma=False,
    )
```

```python
import functools

import jax
import jax.numpy as jnp
from jax import lax
from jax.experimental import pallas as pl
from jax.experimental.pallas import tpu as pltpu
from jax.sharding import PartitionSpec as P

SB = 64
LANES = 128
TAG = 16
CHUNK = 16


def pack_kernel(n_pair, integrals, mu, nu, counts, coeff, *refs):
    outs = refs[:n_pair]
    tiles, shard, mu_in, nu_in, spread, woven, sems = refs[n_pair:]
    p = lax.axis_index("pair")
    copies = [
        pltpu.make_async_copy(source, target, sems.at[n])
        for n, (source, target) in enumerate(((integrals, tiles), (mu, mu_in), (nu, nu_in), (coeff, shard)))
    ]
    for copy in copies:
        copy.start()
    slots, kets, flat = tiles.shape
    wide = flat // LANES
    columns = kets // n_pair
    held, orbitals = shard.shape
    for copy in copies[1:3]:
        copy.wait()
    count = counts[0]
    lane = lax.broadcasted_iota(jnp.int32, (wide, LANES), 1)
    low, kept = lane < SB, lane < SB * count
    lane = lax.broadcasted_iota(jnp.int32, (TAG, LANES), 1)
    tag = jnp.zeros((TAG, LANES), jnp.int32)
    for t in range(slots):
        tag = jnp.where((lane == 2 * t) & (t < count), mu_in[t], tag)
        tag = jnp.where((lane == 2 * t + 1) & (t < count), nu_in[t], tag)
    tag = tag.astype(jnp.float32).astype(jnp.bfloat16)
    copies[0].wait()
    for t in range(slots):
        for j in range(wide):
            at = pl.ds((t * wide + j) * kets, kets)
            spread[at, :] = tiles[t, :, j * LANES : (j + 1) * LANES].astype(jnp.float32)
    tile_at, rows = orbitals // LANES * held, columns * SB
    for s in range(n_pair):
        dest = p ^ s
        for k in range(columns):
            column = dest * columns + k
            one = spread[pl.ds(column, wide, stride=kets), :]
            two = spread[pl.ds(wide * kets + column, wide, stride=kets), :]
            even = jnp.where(low, one, pltpu.roll(two, SB, axis=1))
            odd = jnp.where(low, pltpu.roll(one, SB, axis=1), two)
            begin = (s * columns + k) * SB
            woven[pl.ds(begin, wide, stride=2), :] = jnp.where(kept, even, 0.0)
            woven[pl.ds(begin + 1, wide, stride=2), :] = jnp.where(kept, odd, 0.0)
        outs[s][tile_at : tile_at + rows] = woven[pl.ds(s * rows, rows), :].astype(jnp.bfloat16)
        outs[s][tile_at + rows :] = tag
    copies[3].wait()
    for j in range(orbitals // LANES):
        lanes = shard[:, j * LANES : (j + 1) * LANES]
        for s in range(n_pair):
            outs[s][j * held : (j + 1) * held] = lanes


def pack(n_pair, integrals, mu, nu, counts, coeff):
    slots, kets, flat = integrals.shape
    rows = coeff.shape[0] * coeff.shape[1] // LANES + kets // n_pair * SB + TAG
    hbm, smem = pl.BlockSpec(memory_space=pltpu.HBM), pl.BlockSpec(memory_space=pltpu.SMEM)
    return pl.pallas_call(
        functools.partial(pack_kernel, n_pair),
        out_shape=[pltpu.VMEM((rows, LANES), jnp.bfloat16)] * n_pair,
        in_specs=[hbm, hbm, hbm, smem, hbm],
        out_specs=[pl.BlockSpec(memory_space=pltpu.VMEM)] * n_pair,
        scratch_shapes=[
            pltpu.VMEM(integrals.shape, jnp.bfloat16),
            pltpu.VMEM(coeff.shape, jnp.bfloat16),
            pltpu.SMEM(mu.shape, jnp.int32),
            pltpu.SMEM(nu.shape, jnp.int32),
            pltpu.VMEM((slots * kets * flat // LANES, LANES), jnp.float32),
            pltpu.VMEM((kets * SB, LANES), jnp.float32),
            pltpu.SemaphoreType.DMA((4,)),
        ],
        compiler_params=pltpu.CompilerParams(vmem_limit_bytes=56 << 20),
        name="pack",
    )(integrals, mu, nu, counts, coeff)


def transform_kernel(came, n_orb, orbitals, n_in, *refs):
    pieces = refs[:n_in]
    out, c_all, codes, index, half, left, sem = refs[n_in:]
    p, o = lax.axis_index("pair"), lax.axis_index("orb")
    devices = codes.shape[0]
    blocks = orbitals // LANES
    tile_at = pieces[0].shape[-2] - TAG - 2 * SB
    if came:
        for q, piece in enumerate(pieces):
            codes[q : q + 1, :] = piece[tile_at + 2 * SB :][:1].astype(jnp.float32).astype(jnp.int32)
    else:
        codes[...] = pieces[0][:, 2 * SB :, :][:, 0, :].astype(jnp.float32).astype(jnp.int32)
    to_scalars = pltpu.make_async_copy(codes, index, sem)
    to_scalars.start()
    if came:
        rows = c_all.shape[0] // devices
        for q, piece in enumerate(pieces):
            source = (p ^ came[q][0]) * n_orb + (o ^ came[q][1])
            place = pl.ds(pl.multiple_of(source * rows, rows), rows)
            for j in range(blocks):
                c_all[place, j * LANES : (j + 1) * LANES] = piece[j * rows : (j + 1) * rows, :]
    else:
        c_all = pieces[1]
    to_scalars.wait()

    mine = pl.ds(pl.multiple_of(o * LANES, LANES), LANES)
    low = lax.broadcasted_iota(jnp.int32, (SB, LANES), 1) < SB
    chunks = devices // CHUNK

    def rows_of(block):
        return pl.ds(pl.multiple_of(block * SB, SB), SB)

    def chunk_step(chunk, carry):
        for d in range(CHUNK):
            device = chunk * CHUNK + d
            stacked = []
            for k in range(2):
                if came:
                    tile = pieces[d][tile_at + k * SB : tile_at + (k + 1) * SB, :]
                else:
                    tile = pieces[0][device, k * SB : (k + 1) * SB, :]
                stacked += [jnp.where(low, tile, jnp.zeros_like(tile)), jnp.where(low, jnp.zeros_like(tile), tile)]
            mu_one, nu_one, mu_two, nu_two = (index[device, n] for n in range(4))
            rows = jnp.concatenate([c_all[rows_of(nu_one)], c_all[rows_of(nu_two)]], 0)
            moved = jnp.dot(jnp.concatenate(stacked, 0), rows, preferred_element_type=jnp.float32)
            moved = moved.astype(jnp.bfloat16)
            at = pl.ds(d * 2 * SB, 2 * SB)
            half[at, :orbitals] = moved[: 2 * SB]
            half[at, orbitals:] = moved[2 * SB :]
            left[at, :] = jnp.concatenate([c_all[rows_of(mu_one), mine], c_all[rows_of(mu_two), mine]], 0)
        part = lax.dot_general(
            left[...], half[...], (((0,), (0,)), ((), ())), preferred_element_type=jnp.float32
        )
        for k in range(2):
            for j in range(blocks):
                at = pl.ds(2 * j + k, LANES, stride=2 * blocks)
                begin = k * orbitals + j * LANES
                value = part[:, begin : begin + LANES]
                out[at, :] = value if chunks == 1 else out[at, :] + value
        return carry

    if chunks == 1:
        chunk_step(0, 0)
    else:
        out[...] = jnp.zeros_like(out)
        lax.fori_loop(0, chunks, chunk_step, 0)


def transform(came, n_orb, devices, orbitals, pieces):
    wide = CHUNK * 2 * SB
    held = pieces[0].shape[0] - 2 * SB - TAG if came else TAG
    return pl.pallas_call(
        functools.partial(transform_kernel, came, n_orb, orbitals, len(pieces)),
        out_shape=jax.ShapeDtypeStruct((2 * orbitals // LANES * LANES, LANES), jnp.float32),
        in_specs=[pl.BlockSpec(memory_space=pltpu.VMEM)] * len(pieces),
        out_specs=pl.BlockSpec(memory_space=pltpu.VMEM),
        scratch_shapes=[
            pltpu.VMEM((held * LANES // orbitals * devices if came else TAG, orbitals), jnp.bfloat16),
            pltpu.VMEM((devices, LANES), jnp.int32),
            pltpu.SMEM((devices, LANES), jnp.int32),
            pltpu.VMEM((wide, 2 * orbitals), jnp.bfloat16),
            pltpu.VMEM((wide, LANES), jnp.bfloat16),
            pltpu.SemaphoreType.DMA,
        ],
        compiler_params=pltpu.CompilerParams(vmem_limit_bytes=40 << 20),
        name="transform",
    )(*pieces)


def flip(array, axis, size, bit):
    return lax.ppermute(array, axis, [(i, i ^ bit) for i in range(size)])


def body(n_pair, n_orb, integrals, mu_block, nu_block, counts, coeff):
    slots, kets, flat = integrals.shape
    columns = kets // n_pair
    orbitals = coeff.shape[1]
    if n_orb == 4 and n_pair == 4:
        packed = pack(n_pair, integrals, mu_block, nu_block, counts, coeff)
        pieces, came = [], []
        for s in range(n_pair):
            line = flip(packed[s], "pair", n_pair, s) if s else packed[0]
            across = flip(line, "orb", n_orb, 2)
            pieces += [line, flip(line, "orb", n_orb, 1), across, flip(across, "orb", n_orb, 1)]
            came += [(s, 0), (s, 1), (s, 2), (s, 3)]
    else:
        kept = jnp.arange(slots, dtype=jnp.int32) < counts[0]
        tiles = jnp.where(kept[:, None, None], integrals, jnp.zeros_like(integrals))
        tiles = tiles.reshape(slots, n_pair, columns, SB, SB).transpose(1, 2, 3, 0, 4)
        tiles = tiles.reshape(n_pair, columns * SB, slots * SB)
        tag = jnp.where(kept[:, None], jnp.stack([mu_block, nu_block], 1), 0).reshape(-1)
        tag = jnp.zeros((n_pair, TAG, LANES), jnp.bfloat16).at[:, :, : 2 * slots].set(tag.astype(jnp.bfloat16))
        packed = jnp.concatenate([tiles, tag], 1)
        line = lax.all_to_all(packed, "pair", split_axis=0, concat_axis=0, tiled=True)
        gathered = lax.all_gather(coeff, ("pair", "orb"), axis=0, tiled=True)
        pieces, came = [lax.all_gather(line, "orb", axis=0, tiled=True), gathered], None
    out = transform(came, n_orb, n_pair * n_orb, orbitals, pieces)
    out = out.reshape(orbitals // n_orb, orbitals // LANES, columns, LANES)
    return out.transpose(0, 2, 1, 3).reshape(orbitals // n_orb, columns, orbitals)


def solution(mesh):
    placed = (
        P(("grp", "pair", "orb"), None, None),
        P(("grp", "pair", "orb")),
        P(("grp", "pair", "orb")),
        P(("grp", "pair", "orb")),
        P(("grp", "pair", "orb"), None),
    )
    return jax.shard_map(
        functools.partial(body, mesh.shape["pair"], mesh.shape["orb"]),
        mesh=mesh,
        in_specs=placed,
        out_specs=P(("grp", "orb"), "pair", None),
        check_vma=False,
    )
```

```python
import functools

import jax
import jax.numpy as jnp
from jax import lax
from jax.experimental import pallas as pl
from jax.experimental.pallas import tpu as pltpu
from jax.sharding import PartitionSpec as P

SB = 64
LANES = 128
TAG = 16
CHUNK = 16


def pack_kernel(n_pair, integrals, mu, nu, counts, coeff, *refs):
    outs = refs[:n_pair]
    tiles, shard, mu_in, nu_in, spread, woven, sems = refs[n_pair:]
    p = lax.axis_index("pair")
    copies = [
        pltpu.make_async_copy(source, target, sems.at[n])
        for n, (source, target) in enumerate(((integrals, tiles), (mu, mu_in), (nu, nu_in), (coeff, shard)))
    ]
    for copy in copies:
        copy.start()
    slots, kets, flat = tiles.shape
    wide = flat // LANES
    columns = kets // n_pair
    held, orbitals = shard.shape
    for copy in copies[1:3]:
        copy.wait()
    count = counts[0]
    lane = lax.broadcasted_iota(jnp.int32, (wide, LANES), 1)
    low, kept = lane < SB, lane < SB * count
    lane = lax.broadcasted_iota(jnp.int32, (TAG, LANES), 1)
    tag = jnp.zeros((TAG, LANES), jnp.int32)
    for t in range(slots):
        tag = jnp.where((lane == 2 * t) & (t < count), mu_in[t], tag)
        tag = jnp.where((lane == 2 * t + 1) & (t < count), nu_in[t], tag)
    tag = tag.astype(jnp.float32).astype(jnp.bfloat16)
    copies[0].wait()
    for t in range(slots):
        for j in range(wide):
            at = pl.ds((t * wide + j) * kets, kets)
            spread[at, :] = tiles[t, :, j * LANES : (j + 1) * LANES].astype(jnp.float32)
    tile_at, rows = orbitals // LANES * held, columns * SB
    for s in range(n_pair):
        dest = p ^ s
        for k in range(columns):
            column = dest * columns + k
            one = spread[pl.ds(column, wide, stride=kets), :]
            two = spread[pl.ds(wide * kets + column, wide, stride=kets), :]
            even = jnp.where(low, one, pltpu.roll(two, SB, axis=1))
            odd = jnp.where(low, pltpu.roll(one, SB, axis=1), two)
            begin = (s * columns + k) * SB
            woven[pl.ds(begin, wide, stride=2), :] = jnp.where(kept, even, 0.0)
            woven[pl.ds(begin + 1, wide, stride=2), :] = jnp.where(kept, odd, 0.0)
        outs[s][tile_at : tile_at + rows] = woven[pl.ds(s * rows, rows), :].astype(jnp.bfloat16)
        outs[s][tile_at + rows :] = tag
    copies[3].wait()
    for j in range(orbitals // LANES):
        lanes = shard[:, j * LANES : (j + 1) * LANES]
        for s in range(n_pair):
            outs[s][j * held : (j + 1) * held] = lanes


def pack(n_pair, integrals, mu, nu, counts, coeff):
    slots, kets, flat = integrals.shape
    rows = coeff.shape[0] * coeff.shape[1] // LANES + kets // n_pair * SB + TAG
    hbm, smem = pl.BlockSpec(memory_space=pltpu.HBM), pl.BlockSpec(memory_space=pltpu.SMEM)
    return pl.pallas_call(
        functools.partial(pack_kernel, n_pair),
        out_shape=[pltpu.VMEM((rows, LANES), jnp.bfloat16)] * n_pair,
        in_specs=[hbm, hbm, hbm, smem, hbm],
        out_specs=[pl.BlockSpec(memory_space=pltpu.VMEM)] * n_pair,
        scratch_shapes=[
            pltpu.VMEM(integrals.shape, jnp.bfloat16),
            pltpu.VMEM(coeff.shape, jnp.bfloat16),
            pltpu.SMEM(mu.shape, jnp.int32),
            pltpu.SMEM(nu.shape, jnp.int32),
            pltpu.VMEM((slots * kets * flat // LANES, LANES), jnp.float32),
            pltpu.VMEM((kets * SB, LANES), jnp.float32),
            pltpu.SemaphoreType.DMA((4,)),
        ],
        compiler_params=pltpu.CompilerParams(vmem_limit_bytes=56 << 20),
        name="pack",
    )(integrals, mu, nu, counts, coeff)


def transform_kernel(came, n_orb, orbitals, n_in, *refs):
    pieces = refs[:n_in]
    out, c_all, codes, index, half, left, sem = refs[n_in:]
    p, o = lax.axis_index("pair"), lax.axis_index("orb")
    devices = codes.shape[0]
    blocks = orbitals // LANES
    tile_at = pieces[0].shape[-2] - TAG - 2 * SB
    if came:
        for q, piece in enumerate(pieces):
            codes[q : q + 1, :] = piece[tile_at + 2 * SB :][:1].astype(jnp.float32).astype(jnp.int32)
    else:
        codes[...] = pieces[0][:, 2 * SB :, :][:, 0, :].astype(jnp.float32).astype(jnp.int32)
    to_scalars = pltpu.make_async_copy(codes, index, sem)
    to_scalars.start()
    if came:
        rows = c_all.shape[0] // devices
        for q, piece in enumerate(pieces):
            source = (p ^ came[q][0]) * n_orb + (o ^ came[q][1])
            place = pl.ds(pl.multiple_of(source * rows, rows), rows)
            for j in range(blocks):
                c_all[place, j * LANES : (j + 1) * LANES] = piece[j * rows : (j + 1) * rows, :]
    else:
        c_all = pieces[1]
    to_scalars.wait()

    mine = pl.ds(pl.multiple_of(o * LANES, LANES), LANES)
    low = lax.broadcasted_iota(jnp.int32, (SB, LANES), 1) < SB
    chunks = devices // CHUNK

    def rows_of(block):
        return pl.ds(pl.multiple_of(block * SB, SB), SB)

    def chunk_step(chunk, carry):
        for d in range(CHUNK):
            device = chunk * CHUNK + d
            stacked = []
            for k in range(2):
                if came:
                    tile = pieces[d][tile_at + k * SB : tile_at + (k + 1) * SB, :]
                else:
                    tile = pieces[0][device, k * SB : (k + 1) * SB, :]
                stacked += [jnp.where(low, tile, jnp.zeros_like(tile)), jnp.where(low, jnp.zeros_like(tile), tile)]
            mu_one, nu_one, mu_two, nu_two = (index[device, n] for n in range(4))
            rows = jnp.concatenate([c_all[rows_of(nu_one)], c_all[rows_of(nu_two)]], 0)
            moved = jnp.dot(jnp.concatenate(stacked, 0), rows, preferred_element_type=jnp.float32)
            moved = moved.astype(jnp.bfloat16)
            at = pl.ds(d * 2 * SB, 2 * SB)
            half[at, :orbitals] = moved[: 2 * SB]
            half[at, orbitals:] = moved[2 * SB :]
            left[at, :] = jnp.concatenate([c_all[rows_of(mu_one), mine], c_all[rows_of(mu_two), mine]], 0)
        part = lax.dot_general(
            left[...], half[...], (((0,), (0,)), ((), ())), preferred_element_type=jnp.float32
        )
        for k in range(2):
            for j in range(blocks):
                at = pl.ds(2 * j + k, LANES, stride=2 * blocks)
                begin = k * orbitals + j * LANES
                value = part[:, begin : begin + LANES]
                out[at, :] = value if chunks == 1 else out[at, :] + value
        return carry

    if chunks == 1:
        chunk_step(0, 0)
    else:
        out[...] = jnp.zeros_like(out)
        lax.fori_loop(0, chunks, chunk_step, 0)


def transform(came, n_orb, devices, orbitals, pieces):
    wide = CHUNK * 2 * SB
    held = pieces[0].shape[0] - 2 * SB - TAG if came else TAG
    return pl.pallas_call(
        functools.partial(transform_kernel, came, n_orb, orbitals, len(pieces)),
        out_shape=jax.ShapeDtypeStruct((2 * orbitals // LANES * LANES, LANES), jnp.float32),
        in_specs=[pl.BlockSpec(memory_space=pltpu.VMEM)] * len(pieces),
        out_specs=pl.BlockSpec(memory_space=pltpu.VMEM),
        scratch_shapes=[
            pltpu.VMEM((held * LANES // orbitals * devices if came else TAG, orbitals), jnp.bfloat16),
            pltpu.VMEM((devices, LANES), jnp.int32),
            pltpu.SMEM((devices, LANES), jnp.int32),
            pltpu.VMEM((wide, 2 * orbitals), jnp.bfloat16),
            pltpu.VMEM((wide, LANES), jnp.bfloat16),
            pltpu.SemaphoreType.DMA,
        ],
        compiler_params=pltpu.CompilerParams(vmem_limit_bytes=40 << 20),
        name="transform",
    )(*pieces)


def flip(array, axis, size, bit):
    return lax.ppermute(array, axis, [(i, i ^ bit) for i in range(size)])


def body(n_pair, n_orb, integrals, mu_block, nu_block, counts, coeff):
    slots, kets, flat = integrals.shape
    columns = kets // n_pair
    orbitals = coeff.shape[1]
    if n_orb == 4 and n_pair == 4:
        packed = list(pack(n_pair, integrals, mu_block, nu_block, counts, coeff))
        lines = packed[:1] + [flip(packed[s], "pair", n_pair, s) for s in range(1, n_pair)]
        across = [flip(line, "orb", n_orb, 2) for line in lines[:3]]
        last, across[1] = lax.optimization_barrier((lines[3], across[1]))
        across.append(flip(last, "orb", n_orb, 2))
        early = lax.optimization_barrier(tuple(lines[:3] + across[:3] + [last]))
        pieces = list(early) + across[3:]
        pieces += [flip(piece, "orb", n_orb, 1) for piece in pieces]
        came = [(0, 0), (1, 0), (2, 0), (0, 2), (1, 2), (2, 2), (3, 0), (3, 2)]
        came += [(s, side ^ 1) for s, side in came]
    else:
        kept = jnp.arange(slots, dtype=jnp.int32) < counts[0]
        tiles = jnp.where(kept[:, None, None], integrals, jnp.zeros_like(integrals))
        tiles = tiles.reshape(slots, n_pair, columns, SB, SB).transpose(1, 2, 3, 0, 4)
        tiles = tiles.reshape(n_pair, columns * SB, slots * SB)
        tag = jnp.where(kept[:, None], jnp.stack([mu_block, nu_block], 1), 0).reshape(-1)
        tag = jnp.zeros((n_pair, TAG, LANES), jnp.bfloat16).at[:, :, : 2 * slots].set(tag.astype(jnp.bfloat16))
        packed = jnp.concatenate([tiles, tag], 1)
        line = lax.all_to_all(packed, "pair", split_axis=0, concat_axis=0, tiled=True)
        gathered = lax.all_gather(coeff, ("pair", "orb"), axis=0, tiled=True)
        pieces, came = [lax.all_gather(line, "orb", axis=0, tiled=True), gathered], None
    out = transform(came, n_orb, n_pair * n_orb, orbitals, pieces)
    out = out.reshape(orbitals // n_orb, orbitals // LANES, columns, LANES)
    return out.transpose(0, 2, 1, 3).reshape(orbitals // n_orb, columns, orbitals)


def solution(mesh):
    placed = (
        P(("grp", "pair", "orb"), None, None),
        P(("grp", "pair", "orb")),
        P(("grp", "pair", "orb")),
        P(("grp", "pair", "orb")),
        P(("grp", "pair", "orb"), None),
    )
    return jax.shard_map(
        functools.partial(body, mesh.shape["pair"], mesh.shape["orb"]),
        mesh=mesh,
        in_specs=placed,
        out_specs=P(("grp", "orb"), "pair", None),
        check_vma=False,
    )
```

```python
import functools

import jax
import jax.numpy as jnp
from jax import lax
from jax.experimental import pallas as pl
from jax.experimental.pallas import tpu as pltpu
from jax.sharding import PartitionSpec as P

SB = 64
LANES = 128
TAG = 16
CHUNK = 16


def pack_kernel(n_pair, integrals, mu, nu, counts, coeff, *refs):
    own, one_off, two_off, tiles, shard, mu_in, nu_in, spread, woven, sems = refs
    rows = shard.shape[0] * shard.shape[1] // LANES
    reach = integrals.shape[1] // n_pair * SB + TAG
    tile_spots = ((own, rows), (one_off, rows), (two_off, reach + rows), (two_off, 0))
    shard_spots = ((own, 0), (one_off, 0), (two_off, reach))
    p = lax.axis_index("pair")
    copies = [
        pltpu.make_async_copy(source, target, sems.at[n])
        for n, (source, target) in enumerate(((integrals, tiles), (mu, mu_in), (nu, nu_in), (coeff, shard)))
    ]
    for copy in copies:
        copy.start()
    slots, kets, flat = tiles.shape
    wide = flat // LANES
    columns = kets // n_pair
    held, orbitals = shard.shape
    for copy in copies[1:3]:
        copy.wait()
    count = counts[0]
    lane = lax.broadcasted_iota(jnp.int32, (wide, LANES), 1)
    low, kept = lane < SB, lane < SB * count
    lane = lax.broadcasted_iota(jnp.int32, (TAG, LANES), 1)
    tag = jnp.zeros((TAG, LANES), jnp.int32)
    for t in range(slots):
        tag = jnp.where((lane == 2 * t) & (t < count), mu_in[t], tag)
        tag = jnp.where((lane == 2 * t + 1) & (t < count), nu_in[t], tag)
    tag = tag.astype(jnp.float32).astype(jnp.bfloat16)
    copies[0].wait()
    for t in range(slots):
        for j in range(wide):
            at = pl.ds((t * wide + j) * kets, kets)
            spread[at, :] = tiles[t, :, j * LANES : (j + 1) * LANES].astype(jnp.float32)
    rows = columns * SB
    for s in range(n_pair):
        dest = p ^ s
        for k in range(columns):
            column = dest * columns + k
            one = spread[pl.ds(column, wide, stride=kets), :]
            two = spread[pl.ds(wide * kets + column, wide, stride=kets), :]
            even = jnp.where(low, one, pltpu.roll(two, SB, axis=1))
            odd = jnp.where(low, pltpu.roll(one, SB, axis=1), two)
            begin = (s * columns + k) * SB
            woven[pl.ds(begin, wide, stride=2), :] = jnp.where(kept, even, 0.0)
            woven[pl.ds(begin + 1, wide, stride=2), :] = jnp.where(kept, odd, 0.0)
        target, at = tile_spots[s]
        target[at : at + rows] = woven[pl.ds(s * rows, rows), :].astype(jnp.bfloat16)
        target[at + rows : at + rows + TAG] = tag
    copies[3].wait()
    for j in range(orbitals // LANES):
        lanes = shard[:, j * LANES : (j + 1) * LANES]
        for target, at in shard_spots:
            target[at + j * held : at + (j + 1) * held] = lanes


def pack(n_pair, integrals, mu, nu, counts, coeff):
    slots, kets, flat = integrals.shape
    reach = kets // n_pair * SB + TAG
    rows = coeff.shape[0] * coeff.shape[1] // LANES + reach
    hbm, smem = pl.BlockSpec(memory_space=pltpu.HBM), pl.BlockSpec(memory_space=pltpu.SMEM)
    return pl.pallas_call(
        functools.partial(pack_kernel, n_pair),
        out_shape=[pltpu.VMEM((size, LANES), jnp.bfloat16) for size in (rows, rows, rows + reach)],
        in_specs=[hbm, hbm, hbm, smem, hbm],
        out_specs=[pl.BlockSpec(memory_space=pltpu.VMEM)] * 3,
        scratch_shapes=[
            pltpu.VMEM(integrals.shape, jnp.bfloat16),
            pltpu.VMEM(coeff.shape, jnp.bfloat16),
            pltpu.SMEM(mu.shape, jnp.int32),
            pltpu.SMEM(nu.shape, jnp.int32),
            pltpu.VMEM((slots * kets * flat // LANES, LANES), jnp.float32),
            pltpu.VMEM((kets * SB, LANES), jnp.float32),
            pltpu.SemaphoreType.DMA((4,)),
        ],
        compiler_params=pltpu.CompilerParams(vmem_limit_bytes=56 << 20),
        name="pack",
    )(integrals, mu, nu, counts, coeff)


def transform_kernel(came, n_orb, orbitals, n_in, *refs):
    pieces = refs[:n_in]
    out, c_all, codes, index, half, left, sem = refs[n_in:]
    p, o = lax.axis_index("pair"), lax.axis_index("orb")
    devices = codes.shape[0]
    blocks = orbitals // LANES
    if came:
        rows = c_all.shape[0] // devices
        tile_at = [0 if ahead else blocks * rows for _, _, ahead in came]
        for q, piece in enumerate(pieces):
            codes[q : q + 1, :] = piece[tile_at[q] + 2 * SB : tile_at[q] + 2 * SB + TAG][:1].astype(jnp.float32).astype(jnp.int32)
    else:
        codes[...] = pieces[0][:, 2 * SB :, :][:, 0, :].astype(jnp.float32).astype(jnp.int32)
    to_scalars = pltpu.make_async_copy(codes, index, sem)
    to_scalars.start()
    if came:
        for q, piece in enumerate(pieces):
            begin = 2 * SB + TAG if came[q][2] else 0
            source = (p ^ came[q][0]) * n_orb + (o ^ came[q][1])
            place = pl.ds(pl.multiple_of(source * rows, rows), rows)
            for j in range(blocks):
                c_all[place, j * LANES : (j + 1) * LANES] = piece[begin + j * rows : begin + (j + 1) * rows, :]
    else:
        c_all = pieces[1]
    to_scalars.wait()

    mine = pl.ds(pl.multiple_of(o * LANES, LANES), LANES)
    low = lax.broadcasted_iota(jnp.int32, (SB, LANES), 1) < SB
    chunks = devices // CHUNK

    def rows_of(block):
        return pl.ds(pl.multiple_of(block * SB, SB), SB)

    def chunk_step(chunk, carry):
        for d in range(CHUNK):
            device = chunk * CHUNK + d
            stacked = []
            for k in range(2):
                if came:
                    tile = pieces[d][tile_at[d] + k * SB : tile_at[d] + (k + 1) * SB, :]
                else:
                    tile = pieces[0][device, k * SB : (k + 1) * SB, :]
                stacked += [jnp.where(low, tile, jnp.zeros_like(tile)), jnp.where(low, jnp.zeros_like(tile), tile)]
            mu_one, nu_one, mu_two, nu_two = (index[device, n] for n in range(4))
            rows = jnp.concatenate([c_all[rows_of(nu_one)], c_all[rows_of(nu_two)]], 0)
            moved = jnp.dot(jnp.concatenate(stacked, 0), rows, preferred_element_type=jnp.float32)
            moved = moved.astype(jnp.bfloat16)
            at = pl.ds(d * 2 * SB, 2 * SB)
            half[at, :orbitals] = moved[: 2 * SB]
            half[at, orbitals:] = moved[2 * SB :]
            left[at, :] = jnp.concatenate([c_all[rows_of(mu_one), mine], c_all[rows_of(mu_two), mine]], 0)
        part = lax.dot_general(
            left[...], half[...], (((0,), (0,)), ((), ())), preferred_element_type=jnp.float32
        )
        for k in range(2):
            for j in range(blocks):
                at = pl.ds(2 * j + k, LANES, stride=2 * blocks)
                begin = k * orbitals + j * LANES
                value = part[:, begin : begin + LANES]
                out[at, :] = value if chunks == 1 else out[at, :] + value
        return carry

    if chunks == 1:
        chunk_step(0, 0)
    else:
        out[...] = jnp.zeros_like(out)
        lax.fori_loop(0, chunks, chunk_step, 0)


def transform(came, n_orb, devices, orbitals, pieces):
    wide = CHUNK * 2 * SB
    held = pieces[0].shape[0] - 2 * SB - TAG if came else TAG
    return pl.pallas_call(
        functools.partial(transform_kernel, came, n_orb, orbitals, len(pieces)),
        out_shape=jax.ShapeDtypeStruct((2 * orbitals // LANES * LANES, LANES), jnp.float32),
        in_specs=[pl.BlockSpec(memory_space=pltpu.VMEM)] * len(pieces),
        out_specs=pl.BlockSpec(memory_space=pltpu.VMEM),
        scratch_shapes=[
            pltpu.VMEM((held * LANES // orbitals * devices if came else TAG, orbitals), jnp.bfloat16),
            pltpu.VMEM((devices, LANES), jnp.int32),
            pltpu.SMEM((devices, LANES), jnp.int32),
            pltpu.VMEM((wide, 2 * orbitals), jnp.bfloat16),
            pltpu.VMEM((wide, LANES), jnp.bfloat16),
            pltpu.SemaphoreType.DMA,
        ],
        compiler_params=pltpu.CompilerParams(vmem_limit_bytes=40 << 20),
        name="transform",
    )(*pieces)


def flip(array, axis, size, bit):
    return lax.ppermute(array, axis, [(i, i ^ bit) for i in range(size)])


def body(n_pair, n_orb, integrals, mu_block, nu_block, counts, coeff):
    slots, kets, flat = integrals.shape
    columns = kets // n_pair
    orbitals = coeff.shape[1]
    if n_orb == 4 and n_pair == 4:
        own, one_off, two_off = pack(n_pair, integrals, mu_block, nu_block, counts, coeff)
        two = flip(two_off, "pair", n_pair, 2)
        one = flip(one_off, "pair", n_pair, 1)
        last = flip(two[: own.shape[0]], "pair", n_pair, 1)
        lines = [own, one, two[two.shape[0] - own.shape[0] :]]
        across = [flip(line, "orb", n_orb, 2) for line in lines]
        last, across[1] = lax.optimization_barrier((last, across[1]))
        across.append(flip(last, "orb", n_orb, 2))
        early = lax.optimization_barrier(tuple(lines + across[:3] + [last]))
        pieces = list(early) + across[3:]
        pieces += [flip(piece, "orb", n_orb, 1) for piece in pieces]
        came = [(0, 0, 0), (1, 0, 0), (2, 0, 0), (0, 2, 0), (1, 2, 0), (2, 2, 0), (3, 0, 1), (3, 2, 1)]
        came += [(s, side ^ 1, ahead) for s, side, ahead in came]
    else:
        kept = jnp.arange(slots, dtype=jnp.int32) < counts[0]
        tiles = jnp.where(kept[:, None, None], integrals, jnp.zeros_like(integrals))
        tiles = tiles.reshape(slots, n_pair, columns, SB, SB).transpose(1, 2, 3, 0, 4)
        tiles = tiles.reshape(n_pair, columns * SB, slots * SB)
        tag = jnp.where(kept[:, None], jnp.stack([mu_block, nu_block], 1), 0).reshape(-1)
        tag = jnp.zeros((n_pair, TAG, LANES), jnp.bfloat16).at[:, :, : 2 * slots].set(tag.astype(jnp.bfloat16))
        packed = jnp.concatenate([tiles, tag], 1)
        line = lax.all_to_all(packed, "pair", split_axis=0, concat_axis=0, tiled=True)
        gathered = lax.all_gather(coeff, ("pair", "orb"), axis=0, tiled=True)
        pieces, came = [lax.all_gather(line, "orb", axis=0, tiled=True), gathered], None
    out = transform(came, n_orb, n_pair * n_orb, orbitals, pieces)
    out = out.reshape(orbitals // n_orb, orbitals // LANES, columns, LANES)
    return out.transpose(0, 2, 1, 3).reshape(orbitals // n_orb, columns, orbitals)


def solution(mesh):
    placed = (
        P(("grp", "pair", "orb"), None, None),
        P(("grp", "pair", "orb")),
        P(("grp", "pair", "orb")),
        P(("grp", "pair", "orb")),
        P(("grp", "pair", "orb"), None),
    )
    return jax.shard_map(
        functools.partial(body, mesh.shape["pair"], mesh.shape["orb"]),
        mesh=mesh,
        in_specs=placed,
        out_specs=P(("grp", "orb"), "pair", None),
        check_vma=False,
    )
```

```python
import functools

import jax
import jax.numpy as jnp
from jax import lax
from jax.experimental import pallas as pl
from jax.experimental.pallas import tpu as pltpu
from jax.sharding import PartitionSpec as P

SB = 64
LANES = 128
TAG = 16
CHUNK = 16


def pack_kernel(n_pair, integrals, mu, nu, counts, coeff, *refs):
    own, one_off, two_off, tiles, shard, mu_in, nu_in, spread, woven, sems = refs
    rows = shard.shape[0] * shard.shape[1] // LANES
    reach = integrals.shape[1] // n_pair * SB + TAG
    tile_spots = ((own, rows), (one_off, rows), (two_off, reach + rows), (two_off, 0))
    shard_spots = ((own, 0), (one_off, 0), (two_off, reach))
    p = lax.axis_index("pair")
    copies = [
        pltpu.make_async_copy(source, target, sems.at[n])
        for n, (source, target) in enumerate(((integrals, tiles), (mu, mu_in), (nu, nu_in), (coeff, shard)))
    ]
    for copy in copies:
        copy.start()
    slots, kets, flat = tiles.shape
    wide = flat // LANES
    columns = kets // n_pair
    held, orbitals = shard.shape
    for copy in copies[1:3]:
        copy.wait()
    count = counts[0]
    lane = lax.broadcasted_iota(jnp.int32, (wide, LANES), 1)
    low, kept = lane < SB, lane < SB * count
    lane = lax.broadcasted_iota(jnp.int32, (TAG, LANES), 1)
    tag = jnp.zeros((TAG, LANES), jnp.int32)
    for t in range(slots):
        tag = jnp.where((lane == 2 * t) & (t < count), mu_in[t], tag)
        tag = jnp.where((lane == 2 * t + 1) & (t < count), nu_in[t], tag)
    tag = tag.astype(jnp.float32).astype(jnp.bfloat16)
    copies[0].wait()
    for t in range(slots):
        for j in range(wide):
            at = pl.ds((t * wide + j) * kets, kets)
            spread[at, :] = tiles[t, :, j * LANES : (j + 1) * LANES].astype(jnp.float32)
    rows = columns * SB
    for s in range(n_pair):
        dest = p ^ s
        for k in range(columns):
            column = dest * columns + k
            one = spread[pl.ds(column, wide, stride=kets), :]
            two = spread[pl.ds(wide * kets + column, wide, stride=kets), :]
            even = jnp.where(low, one, pltpu.roll(two, SB, axis=1))
            odd = jnp.where(low, pltpu.roll(one, SB, axis=1), two)
            begin = (s * columns + k) * SB
            woven[pl.ds(begin, wide, stride=2), :] = jnp.where(kept, even, 0.0)
            woven[pl.ds(begin + 1, wide, stride=2), :] = jnp.where(kept, odd, 0.0)
        target, at = tile_spots[s]
        target[at : at + rows] = woven[pl.ds(s * rows, rows), :].astype(jnp.bfloat16)
        target[at + rows : at + rows + TAG] = tag
    copies[3].wait()
    for j in range(orbitals // LANES):
        lanes = shard[:, j * LANES : (j + 1) * LANES]
        for target, at in shard_spots:
            target[at + j * held : at + (j + 1) * held] = lanes


def pack(n_pair, integrals, mu, nu, counts, coeff):
    slots, kets, flat = integrals.shape
    reach = kets // n_pair * SB + TAG
    rows = coeff.shape[0] * coeff.shape[1] // LANES + reach
    hbm, smem = pl.BlockSpec(memory_space=pltpu.HBM), pl.BlockSpec(memory_space=pltpu.SMEM)
    return pl.pallas_call(
        functools.partial(pack_kernel, n_pair),
        out_shape=[pltpu.VMEM((size, LANES), jnp.bfloat16) for size in (rows, rows, rows + reach)],
        in_specs=[hbm, hbm, hbm, smem, hbm],
        out_specs=[pl.BlockSpec(memory_space=pltpu.VMEM)] * 3,
        scratch_shapes=[
            pltpu.VMEM(integrals.shape, jnp.bfloat16),
            pltpu.VMEM(coeff.shape, jnp.bfloat16),
            pltpu.SMEM(mu.shape, jnp.int32),
            pltpu.SMEM(nu.shape, jnp.int32),
            pltpu.VMEM((slots * kets * flat // LANES, LANES), jnp.float32),
            pltpu.VMEM((kets * SB, LANES), jnp.float32),
            pltpu.SemaphoreType.DMA((4,)),
        ],
        compiler_params=pltpu.CompilerParams(vmem_limit_bytes=56 << 20),
        name="pack",
    )(integrals, mu, nu, counts, coeff)


def transform_kernel(came, n_orb, orbitals, n_in, *refs):
    pieces = refs[:n_in]
    out, c_all, codes, index, half, left, sem = refs[n_in:]
    p, o = lax.axis_index("pair"), lax.axis_index("orb")
    devices = codes.shape[0]
    blocks = orbitals // LANES
    if came:
        rows = c_all.shape[0] // devices
        tile_at = [0 if ahead else blocks * rows for _, _, ahead in came]
        for q, piece in enumerate(pieces):
            codes[q : q + 1, :] = piece[tile_at[q] + 2 * SB : tile_at[q] + 2 * SB + TAG][:1].astype(jnp.float32).astype(jnp.int32)
    else:
        codes[...] = pieces[0][:, 2 * SB :, :][:, 0, :].astype(jnp.float32).astype(jnp.int32)
    to_scalars = pltpu.make_async_copy(codes, index, sem)
    to_scalars.start()
    if came:
        for q, piece in enumerate(pieces):
            begin = 2 * SB + TAG if came[q][2] else 0
            source = (p ^ came[q][0]) * n_orb + (o ^ came[q][1])
            place = pl.ds(pl.multiple_of(source * rows, rows), rows)
            for j in range(blocks):
                c_all[place, j * LANES : (j + 1) * LANES] = piece[begin + j * rows : begin + (j + 1) * rows, :]
    else:
        c_all = pieces[1]
    to_scalars.wait()

    mine = pl.ds(pl.multiple_of(o * LANES, LANES), LANES)
    low = lax.broadcasted_iota(jnp.int32, (SB, LANES), 1) < SB
    chunks = devices // CHUNK

    def rows_of(block):
        return pl.ds(pl.multiple_of(block * SB, SB), SB)

    def chunk_step(chunk, carry):
        for d in range(CHUNK):
            device = chunk * CHUNK + d
            stacked = []
            for k in range(2):
                if came:
                    tile = pieces[d][tile_at[d] + k * SB : tile_at[d] + (k + 1) * SB, :]
                else:
                    tile = pieces[0][device, k * SB : (k + 1) * SB, :]
                stacked += [jnp.where(low, tile, jnp.zeros_like(tile)), jnp.where(low, jnp.zeros_like(tile), tile)]
            mu_one, nu_one, mu_two, nu_two = (index[device, n] for n in range(4))
            rows = jnp.concatenate([c_all[rows_of(nu_one)], c_all[rows_of(nu_two)]], 0)
            moved = jnp.dot(jnp.concatenate(stacked, 0), rows, preferred_element_type=jnp.float32)
            moved = moved.astype(jnp.bfloat16)
            at = pl.ds(d * 2 * SB, 2 * SB)
            half[at, :orbitals] = moved[: 2 * SB]
            half[at, orbitals:] = moved[2 * SB :]
            left[at, :] = jnp.concatenate([c_all[rows_of(mu_one), mine], c_all[rows_of(mu_two), mine]], 0)
        part = lax.dot_general(
            left[...], half[...], (((0,), (0,)), ((), ())), preferred_element_type=jnp.float32
        )
        for k in range(2):
            for j in range(blocks):
                at = pl.ds(2 * j + k, LANES, stride=2 * blocks)
                begin = k * orbitals + j * LANES
                value = part[:, begin : begin + LANES]
                out[at, :] = value if chunks == 1 else out[at, :] + value
        return carry

    if chunks == 1:
        chunk_step(0, 0)
    else:
        out[...] = jnp.zeros_like(out)
        lax.fori_loop(0, chunks, chunk_step, 0)


def transform(came, n_orb, devices, orbitals, pieces):
    wide = CHUNK * 2 * SB
    held = pieces[0].shape[0] - 2 * SB - TAG if came else TAG
    return pl.pallas_call(
        functools.partial(transform_kernel, came, n_orb, orbitals, len(pieces)),
        out_shape=jax.ShapeDtypeStruct((2 * orbitals // LANES * LANES, LANES), jnp.float32),
        in_specs=[pl.BlockSpec(memory_space=pltpu.VMEM)] * len(pieces),
        out_specs=pl.BlockSpec(memory_space=pltpu.VMEM),
        scratch_shapes=[
            pltpu.VMEM((held * LANES // orbitals * devices if came else TAG, orbitals), jnp.bfloat16),
            pltpu.VMEM((devices, LANES), jnp.int32),
            pltpu.SMEM((devices, LANES), jnp.int32),
            pltpu.VMEM((wide, 2 * orbitals), jnp.bfloat16),
            pltpu.VMEM((wide, LANES), jnp.bfloat16),
            pltpu.SemaphoreType.DMA,
        ],
        compiler_params=pltpu.CompilerParams(vmem_limit_bytes=40 << 20),
        name="transform",
    )(*pieces)


def flip(array, axis, size, bit):
    return lax.ppermute(array, axis, [(i, i ^ bit) for i in range(size)])


def body(n_pair, n_orb, integrals, mu_block, nu_block, counts, coeff):
    slots, kets, flat = integrals.shape
    columns = kets // n_pair
    orbitals = coeff.shape[1]
    if n_orb == 4 and n_pair == 4:
        own, one_off, two_off = pack(n_pair, integrals, mu_block, nu_block, counts, coeff)
        size = own.shape[0]
        two = flip(two_off, "pair", n_pair, 2)
        one = flip(one_off, "pair", n_pair, 1)
        own_across = flip(own, "orb", n_orb, 2)
        one, own_across = lax.optimization_barrier((one, own_across))
        one_across = flip(one, "orb", n_orb, 2)
        three = flip(two[:size], "pair", n_pair, 1)
        two = two[two.shape[0] - size :]
        two_across = flip(two, "orb", n_orb, 2)
        pieces = [own, one, two, own_across, one_across]
        swapped = [flip(piece, "orb", n_orb, 1) for piece in pieces]
        three, *swapped = lax.optimization_barrier((three, *swapped))
        pieces += [two_across, three, flip(three, "orb", n_orb, 2)]
        swapped += [flip(piece, "orb", n_orb, 1) for piece in pieces[5:]]
        pieces += swapped
        came = [(0, 0, 0), (1, 0, 0), (2, 0, 0), (0, 2, 0), (1, 2, 0), (2, 2, 0), (3, 0, 1), (3, 2, 1)]
        came += [(s, side ^ 1, ahead) for s, side, ahead in came]
    else:
        kept = jnp.arange(slots, dtype=jnp.int32) < counts[0]
        tiles = jnp.where(kept[:, None, None], integrals, jnp.zeros_like(integrals))
        tiles = tiles.reshape(slots, n_pair, columns, SB, SB).transpose(1, 2, 3, 0, 4)
        tiles = tiles.reshape(n_pair, columns * SB, slots * SB)
        tag = jnp.where(kept[:, None], jnp.stack([mu_block, nu_block], 1), 0).reshape(-1)
        tag = jnp.zeros((n_pair, TAG, LANES), jnp.bfloat16).at[:, :, : 2 * slots].set(tag.astype(jnp.bfloat16))
        packed = jnp.concatenate([tiles, tag], 1)
        line = lax.all_to_all(packed, "pair", split_axis=0, concat_axis=0, tiled=True)
        gathered = lax.all_gather(coeff, ("pair", "orb"), axis=0, tiled=True)
        pieces, came = [lax.all_gather(line, "orb", axis=0, tiled=True), gathered], None
    out = transform(came, n_orb, n_pair * n_orb, orbitals, pieces)
    out = out.reshape(orbitals // n_orb, orbitals // LANES, columns, LANES)
    return out.transpose(0, 2, 1, 3).reshape(orbitals // n_orb, columns, orbitals)


def solution(mesh):
    placed = (
        P(("grp", "pair", "orb"), None, None),
        P(("grp", "pair", "orb")),
        P(("grp", "pair", "orb")),
        P(("grp", "pair", "orb")),
        P(("grp", "pair", "orb"), None),
    )
    return jax.shard_map(
        functools.partial(body, mesh.shape["pair"], mesh.shape["orb"]),
        mesh=mesh,
        in_specs=placed,
        out_specs=P(("grp", "orb"), "pair", None),
        check_vma=False,
    )
```

```python
import functools

import jax
import jax.numpy as jnp
from jax import lax
from jax.experimental import pallas as pl
from jax.experimental.pallas import tpu as pltpu
from jax.sharding import PartitionSpec as P

SB = 64
LANES = 128
TAG = 16
CHUNK = 16


def pack_kernel(n_pair, integrals, mu, nu, counts, coeff, *refs):
    outs = refs[:n_pair]
    tiles, shard, mu_in, nu_in, spread, woven, sems = refs[n_pair:]
    p = lax.axis_index("pair")
    copies = [
        pltpu.make_async_copy(source, target, sems.at[n])
        for n, (source, target) in enumerate(((integrals, tiles), (mu, mu_in), (nu, nu_in), (coeff, shard)))
    ]
    for copy in copies:
        copy.start()
    slots, kets, flat = tiles.shape
    wide = flat // LANES
    columns = kets // n_pair
    held, orbitals = shard.shape
    for copy in copies[1:3]:
        copy.wait()
    count = counts[0]
    lane = lax.broadcasted_iota(jnp.int32, (wide, LANES), 1)
    low, kept = lane < SB, lane < SB * count
    lane = lax.broadcasted_iota(jnp.int32, (TAG, LANES), 1)
    tag = jnp.zeros((TAG, LANES), jnp.int32)
    for t in range(slots):
        tag = jnp.where((lane == 2 * t) & (t < count), mu_in[t], tag)
        tag = jnp.where((lane == 2 * t + 1) & (t < count), nu_in[t], tag)
    tag = tag.astype(jnp.float32).astype(jnp.bfloat16)
    copies[0].wait()
    for t in range(slots):
        for j in range(wide):
            at = pl.ds((t * wide + j) * kets, kets)
            spread[at, :] = tiles[t, :, j * LANES : (j + 1) * LANES].astype(jnp.float32)
    tile_at, rows = orbitals // LANES * held, columns * SB
    for s in range(n_pair):
        dest = p ^ s
        for k in range(columns):
            column = dest * columns + k
            one = spread[pl.ds(column, wide, stride=kets), :]
            two = spread[pl.ds(wide * kets + column, wide, stride=kets), :]
            even = jnp.where(low, one, pltpu.roll(two, SB, axis=1))
            odd = jnp.where(low, pltpu.roll(one, SB, axis=1), two)
            begin = (s * columns + k) * SB
            woven[pl.ds(begin, wide, stride=2), :] = jnp.where(kept, even, 0.0)
            woven[pl.ds(begin + 1, wide, stride=2), :] = jnp.where(kept, odd, 0.0)
        outs[s][tile_at : tile_at + rows] = woven[pl.ds(s * rows, rows), :].astype(jnp.bfloat16)
        outs[s][tile_at + rows :] = tag
    copies[3].wait()
    for j in range(orbitals // LANES):
        lanes = shard[:, j * LANES : (j + 1) * LANES]
        for s in range(n_pair):
            outs[s][j * held : (j + 1) * held] = lanes


def pack(n_pair, integrals, mu, nu, counts, coeff):
    slots, kets, flat = integrals.shape
    rows = coeff.shape[0] * coeff.shape[1] // LANES + kets // n_pair * SB + TAG
    hbm, smem = pl.BlockSpec(memory_space=pltpu.HBM), pl.BlockSpec(memory_space=pltpu.SMEM)
    return pl.pallas_call(
        functools.partial(pack_kernel, n_pair),
        out_shape=[pltpu.VMEM((rows, LANES), jnp.bfloat16)] * n_pair,
        in_specs=[hbm, hbm, hbm, smem, hbm],
        out_specs=[pl.BlockSpec(memory_space=pltpu.VMEM)] * n_pair,
        scratch_shapes=[
            pltpu.VMEM(integrals.shape, jnp.bfloat16),
            pltpu.VMEM(coeff.shape, jnp.bfloat16),
            pltpu.SMEM(mu.shape, jnp.int32),
            pltpu.SMEM(nu.shape, jnp.int32),
            pltpu.VMEM((slots * kets * flat // LANES, LANES), jnp.float32),
            pltpu.VMEM((kets * SB, LANES), jnp.float32),
            pltpu.SemaphoreType.DMA((4,)),
        ],
        compiler_params=pltpu.CompilerParams(vmem_limit_bytes=56 << 20),
        name="pack",
    )(integrals, mu, nu, counts, coeff)


def transform_kernel(came, n_orb, orbitals, n_in, *refs):
    pieces = refs[:n_in]
    out, c_all, codes, index, half, left, sem = refs[n_in:]
    p, o = lax.axis_index("pair"), lax.axis_index("orb")
    devices = codes.shape[0]
    blocks = orbitals // LANES
    tile_at = pieces[0].shape[-2] - TAG - 2 * SB
    if came:
        for q, piece in enumerate(pieces):
            codes[q : q + 1, :] = piece[tile_at + 2 * SB :][:1].astype(jnp.float32).astype(jnp.int32)
    else:
        codes[...] = pieces[0][:, 2 * SB :, :][:, 0, :].astype(jnp.float32).astype(jnp.int32)
    to_scalars = pltpu.make_async_copy(codes, index, sem)
    to_scalars.start()
    if came:
        rows = c_all.shape[0] // devices
        for q, piece in enumerate(pieces):
            source = (p ^ came[q][0]) * n_orb + (o ^ came[q][1])
            place = pl.ds(pl.multiple_of(source * rows, rows), rows)
            for j in range(blocks):
                c_all[place, j * LANES : (j + 1) * LANES] = piece[j * rows : (j + 1) * rows, :]
    else:
        c_all = pieces[1]
    to_scalars.wait()

    mine = pl.ds(pl.multiple_of(o * LANES, LANES), LANES)
    low = lax.broadcasted_iota(jnp.int32, (SB, LANES), 1) < SB
    chunks = devices // CHUNK

    def rows_of(block):
        return pl.ds(pl.multiple_of(block * SB, SB), SB)

    def chunk_step(chunk, carry):
        for d in range(CHUNK):
            device = chunk * CHUNK + d
            stacked = []
            for k in range(2):
                if came:
                    tile = pieces[d][tile_at + k * SB : tile_at + (k + 1) * SB, :]
                else:
                    tile = pieces[0][device, k * SB : (k + 1) * SB, :]
                stacked += [jnp.where(low, tile, jnp.zeros_like(tile)), jnp.where(low, jnp.zeros_like(tile), tile)]
            mu_one, nu_one, mu_two, nu_two = (index[device, n] for n in range(4))
            rows = jnp.concatenate([c_all[rows_of(nu_one)], c_all[rows_of(nu_two)]], 0)
            moved = jnp.dot(jnp.concatenate(stacked, 0), rows, preferred_element_type=jnp.float32)
            moved = moved.astype(jnp.bfloat16)
            at = pl.ds(d * 2 * SB, 2 * SB)
            half[at, :orbitals] = moved[: 2 * SB]
            half[at, orbitals:] = moved[2 * SB :]
            left[at, :] = jnp.concatenate([c_all[rows_of(mu_one), mine], c_all[rows_of(mu_two), mine]], 0)
        part = lax.dot_general(
            left[...], half[...], (((0,), (0,)), ((), ())), preferred_element_type=jnp.float32
        )
        for k in range(2):
            for j in range(blocks):
                at = pl.ds(2 * j + k, LANES, stride=2 * blocks)
                begin = k * orbitals + j * LANES
                value = part[:, begin : begin + LANES]
                out[at, :] = value if chunks == 1 else out[at, :] + value
        return carry

    if chunks == 1:
        chunk_step(0, 0)
    else:
        out[...] = jnp.zeros_like(out)
        lax.fori_loop(0, chunks, chunk_step, 0)


def transform(came, n_orb, devices, orbitals, pieces):
    wide = CHUNK * 2 * SB
    held = pieces[0].shape[0] - 2 * SB - TAG if came else TAG
    return pl.pallas_call(
        functools.partial(transform_kernel, came, n_orb, orbitals, len(pieces)),
        out_shape=jax.ShapeDtypeStruct((2 * orbitals // LANES * LANES, LANES), jnp.float32),
        in_specs=[pl.BlockSpec(memory_space=pltpu.VMEM)] * len(pieces),
        out_specs=pl.BlockSpec(memory_space=pltpu.VMEM),
        scratch_shapes=[
            pltpu.VMEM((held * LANES // orbitals * devices if came else TAG, orbitals), jnp.bfloat16),
            pltpu.VMEM((devices, LANES), jnp.int32),
            pltpu.SMEM((devices, LANES), jnp.int32),
            pltpu.VMEM((wide, 2 * orbitals), jnp.bfloat16),
            pltpu.VMEM((wide, LANES), jnp.bfloat16),
            pltpu.SemaphoreType.DMA,
        ],
        compiler_params=pltpu.CompilerParams(vmem_limit_bytes=40 << 20),
        name="transform",
    )(*pieces)


def flip(array, axis, size, bit):
    return lax.ppermute(array, axis, [(i, i ^ bit) for i in range(size)])


def body(n_pair, n_orb, integrals, mu_block, nu_block, counts, coeff):
    slots, kets, flat = integrals.shape
    columns = kets // n_pair
    orbitals = coeff.shape[1]
    if n_orb == 4 and n_pair == 4:
        packed = list(pack(n_pair, integrals, mu_block, nu_block, counts, coeff))
        lines = packed[:1] + [flip(packed[s], "pair", n_pair, s) for s in range(1, n_pair)]
        across = [None, flip(lines[1], "orb", n_orb, 2)]
        lines[0], lines[1] = lax.optimization_barrier((lines[0], lines[1]))
        across[0] = flip(lines[0], "orb", n_orb, 2)
        lines[2], across[1] = lax.optimization_barrier((lines[2], across[1]))
        across.append(flip(lines[2], "orb", n_orb, 2))
        swapped = [flip(piece, "orb", n_orb, 1) for piece in lines[:2]]
        last, across[1], *swapped = lax.optimization_barrier((lines[3], across[1], *swapped))
        across.append(flip(last, "orb", n_orb, 2))
        later = list(lax.optimization_barrier(tuple([lines[2], last] + across[:3]))) + across[3:]
        swapped += [flip(piece, "orb", n_orb, 1) for piece in later]
        pieces = lines[:2] + later + swapped
        came = [(0, 0), (1, 0), (2, 0), (3, 0), (0, 2), (1, 2), (2, 2), (3, 2)]
        came += [(s, side ^ 1) for s, side in came]
    else:
        kept = jnp.arange(slots, dtype=jnp.int32) < counts[0]
        tiles = jnp.where(kept[:, None, None], integrals, jnp.zeros_like(integrals))
        tiles = tiles.reshape(slots, n_pair, columns, SB, SB).transpose(1, 2, 3, 0, 4)
        tiles = tiles.reshape(n_pair, columns * SB, slots * SB)
        tag = jnp.where(kept[:, None], jnp.stack([mu_block, nu_block], 1), 0).reshape(-1)
        tag = jnp.zeros((n_pair, TAG, LANES), jnp.bfloat16).at[:, :, : 2 * slots].set(tag.astype(jnp.bfloat16))
        packed = jnp.concatenate([tiles, tag], 1)
        line = lax.all_to_all(packed, "pair", split_axis=0, concat_axis=0, tiled=True)
        gathered = lax.all_gather(coeff, ("pair", "orb"), axis=0, tiled=True)
        pieces, came = [lax.all_gather(line, "orb", axis=0, tiled=True), gathered], None
    out = transform(came, n_orb, n_pair * n_orb, orbitals, pieces)
    out = out.reshape(orbitals // n_orb, orbitals // LANES, columns, LANES)
    return out.transpose(0, 2, 1, 3).reshape(orbitals // n_orb, columns, orbitals)


def solution(mesh):
    placed = (
        P(("grp", "pair", "orb"), None, None),
        P(("grp", "pair", "orb")),
        P(("grp", "pair", "orb")),
        P(("grp", "pair", "orb")),
        P(("grp", "pair", "orb"), None),
    )
    return jax.shard_map(
        functools.partial(body, mesh.shape["pair"], mesh.shape["orb"]),
        mesh=mesh,
        in_specs=placed,
        out_specs=P(("grp", "orb"), "pair", None),
        check_vma=False,
    )
```

```python
import functools

import jax
import jax.numpy as jnp
from jax import lax
from jax.experimental import pallas as pl
from jax.experimental.pallas import tpu as pltpu
from jax.sharding import PartitionSpec as P

SB = 64
LANES = 128
TAG = 16
CHUNK = 16


def pack_kernel(n_pair, integrals, mu, nu, counts, coeff, *refs):
    outs = refs[:n_pair]
    tiles, shard, mu_in, nu_in, spread, woven, sems = refs[n_pair:]
    p = lax.axis_index("pair")
    copies = [
        pltpu.make_async_copy(source, target, sems.at[n])
        for n, (source, target) in enumerate(((integrals, tiles), (mu, mu_in), (nu, nu_in), (coeff, shard)))
    ]
    for copy in copies:
        copy.start()
    slots, kets, flat = tiles.shape
    wide = flat // LANES
    columns = kets // n_pair
    held, orbitals = shard.shape
    for copy in copies[1:3]:
        copy.wait()
    count = counts[0]
    lane = lax.broadcasted_iota(jnp.int32, (wide, LANES), 1)
    low, kept = lane < SB, lane < SB * count
    lane = lax.broadcasted_iota(jnp.int32, (TAG, LANES), 1)
    tag = jnp.zeros((TAG, LANES), jnp.int32)
    for t in range(slots):
        tag = jnp.where((lane == 2 * t) & (t < count), mu_in[t], tag)
        tag = jnp.where((lane == 2 * t + 1) & (t < count), nu_in[t], tag)
    tag = tag.astype(jnp.float32).astype(jnp.bfloat16)
    copies[0].wait()
    for t in range(slots):
        for j in range(wide):
            at = pl.ds((t * wide + j) * kets, kets)
            spread[at, :] = tiles[t, :, j * LANES : (j + 1) * LANES].astype(jnp.float32)
    tile_at, rows = orbitals // LANES * held, columns * SB
    for s in range(n_pair):
        dest = p ^ s
        for k in range(columns):
            column = dest * columns + k
            one = spread[pl.ds(column, wide, stride=kets), :]
            two = spread[pl.ds(wide * kets + column, wide, stride=kets), :]
            even = jnp.where(low, one, pltpu.roll(two, SB, axis=1))
            odd = jnp.where(low, pltpu.roll(one, SB, axis=1), two)
            begin = (s * columns + k) * SB
            woven[pl.ds(begin, wide, stride=2), :] = jnp.where(kept, even, 0.0)
            woven[pl.ds(begin + 1, wide, stride=2), :] = jnp.where(kept, odd, 0.0)
        outs[s][tile_at : tile_at + rows] = woven[pl.ds(s * rows, rows), :].astype(jnp.bfloat16)
        outs[s][tile_at + rows :] = tag
    copies[3].wait()
    for j in range(orbitals // LANES):
        lanes = shard[:, j * LANES : (j + 1) * LANES]
        for s in range(n_pair):
            outs[s][j * held : (j + 1) * held] = lanes


def pack(n_pair, integrals, mu, nu, counts, coeff):
    slots, kets, flat = integrals.shape
    rows = coeff.shape[0] * coeff.shape[1] // LANES + kets // n_pair * SB + TAG
    hbm, smem = pl.BlockSpec(memory_space=pltpu.HBM), pl.BlockSpec(memory_space=pltpu.SMEM)
    return pl.pallas_call(
        functools.partial(pack_kernel, n_pair),
        out_shape=[pltpu.VMEM((rows, LANES), jnp.bfloat16)] * n_pair,
        in_specs=[hbm, hbm, hbm, smem, hbm],
        out_specs=[pl.BlockSpec(memory_space=pltpu.VMEM)] * n_pair,
        scratch_shapes=[
            pltpu.VMEM(integrals.shape, jnp.bfloat16),
            pltpu.VMEM(coeff.shape, jnp.bfloat16),
            pltpu.SMEM(mu.shape, jnp.int32),
            pltpu.SMEM(nu.shape, jnp.int32),
            pltpu.VMEM((slots * kets * flat // LANES, LANES), jnp.float32),
            pltpu.VMEM((kets * SB, LANES), jnp.float32),
            pltpu.SemaphoreType.DMA((4,)),
        ],
        compiler_params=pltpu.CompilerParams(vmem_limit_bytes=56 << 20),
        name="pack",
    )(integrals, mu, nu, counts, coeff)


def transform_kernel(came, n_orb, orbitals, n_in, *refs):
    pieces = refs[:n_in]
    out, c_all, codes, index, half, left, sem = refs[n_in:]
    p, o = lax.axis_index("pair"), lax.axis_index("orb")
    devices = codes.shape[0]
    blocks = orbitals // LANES
    tile_at = pieces[0].shape[-2] - TAG - 2 * SB
    if came:
        for q, piece in enumerate(pieces):
            codes[q : q + 1, :] = piece[tile_at + 2 * SB :][:1].astype(jnp.float32).astype(jnp.int32)
    else:
        codes[...] = pieces[0][:, 2 * SB :, :][:, 0, :].astype(jnp.float32).astype(jnp.int32)
    to_scalars = pltpu.make_async_copy(codes, index, sem)
    to_scalars.start()
    if came:
        rows = c_all.shape[0] // devices
        for q, piece in enumerate(pieces):
            source = (p ^ came[q][0]) * n_orb + (o ^ came[q][1])
            place = pl.ds(pl.multiple_of(source * rows, rows), rows)
            for j in range(blocks):
                c_all[place, j * LANES : (j + 1) * LANES] = piece[j * rows : (j + 1) * rows, :]
    else:
        c_all = pieces[1]
    to_scalars.wait()

    mine = pl.ds(pl.multiple_of(o * LANES, LANES), LANES)
    low = lax.broadcasted_iota(jnp.int32, (SB, LANES), 1) < SB
    chunks = devices // CHUNK

    def rows_of(block):
        return pl.ds(pl.multiple_of(block * SB, SB), SB)

    def chunk_step(chunk, carry):
        for d in range(CHUNK):
            device = chunk * CHUNK + d
            stacked = []
            for k in range(2):
                if came:
                    tile = pieces[d][tile_at + k * SB : tile_at + (k + 1) * SB, :]
                else:
                    tile = pieces[0][device, k * SB : (k + 1) * SB, :]
                stacked += [jnp.where(low, tile, jnp.zeros_like(tile)), jnp.where(low, jnp.zeros_like(tile), tile)]
            mu_one, nu_one, mu_two, nu_two = (index[device, n] for n in range(4))
            rows = jnp.concatenate([c_all[rows_of(nu_one)], c_all[rows_of(nu_two)]], 0)
            moved = jnp.dot(jnp.concatenate(stacked, 0), rows, preferred_element_type=jnp.float32)
            moved = moved.astype(jnp.bfloat16)
            at = pl.ds(d * 2 * SB, 2 * SB)
            half[at, :orbitals] = moved[: 2 * SB]
            half[at, orbitals:] = moved[2 * SB :]
            left[at, :] = jnp.concatenate([c_all[rows_of(mu_one), mine], c_all[rows_of(mu_two), mine]], 0)
        part = lax.dot_general(
            left[...], half[...], (((0,), (0,)), ((), ())), preferred_element_type=jnp.float32
        )
        for k in range(2):
            for j in range(blocks):
                at = pl.ds(2 * j + k, LANES, stride=2 * blocks)
                begin = k * orbitals + j * LANES
                value = part[:, begin : begin + LANES]
                out[at, :] = value if chunks == 1 else out[at, :] + value
        return carry

    if chunks == 1:
        chunk_step(0, 0)
    else:
        out[...] = jnp.zeros_like(out)
        lax.fori_loop(0, chunks, chunk_step, 0)


def transform(came, n_orb, devices, orbitals, pieces):
    wide = CHUNK * 2 * SB
    held = pieces[0].shape[0] - 2 * SB - TAG if came else TAG
    return pl.pallas_call(
        functools.partial(transform_kernel, came, n_orb, orbitals, len(pieces)),
        out_shape=jax.ShapeDtypeStruct((2 * orbitals // LANES * LANES, LANES), jnp.float32),
        in_specs=[pl.BlockSpec(memory_space=pltpu.VMEM)] * len(pieces),
        out_specs=pl.BlockSpec(memory_space=pltpu.VMEM),
        scratch_shapes=[
            pltpu.VMEM((held * LANES // orbitals * devices if came else TAG, orbitals), jnp.bfloat16),
            pltpu.VMEM((devices, LANES), jnp.int32),
            pltpu.SMEM((devices, LANES), jnp.int32),
            pltpu.VMEM((wide, 2 * orbitals), jnp.bfloat16),
            pltpu.VMEM((wide, LANES), jnp.bfloat16),
            pltpu.SemaphoreType.DMA,
        ],
        compiler_params=pltpu.CompilerParams(vmem_limit_bytes=40 << 20),
        name="transform",
    )(*pieces)


def flip(array, axis, size, bit):
    return lax.ppermute(array, axis, [(i, i ^ bit) for i in range(size)])


def body(n_pair, n_orb, integrals, mu_block, nu_block, counts, coeff):
    slots, kets, flat = integrals.shape
    columns = kets // n_pair
    orbitals = coeff.shape[1]
    if n_orb == 4 and n_pair == 4:
        packed = list(pack(n_pair, integrals, mu_block, nu_block, counts, coeff))
        lines = packed[:1] + [flip(packed[s], "pair", n_pair, s) for s in range(1, n_pair)]
        across = [flip(line, "orb", n_orb, 2) for line in lines[:3]]
        last, across[1] = lax.optimization_barrier((lines[3], across[1]))
        across.append(flip(last, "orb", n_orb, 2))
        first = list(lax.optimization_barrier((lines[0], lines[1], last)))[:2]
        swapped = [flip(piece, "orb", n_orb, 1) for piece in first]
        later = list(lax.optimization_barrier((lines[2], last, *across[:3]))) + across[3:]
        swapped += [flip(piece, "orb", n_orb, 1) for piece in later]
        pieces = first + later + swapped
        came = [(0, 0), (1, 0), (2, 0), (3, 0), (0, 2), (1, 2), (2, 2), (3, 2)]
        came += [(s, side ^ 1) for s, side in came]
    else:
        kept = jnp.arange(slots, dtype=jnp.int32) < counts[0]
        tiles = jnp.where(kept[:, None, None], integrals, jnp.zeros_like(integrals))
        tiles = tiles.reshape(slots, n_pair, columns, SB, SB).transpose(1, 2, 3, 0, 4)
        tiles = tiles.reshape(n_pair, columns * SB, slots * SB)
        tag = jnp.where(kept[:, None], jnp.stack([mu_block, nu_block], 1), 0).reshape(-1)
        tag = jnp.zeros((n_pair, TAG, LANES), jnp.bfloat16).at[:, :, : 2 * slots].set(tag.astype(jnp.bfloat16))
        packed = jnp.concatenate([tiles, tag], 1)
        line = lax.all_to_all(packed, "pair", split_axis=0, concat_axis=0, tiled=True)
        gathered = lax.all_gather(coeff, ("pair", "orb"), axis=0, tiled=True)
        pieces, came = [lax.all_gather(line, "orb", axis=0, tiled=True), gathered], None
    out = transform(came, n_orb, n_pair * n_orb, orbitals, pieces)
    out = out.reshape(orbitals // n_orb, orbitals // LANES, columns, LANES)
    return out.transpose(0, 2, 1, 3).reshape(orbitals // n_orb, columns, orbitals)


def solution(mesh):
    placed = (
        P(("grp", "pair", "orb"), None, None),
        P(("grp", "pair", "orb")),
        P(("grp", "pair", "orb")),
        P(("grp", "pair", "orb")),
        P(("grp", "pair", "orb"), None),
    )
    return jax.shard_map(
        functools.partial(body, mesh.shape["pair"], mesh.shape["orb"]),
        mesh=mesh,
        in_specs=placed,
        out_specs=P(("grp", "orb"), "pair", None),
        check_vma=False,
    )
```

```python
import functools

import jax
import jax.numpy as jnp
from jax import lax
from jax.experimental import pallas as pl
from jax.experimental.pallas import tpu as pltpu
from jax.sharding import PartitionSpec as P

SB = 64
LANES = 128
TAG = 16
CHUNK = 16


def pack_kernel(n_pair, integrals, mu, nu, counts, coeff, *refs):
    outs = refs[:n_pair]
    tiles, shard, mu_in, nu_in, spread, woven, sems = refs[n_pair:]
    p = lax.axis_index("pair")
    copies = [
        pltpu.make_async_copy(source, target, sems.at[n])
        for n, (source, target) in enumerate(((integrals, tiles), (mu, mu_in), (nu, nu_in), (coeff, shard)))
    ]
    for copy in copies:
        copy.start()
    slots, kets, flat = tiles.shape
    wide = flat // LANES
    columns = kets // n_pair
    held, orbitals = shard.shape
    for copy in copies[1:3]:
        copy.wait()
    count = counts[0]
    lane = lax.broadcasted_iota(jnp.int32, (wide, LANES), 1)
    low, kept = lane < SB, lane < SB * count
    lane = lax.broadcasted_iota(jnp.int32, (TAG, LANES), 1)
    tag = jnp.zeros((TAG, LANES), jnp.int32)
    for t in range(slots):
        tag = jnp.where((lane == 2 * t) & (t < count), mu_in[t], tag)
        tag = jnp.where((lane == 2 * t + 1) & (t < count), nu_in[t], tag)
    tag = tag.astype(jnp.float32).astype(jnp.bfloat16)
    copies[0].wait()
    for t in range(slots):
        for j in range(wide):
            at = pl.ds((t * wide + j) * kets, kets)
            spread[at, :] = tiles[t, :, j * LANES : (j + 1) * LANES].astype(jnp.float32)
    tile_at, rows = orbitals // LANES * held, columns * SB
    for s in range(n_pair):
        dest = p ^ s
        for k in range(columns):
            column = dest * columns + k
            one = spread[pl.ds(column, wide, stride=kets), :]
            two = spread[pl.ds(wide * kets + column, wide, stride=kets), :]
            even = jnp.where(low, one, pltpu.roll(two, SB, axis=1))
            odd = jnp.where(low, pltpu.roll(one, SB, axis=1), two)
            begin = (s * columns + k) * SB
            woven[pl.ds(begin, wide, stride=2), :] = jnp.where(kept, even, 0.0)
            woven[pl.ds(begin + 1, wide, stride=2), :] = jnp.where(kept, odd, 0.0)
        outs[s][tile_at : tile_at + rows] = woven[pl.ds(s * rows, rows), :].astype(jnp.bfloat16)
        outs[s][tile_at + rows :] = tag
    copies[3].wait()
    for j in range(orbitals // LANES):
        lanes = shard[:, j * LANES : (j + 1) * LANES]
        for s in range(n_pair):
            outs[s][j * held : (j + 1) * held] = lanes


def pack(n_pair, integrals, mu, nu, counts, coeff):
    slots, kets, flat = integrals.shape
    rows = coeff.shape[0] * coeff.shape[1] // LANES + kets // n_pair * SB + TAG
    hbm, smem = pl.BlockSpec(memory_space=pltpu.HBM), pl.BlockSpec(memory_space=pltpu.SMEM)
    return pl.pallas_call(
        functools.partial(pack_kernel, n_pair),
        out_shape=[pltpu.VMEM((rows, LANES), jnp.bfloat16)] * n_pair,
        in_specs=[hbm, hbm, hbm, smem, hbm],
        out_specs=[pl.BlockSpec(memory_space=pltpu.VMEM)] * n_pair,
        scratch_shapes=[
            pltpu.VMEM(integrals.shape, jnp.bfloat16),
            pltpu.VMEM(coeff.shape, jnp.bfloat16),
            pltpu.SMEM(mu.shape, jnp.int32),
            pltpu.SMEM(nu.shape, jnp.int32),
            pltpu.VMEM((slots * kets * flat // LANES, LANES), jnp.float32),
            pltpu.VMEM((kets * SB, LANES), jnp.float32),
            pltpu.SemaphoreType.DMA((4,)),
        ],
        compiler_params=pltpu.CompilerParams(vmem_limit_bytes=56 << 20),
        name="pack",
    )(integrals, mu, nu, counts, coeff)


def transform_kernel(came, n_orb, orbitals, n_in, *refs):
    pieces = refs[:n_in]
    out, c_all, codes, index, half, left, sem = refs[n_in:]
    p, o = lax.axis_index("pair"), lax.axis_index("orb")
    devices = codes.shape[0]
    blocks = orbitals // LANES
    tile_at = pieces[0].shape[-2] - TAG - 2 * SB
    if came:
        for q, piece in enumerate(pieces):
            codes[q : q + 1, :] = piece[tile_at + 2 * SB :][:1].astype(jnp.float32).astype(jnp.int32)
    else:
        codes[...] = pieces[0][:, 2 * SB :, :][:, 0, :].astype(jnp.float32).astype(jnp.int32)
    to_scalars = pltpu.make_async_copy(codes, index, sem)
    to_scalars.start()
    if came:
        rows = c_all.shape[0] // devices
        for q, piece in enumerate(pieces):
            source = (p ^ came[q][0]) * n_orb + (o ^ came[q][1])
            place = pl.ds(pl.multiple_of(source * rows, rows), rows)
            for j in range(blocks):
                c_all[place, j * LANES : (j + 1) * LANES] = piece[j * rows : (j + 1) * rows, :]
    else:
        c_all = pieces[1]
    to_scalars.wait()

    mine = pl.ds(pl.multiple_of(o * LANES, LANES), LANES)
    low = lax.broadcasted_iota(jnp.int32, (SB, LANES), 1) < SB
    chunks = devices // CHUNK

    def rows_of(block):
        return pl.ds(pl.multiple_of(block * SB, SB), SB)

    def chunk_step(chunk, carry):
        for d in range(CHUNK):
            device = chunk * CHUNK + d
            stacked = []
            for k in range(2):
                if came:
                    tile = pieces[d][tile_at + k * SB : tile_at + (k + 1) * SB, :]
                else:
                    tile = pieces[0][device, k * SB : (k + 1) * SB, :]
                stacked += [jnp.where(low, tile, jnp.zeros_like(tile)), jnp.where(low, jnp.zeros_like(tile), tile)]
            mu_one, nu_one, mu_two, nu_two = (index[device, n] for n in range(4))
            rows = jnp.concatenate([c_all[rows_of(nu_one)], c_all[rows_of(nu_two)]], 0)
            moved = jnp.dot(jnp.concatenate(stacked, 0), rows, preferred_element_type=jnp.float32)
            moved = moved.astype(jnp.bfloat16)
            at = pl.ds(d * 2 * SB, 2 * SB)
            half[at, :orbitals] = moved[: 2 * SB]
            half[at, orbitals:] = moved[2 * SB :]
            left[:, at] = jnp.concatenate([c_all[rows_of(mu_one), mine], c_all[rows_of(mu_two), mine]], 0).T
        part = jnp.dot(left[...], half[...], preferred_element_type=jnp.float32)
        for k in range(2):
            for j in range(blocks):
                at = pl.ds(2 * j + k, LANES, stride=2 * blocks)
                begin = k * orbitals + j * LANES
                value = part[:, begin : begin + LANES]
                out[at, :] = value if chunks == 1 else out[at, :] + value
        return carry

    if chunks == 1:
        chunk_step(0, 0)
    else:
        out[...] = jnp.zeros_like(out)
        lax.fori_loop(0, chunks, chunk_step, 0)


def transform(came, n_orb, devices, orbitals, pieces):
    wide = CHUNK * 2 * SB
    held = pieces[0].shape[0] - 2 * SB - TAG if came else TAG
    return pl.pallas_call(
        functools.partial(transform_kernel, came, n_orb, orbitals, len(pieces)),
        out_shape=jax.ShapeDtypeStruct((2 * orbitals // LANES * LANES, LANES), jnp.float32),
        in_specs=[pl.BlockSpec(memory_space=pltpu.VMEM)] * len(pieces),
        out_specs=pl.BlockSpec(memory_space=pltpu.VMEM),
        scratch_shapes=[
            pltpu.VMEM((held * LANES // orbitals * devices if came else TAG, orbitals), jnp.bfloat16),
            pltpu.VMEM((devices, LANES), jnp.int32),
            pltpu.SMEM((devices, LANES), jnp.int32),
            pltpu.VMEM((wide, 2 * orbitals), jnp.bfloat16),
            pltpu.VMEM((LANES, wide), jnp.bfloat16),
            pltpu.SemaphoreType.DMA,
        ],
        compiler_params=pltpu.CompilerParams(vmem_limit_bytes=40 << 20),
        name="transform",
    )(*pieces)


def flip(array, axis, size, bit):
    return lax.ppermute(array, axis, [(i, i ^ bit) for i in range(size)])


def body(n_pair, n_orb, integrals, mu_block, nu_block, counts, coeff):
    slots, kets, flat = integrals.shape
    columns = kets // n_pair
    orbitals = coeff.shape[1]
    if n_orb == 4 and n_pair == 4:
        packed = list(pack(n_pair, integrals, mu_block, nu_block, counts, coeff))
        lines = packed[:1] + [flip(packed[s], "pair", n_pair, s) for s in range(1, n_pair)]
        across = [flip(line, "orb", n_orb, 2) for line in lines[:3]]
        last, across[1] = lax.optimization_barrier((lines[3], across[1]))
        across.append(flip(last, "orb", n_orb, 2))
        first = list(lax.optimization_barrier((lines[0], lines[1], last)))[:2]
        swapped = [flip(piece, "orb", n_orb, 1) for piece in first]
        later = list(lax.optimization_barrier((lines[2], last, *across[:3]))) + across[3:]
        swapped += [flip(piece, "orb", n_orb, 1) for piece in later]
        pieces = first + later + swapped
        came = [(0, 0), (1, 0), (2, 0), (3, 0), (0, 2), (1, 2), (2, 2), (3, 2)]
        came += [(s, side ^ 1) for s, side in came]
    else:
        kept = jnp.arange(slots, dtype=jnp.int32) < counts[0]
        tiles = jnp.where(kept[:, None, None], integrals, jnp.zeros_like(integrals))
        tiles = tiles.reshape(slots, n_pair, columns, SB, SB).transpose(1, 2, 3, 0, 4)
        tiles = tiles.reshape(n_pair, columns * SB, slots * SB)
        tag = jnp.where(kept[:, None], jnp.stack([mu_block, nu_block], 1), 0).reshape(-1)
        tag = jnp.zeros((n_pair, TAG, LANES), jnp.bfloat16).at[:, :, : 2 * slots].set(tag.astype(jnp.bfloat16))
        packed = jnp.concatenate([tiles, tag], 1)
        line = lax.all_to_all(packed, "pair", split_axis=0, concat_axis=0, tiled=True)
        gathered = lax.all_gather(coeff, ("pair", "orb"), axis=0, tiled=True)
        pieces, came = [lax.all_gather(line, "orb", axis=0, tiled=True), gathered], None
    out = transform(came, n_orb, n_pair * n_orb, orbitals, pieces)
    out = out.reshape(orbitals // n_orb, orbitals // LANES, columns, LANES)
    return out.transpose(0, 2, 1, 3).reshape(orbitals // n_orb, columns, orbitals)


def solution(mesh):
    placed = (
        P(("grp", "pair", "orb"), None, None),
        P(("grp", "pair", "orb")),
        P(("grp", "pair", "orb")),
        P(("grp", "pair", "orb")),
        P(("grp", "pair", "orb"), None),
    )
    return jax.shard_map(
        functools.partial(body, mesh.shape["pair"], mesh.shape["orb"]),
        mesh=mesh,
        in_specs=placed,
        out_specs=P(("grp", "orb"), "pair", None),
        check_vma=False,
    )
```

```python
import functools

import jax
import jax.numpy as jnp
from jax import lax
from jax.experimental import pallas as pl
from jax.experimental.pallas import tpu as pltpu
from jax.sharding import PartitionSpec as P

SB = 64
LANES = 128
TAG = 16
PARTS = 8
CHUNK = 16


def pack_kernel(n_pair, integrals, mu, nu, counts, coeff, *refs):
    outs = refs[:n_pair]
    tiles, shard, mu_in, nu_in, spread, woven, sems = refs[n_pair:]
    p = lax.axis_index("pair")
    slots, kets, flat = tiles.shape
    ends = [(mu, mu_in), (nu, nu_in)]
    for n in range(PARTS):
        lanes = pl.ds(n * (flat // PARTS), flat // PARTS)
        ends.append((integrals.at[:, :, lanes], tiles.at[:, :, lanes]))
    for n in range(PARTS):
        part = pl.ds(n * (shard.shape[0] // PARTS), shard.shape[0] // PARTS)
        ends.append((coeff.at[part], shard.at[part]))
    copies = [pltpu.make_async_copy(source, target, sems.at[n]) for n, (source, target) in enumerate(ends)]
    for copy in copies:
        copy.start()
    wide = flat // LANES
    columns = kets // n_pair
    held, orbitals = shard.shape
    for copy in copies[:2]:
        copy.wait()
    count = counts[0]
    lane = lax.broadcasted_iota(jnp.int32, (wide, LANES), 1)
    low, kept = lane < SB, lane < SB * count
    lane = lax.broadcasted_iota(jnp.int32, (TAG, LANES), 1)
    tag = jnp.zeros((TAG, LANES), jnp.int32)
    for t in range(slots):
        tag = jnp.where((lane == 2 * t) & (t < count), mu_in[t], tag)
        tag = jnp.where((lane == 2 * t + 1) & (t < count), nu_in[t], tag)
    tag = tag.astype(jnp.float32).astype(jnp.bfloat16)
    for j in range(wide):
        if j % (wide // PARTS) == 0:
            copies[2 + j // (wide // PARTS)].wait()
        for t in range(slots):
            at = pl.ds((t * wide + j) * kets, kets)
            spread[at, :] = tiles[t, :, j * LANES : (j + 1) * LANES].astype(jnp.float32)
    tile_at, rows = orbitals // LANES * held, columns * SB
    for s in range(n_pair):
        dest = p ^ s
        for k in range(columns):
            column = dest * columns + k
            one = spread[pl.ds(column, wide, stride=kets), :]
            two = spread[pl.ds(wide * kets + column, wide, stride=kets), :]
            even = jnp.where(low, one, pltpu.roll(two, SB, axis=1))
            odd = jnp.where(low, pltpu.roll(one, SB, axis=1), two)
            begin = (s * columns + k) * SB
            woven[pl.ds(begin, wide, stride=2), :] = jnp.where(kept, even, 0.0)
            woven[pl.ds(begin + 1, wide, stride=2), :] = jnp.where(kept, odd, 0.0)
        outs[s][tile_at : tile_at + rows] = woven[pl.ds(s * rows, rows), :].astype(jnp.bfloat16)
        outs[s][tile_at + rows :] = tag
    for copy in copies[2 + PARTS :]:
        copy.wait()
    for j in range(orbitals // LANES):
        lanes = shard[:, j * LANES : (j + 1) * LANES]
        for s in range(n_pair):
            outs[s][j * held : (j + 1) * held] = lanes


def pack(n_pair, integrals, mu, nu, counts, coeff):
    slots, kets, flat = integrals.shape
    rows = coeff.shape[0] * coeff.shape[1] // LANES + kets // n_pair * SB + TAG
    hbm, smem = pl.BlockSpec(memory_space=pltpu.HBM), pl.BlockSpec(memory_space=pltpu.SMEM)
    return pl.pallas_call(
        functools.partial(pack_kernel, n_pair),
        out_shape=[pltpu.VMEM((rows, LANES), jnp.bfloat16)] * n_pair,
        in_specs=[hbm, hbm, hbm, smem, hbm],
        out_specs=[pl.BlockSpec(memory_space=pltpu.VMEM)] * n_pair,
        scratch_shapes=[
            pltpu.VMEM(integrals.shape, jnp.bfloat16),
            pltpu.VMEM(coeff.shape, jnp.bfloat16),
            pltpu.SMEM(mu.shape, jnp.int32),
            pltpu.SMEM(nu.shape, jnp.int32),
            pltpu.VMEM((slots * kets * flat // LANES, LANES), jnp.float32),
            pltpu.VMEM((kets * SB, LANES), jnp.float32),
            pltpu.SemaphoreType.DMA((2 + 2 * PARTS,)),
        ],
        compiler_params=pltpu.CompilerParams(vmem_limit_bytes=56 << 20),
        name="pack",
    )(integrals, mu, nu, counts, coeff)


def transform_kernel(came, n_orb, orbitals, n_in, *refs):
    pieces = refs[:n_in]
    out, c_all, codes, index, half, left, sem = refs[n_in:]
    p, o = lax.axis_index("pair"), lax.axis_index("orb")
    devices = codes.shape[0]
    blocks = orbitals // LANES
    tile_at = pieces[0].shape[-2] - TAG - 2 * SB
    if came:
        for q, piece in enumerate(pieces):
            codes[q : q + 1, :] = piece[tile_at + 2 * SB :][:1].astype(jnp.float32).astype(jnp.int32)
    else:
        codes[...] = pieces[0][:, 2 * SB :, :][:, 0, :].astype(jnp.float32).astype(jnp.int32)
    to_scalars = pltpu.make_async_copy(codes, index, sem)
    to_scalars.start()
    if came:
        rows = c_all.shape[0] // devices
        for q, piece in enumerate(pieces):
            source = (p ^ came[q][0]) * n_orb + (o ^ came[q][1])
            place = pl.ds(pl.multiple_of(source * rows, rows), rows)
            for j in range(blocks):
                c_all[place, j * LANES : (j + 1) * LANES] = piece[j * rows : (j + 1) * rows, :]
    else:
        c_all = pieces[1]
    to_scalars.wait()

    mine = pl.ds(pl.multiple_of(o * LANES, LANES), LANES)
    low = lax.broadcasted_iota(jnp.int32, (SB, LANES), 1) < SB
    chunks = devices // CHUNK

    def rows_of(block):
        return pl.ds(pl.multiple_of(block * SB, SB), SB)

    def chunk_step(chunk, carry):
        for d in range(CHUNK):
            device = chunk * CHUNK + d
            stacked = []
            for k in range(2):
                if came:
                    tile = pieces[d][tile_at + k * SB : tile_at + (k + 1) * SB, :]
                else:
                    tile = pieces[0][device, k * SB : (k + 1) * SB, :]
                stacked += [jnp.where(low, tile, jnp.zeros_like(tile)), jnp.where(low, jnp.zeros_like(tile), tile)]
            mu_one, nu_one, mu_two, nu_two = (index[device, n] for n in range(4))
            rows = jnp.concatenate([c_all[rows_of(nu_one)], c_all[rows_of(nu_two)]], 0)
            moved = jnp.dot(jnp.concatenate(stacked, 0), rows, preferred_element_type=jnp.float32)
            moved = moved.astype(jnp.bfloat16)
            at = pl.ds(d * 2 * SB, 2 * SB)
            half[at, :orbitals] = moved[: 2 * SB]
            half[at, orbitals:] = moved[2 * SB :]
            left[:, at] = jnp.concatenate([c_all[rows_of(mu_one), mine], c_all[rows_of(mu_two), mine]], 0).T
        part = jnp.dot(left[...], half[...], preferred_element_type=jnp.float32)
        for k in range(2):
            for j in range(blocks):
                at = pl.ds(2 * j + k, LANES, stride=2 * blocks)
                begin = k * orbitals + j * LANES
                value = part[:, begin : begin + LANES]
                out[at, :] = value if chunks == 1 else out[at, :] + value
        return carry

    if chunks == 1:
        chunk_step(0, 0)
    else:
        out[...] = jnp.zeros_like(out)
        lax.fori_loop(0, chunks, chunk_step, 0)


def transform(came, n_orb, devices, orbitals, pieces):
    wide = CHUNK * 2 * SB
    held = pieces[0].shape[0] - 2 * SB - TAG if came else TAG
    return pl.pallas_call(
        functools.partial(transform_kernel, came, n_orb, orbitals, len(pieces)),
        out_shape=jax.ShapeDtypeStruct((2 * orbitals // LANES * LANES, LANES), jnp.float32),
        in_specs=[pl.BlockSpec(memory_space=pltpu.VMEM)] * len(pieces),
        out_specs=pl.BlockSpec(memory_space=pltpu.VMEM),
        scratch_shapes=[
            pltpu.VMEM((held * LANES // orbitals * devices if came else TAG, orbitals), jnp.bfloat16),
            pltpu.VMEM((devices, LANES), jnp.int32),
            pltpu.SMEM((devices, LANES), jnp.int32),
            pltpu.VMEM((wide, 2 * orbitals), jnp.bfloat16),
            pltpu.VMEM((LANES, wide), jnp.bfloat16),
            pltpu.SemaphoreType.DMA,
        ],
        compiler_params=pltpu.CompilerParams(vmem_limit_bytes=40 << 20),
        name="transform",
    )(*pieces)


def flip(array, axis, size, bit):
    return lax.ppermute(array, axis, [(i, i ^ bit) for i in range(size)])


def body(n_pair, n_orb, integrals, mu_block, nu_block, counts, coeff):
    slots, kets, flat = integrals.shape
    columns = kets // n_pair
    orbitals = coeff.shape[1]
    if n_orb == 4 and n_pair == 4:
        packed = list(pack(n_pair, integrals, mu_block, nu_block, counts, coeff))
        lines = packed[:1] + [flip(packed[s], "pair", n_pair, s) for s in range(1, n_pair)]
        across = [flip(line, "orb", n_orb, 2) for line in lines[:3]]
        last, across[1] = lax.optimization_barrier((lines[3], across[1]))
        across.append(flip(last, "orb", n_orb, 2))
        first = list(lax.optimization_barrier((lines[0], lines[1], last)))[:2]
        swapped = [flip(piece, "orb", n_orb, 1) for piece in first]
        later = list(lax.optimization_barrier((lines[2], last, *across[:3]))) + across[3:]
        swapped += [flip(piece, "orb", n_orb, 1) for piece in later]
        pieces = first + later + swapped
        came = [(0, 0), (1, 0), (2, 0), (3, 0), (0, 2), (1, 2), (2, 2), (3, 2)]
        came += [(s, side ^ 1) for s, side in came]
    else:
        kept = jnp.arange(slots, dtype=jnp.int32) < counts[0]
        tiles = jnp.where(kept[:, None, None], integrals, jnp.zeros_like(integrals))
        tiles = tiles.reshape(slots, n_pair, columns, SB, SB).transpose(1, 2, 3, 0, 4)
        tiles = tiles.reshape(n_pair, columns * SB, slots * SB)
        tag = jnp.where(kept[:, None], jnp.stack([mu_block, nu_block], 1), 0).reshape(-1)
        tag = jnp.zeros((n_pair, TAG, LANES), jnp.bfloat16).at[:, :, : 2 * slots].set(tag.astype(jnp.bfloat16))
        packed = jnp.concatenate([tiles, tag], 1)
        line = lax.all_to_all(packed, "pair", split_axis=0, concat_axis=0, tiled=True)
        gathered = lax.all_gather(coeff, ("pair", "orb"), axis=0, tiled=True)
        pieces, came = [lax.all_gather(line, "orb", axis=0, tiled=True), gathered], None
    out = transform(came, n_orb, n_pair * n_orb, orbitals, pieces)
    out = out.reshape(orbitals // n_orb, orbitals // LANES, columns, LANES)
    return out.transpose(0, 2, 1, 3).reshape(orbitals // n_orb, columns, orbitals)


def solution(mesh):
    placed = (
        P(("grp", "pair", "orb"), None, None),
        P(("grp", "pair", "orb")),
        P(("grp", "pair", "orb")),
        P(("grp", "pair", "orb")),
        P(("grp", "pair", "orb"), None),
    )
    return jax.shard_map(
        functools.partial(body, mesh.shape["pair"], mesh.shape["orb"]),
        mesh=mesh,
        in_specs=placed,
        out_specs=P(("grp", "orb"), "pair", None),
        check_vma=False,
    )
```

```python
import functools

import jax
import jax.numpy as jnp
from jax import lax
from jax.experimental import pallas as pl
from jax.experimental.pallas import tpu as pltpu
from jax.sharding import PartitionSpec as P

SB = 64
LANES = 128
TAG = 16
CHUNK = 16


def pack_kernel(n_pair, integrals, mu, nu, counts, coeff, *refs):
    outs = refs[:n_pair]
    tiles, shard, mu_in, nu_in, spread, woven, sems = refs[n_pair:]
    p = lax.axis_index("pair")
    copies = [
        pltpu.make_async_copy(source, target, sems.at[n])
        for n, (source, target) in enumerate(((integrals, tiles), (mu, mu_in), (nu, nu_in), (coeff, shard)))
    ]
    for copy in copies:
        copy.start()
    slots, kets, flat = tiles.shape
    wide = flat // LANES
    columns = kets // n_pair
    held, orbitals = shard.shape
    for copy in copies[1:3]:
        copy.wait()
    count = counts[0]
    lane = lax.broadcasted_iota(jnp.int32, (wide, LANES), 1)
    low, kept = lane < SB, lane < SB * count
    lane = lax.broadcasted_iota(jnp.int32, (TAG, LANES), 1)
    tag = jnp.zeros((TAG, LANES), jnp.int32)
    for t in range(slots):
        tag = jnp.where((lane == 2 * t) & (t < count), mu_in[t], tag)
        tag = jnp.where((lane == 2 * t + 1) & (t < count), nu_in[t], tag)
    tag = tag.astype(jnp.float32).astype(jnp.bfloat16)
    copies[0].wait()
    for t in range(slots):
        for j in range(wide):
            at = pl.ds((t * wide + j) * kets, kets)
            spread[at, :] = tiles[t, :, j * LANES : (j + 1) * LANES].astype(jnp.float32)
    tile_at, rows = orbitals // LANES * held, columns * SB
    for s in range(n_pair):
        dest = p ^ s
        for k in range(columns):
            column = dest * columns + k
            one = spread[pl.ds(column, wide, stride=kets), :]
            two = spread[pl.ds(wide * kets + column, wide, stride=kets), :]
            even = jnp.where(low, one, pltpu.roll(two, SB, axis=1))
            odd = jnp.where(low, pltpu.roll(one, SB, axis=1), two)
            begin = (s * columns + k) * SB
            woven[pl.ds(begin, wide, stride=2), :] = jnp.where(kept, even, 0.0)
            woven[pl.ds(begin + 1, wide, stride=2), :] = jnp.where(kept, odd, 0.0)
        outs[s][tile_at : tile_at + rows] = woven[pl.ds(s * rows, rows), :].astype(jnp.bfloat16)
        outs[s][tile_at + rows :] = tag
    copies[3].wait()
    for j in range(orbitals // LANES):
        lanes = shard[:, j * LANES : (j + 1) * LANES]
        for s in range(n_pair):
            outs[s][j * held : (j + 1) * held] = lanes


def pack(n_pair, integrals, mu, nu, counts, coeff):
    slots, kets, flat = integrals.shape
    rows = coeff.shape[0] * coeff.shape[1] // LANES + kets // n_pair * SB + TAG
    hbm, smem = pl.BlockSpec(memory_space=pltpu.HBM), pl.BlockSpec(memory_space=pltpu.SMEM)
    return pl.pallas_call(
        functools.partial(pack_kernel, n_pair),
        out_shape=[pltpu.VMEM((rows, LANES), jnp.bfloat16)] * n_pair,
        in_specs=[hbm, hbm, hbm, smem, hbm],
        out_specs=[pl.BlockSpec(memory_space=pltpu.VMEM)] * n_pair,
        scratch_shapes=[
            pltpu.VMEM(integrals.shape, jnp.bfloat16),
            pltpu.VMEM(coeff.shape, jnp.bfloat16),
            pltpu.SMEM(mu.shape, jnp.int32),
            pltpu.SMEM(nu.shape, jnp.int32),
            pltpu.VMEM((slots * kets * flat // LANES, LANES), jnp.float32),
            pltpu.VMEM((kets * SB, LANES), jnp.float32),
            pltpu.SemaphoreType.DMA((4,)),
        ],
        compiler_params=pltpu.CompilerParams(vmem_limit_bytes=56 << 20),
        name="pack",
    )(integrals, mu, nu, counts, coeff)


def transform_kernel(came, n_orb, orbitals, n_in, *refs):
    pieces = refs[:n_in]
    out, c_all, codes, index, half, left, sem = refs[n_in:]
    p, o = lax.axis_index("pair"), lax.axis_index("orb")
    devices = codes.shape[0]
    blocks = orbitals // LANES
    tile_at = pieces[0].shape[-2] - TAG - 2 * SB
    if came:
        for q, piece in enumerate(pieces):
            codes[q : q + 1, :] = piece[tile_at + 2 * SB :][:1].astype(jnp.float32).astype(jnp.int32)
    else:
        codes[...] = pieces[0][:, 2 * SB :, :][:, 0, :].astype(jnp.float32).astype(jnp.int32)
    to_scalars = pltpu.make_async_copy(codes, index, sem)
    to_scalars.start()
    if came:
        rows = c_all.shape[0] // devices
        for q, piece in enumerate(pieces):
            source = (p ^ came[q][0]) * n_orb + (o ^ came[q][1])
            place = pl.ds(pl.multiple_of(source * rows, rows), rows)
            for j in range(blocks):
                c_all[place, j * LANES : (j + 1) * LANES] = piece[j * rows : (j + 1) * rows, :]
    else:
        c_all = pieces[1]
    to_scalars.wait()

    mine = pl.ds(pl.multiple_of(o * LANES, LANES), LANES)
    low = lax.broadcasted_iota(jnp.int32, (SB, LANES), 1) < SB
    chunks = devices // CHUNK

    def rows_of(block):
        return pl.ds(pl.multiple_of(block * SB, SB), SB)

    def chunk_step(chunk, carry):
        part = None
        for d in range(CHUNK):
            device = chunk * CHUNK + d
            stacked = []
            for k in range(2):
                if came:
                    tile = pieces[d][tile_at + k * SB : tile_at + (k + 1) * SB, :]
                else:
                    tile = pieces[0][device, k * SB : (k + 1) * SB, :]
                stacked += [jnp.where(low, tile, jnp.zeros_like(tile)), jnp.where(low, jnp.zeros_like(tile), tile)]
            mu_one, nu_one, mu_two, nu_two = (index[device, n] for n in range(4))
            rows = jnp.concatenate([c_all[rows_of(nu_one)], c_all[rows_of(nu_two)]], 0)
            moved = jnp.dot(jnp.concatenate(stacked, 0), rows, preferred_element_type=jnp.float32)
            moved = moved.astype(jnp.bfloat16)
            at = pl.ds(d * 2 * SB, 2 * SB)
            half[at, :orbitals] = moved[: 2 * SB]
            half[at, orbitals:] = moved[2 * SB :]
            left[:, at] = jnp.concatenate([c_all[rows_of(mu_one), mine], c_all[rows_of(mu_two), mine]], 0).T
            if d % (CHUNK // 2) == CHUNK // 2 - 1:
                done = slice((d + 1 - CHUNK // 2) * 2 * SB, (d + 1) * 2 * SB)
                term = jnp.dot(left[:, done], half[done, :], preferred_element_type=jnp.float32)
                part = term if part is None else part + term
        for k in range(2):
            for j in range(blocks):
                at = pl.ds(2 * j + k, LANES, stride=2 * blocks)
                begin = k * orbitals + j * LANES
                value = part[:, begin : begin + LANES]
                out[at, :] = value if chunks == 1 else out[at, :] + value
        return carry

    if chunks == 1:
        chunk_step(0, 0)
    else:
        out[...] = jnp.zeros_like(out)
        lax.fori_loop(0, chunks, chunk_step, 0)


def transform(came, n_orb, devices, orbitals, pieces):
    wide = CHUNK * 2 * SB
    held = pieces[0].shape[0] - 2 * SB - TAG if came else TAG
    return pl.pallas_call(
        functools.partial(transform_kernel, came, n_orb, orbitals, len(pieces)),
        out_shape=jax.ShapeDtypeStruct((2 * orbitals // LANES * LANES, LANES), jnp.float32),
        in_specs=[pl.BlockSpec(memory_space=pltpu.VMEM)] * len(pieces),
        out_specs=pl.BlockSpec(memory_space=pltpu.VMEM),
        scratch_shapes=[
            pltpu.VMEM((held * LANES // orbitals * devices if came else TAG, orbitals), jnp.bfloat16),
            pltpu.VMEM((devices, LANES), jnp.int32),
            pltpu.SMEM((devices, LANES), jnp.int32),
            pltpu.VMEM((wide, 2 * orbitals), jnp.bfloat16),
            pltpu.VMEM((LANES, wide), jnp.bfloat16),
            pltpu.SemaphoreType.DMA,
        ],
        compiler_params=pltpu.CompilerParams(vmem_limit_bytes=40 << 20),
        name="transform",
    )(*pieces)


def flip(array, axis, size, bit):
    return lax.ppermute(array, axis, [(i, i ^ bit) for i in range(size)])


def body(n_pair, n_orb, integrals, mu_block, nu_block, counts, coeff):
    slots, kets, flat = integrals.shape
    columns = kets // n_pair
    orbitals = coeff.shape[1]
    if n_orb == 4 and n_pair == 4:
        packed = list(pack(n_pair, integrals, mu_block, nu_block, counts, coeff))
        lines = packed[:1] + [flip(packed[s], "pair", n_pair, s) for s in range(1, n_pair)]
        across = [flip(line, "orb", n_orb, 2) for line in lines[:3]]
        last, across[1] = lax.optimization_barrier((lines[3], across[1]))
        across.append(flip(last, "orb", n_orb, 2))
        first = list(lax.optimization_barrier((lines[0], lines[1], last)))[:2]
        swapped = [flip(piece, "orb", n_orb, 1) for piece in first]
        later = list(lax.optimization_barrier((lines[2], last, *across[:3]))) + across[3:]
        swapped += [flip(piece, "orb", n_orb, 1) for piece in later]
        pieces = first + later + swapped
        came = [(0, 0), (1, 0), (2, 0), (3, 0), (0, 2), (1, 2), (2, 2), (3, 2)]
        came += [(s, side ^ 1) for s, side in came]
    else:
        kept = jnp.arange(slots, dtype=jnp.int32) < counts[0]
        tiles = jnp.where(kept[:, None, None], integrals, jnp.zeros_like(integrals))
        tiles = tiles.reshape(slots, n_pair, columns, SB, SB).transpose(1, 2, 3, 0, 4)
        tiles = tiles.reshape(n_pair, columns * SB, slots * SB)
        tag = jnp.where(kept[:, None], jnp.stack([mu_block, nu_block], 1), 0).reshape(-1)
        tag = jnp.zeros((n_pair, TAG, LANES), jnp.bfloat16).at[:, :, : 2 * slots].set(tag.astype(jnp.bfloat16))
        packed = jnp.concatenate([tiles, tag], 1)
        line = lax.all_to_all(packed, "pair", split_axis=0, concat_axis=0, tiled=True)
        gathered = lax.all_gather(coeff, ("pair", "orb"), axis=0, tiled=True)
        pieces, came = [lax.all_gather(line, "orb", axis=0, tiled=True), gathered], None
    out = transform(came, n_orb, n_pair * n_orb, orbitals, pieces)
    out = out.reshape(orbitals // n_orb, orbitals // LANES, columns, LANES)
    return out.transpose(0, 2, 1, 3).reshape(orbitals // n_orb, columns, orbitals)


def solution(mesh):
    placed = (
        P(("grp", "pair", "orb"), None, None),
        P(("grp", "pair", "orb")),
        P(("grp", "pair", "orb")),
        P(("grp", "pair", "orb")),
        P(("grp", "pair", "orb"), None),
    )
    return jax.shard_map(
        functools.partial(body, mesh.shape["pair"], mesh.shape["orb"]),
        mesh=mesh,
        in_specs=placed,
        out_specs=P(("grp", "orb"), "pair", None),
        check_vma=False,
    )
```

```python
import functools

import jax
import jax.numpy as jnp
from jax import lax
from jax.experimental import pallas as pl
from jax.experimental.pallas import tpu as pltpu
from jax.sharding import PartitionSpec as P

SB = 64
LANES = 128
TAG = 16
CHUNK = 16


def pack_kernel(n_pair, integrals, mu, nu, counts, coeff, *refs):
    outs = refs[:n_pair]
    tiles, shard, mu_in, nu_in, spread, woven, sems = refs[n_pair:]
    p = lax.axis_index("pair")
    copies = [
        pltpu.make_async_copy(source, target, sems.at[n])
        for n, (source, target) in enumerate(((integrals, tiles), (mu, mu_in), (nu, nu_in), (coeff, shard)))
    ]
    for copy in copies:
        copy.start()
    slots, kets, flat = tiles.shape
    wide = flat // LANES
    columns = kets // n_pair
    held, orbitals = shard.shape
    for copy in copies[1:3]:
        copy.wait()
    count = counts[0]
    lane = lax.broadcasted_iota(jnp.int32, (wide, LANES), 1)
    low, kept = lane < SB, lane < SB * count
    lane = lax.broadcasted_iota(jnp.int32, (TAG, LANES), 1)
    tag = jnp.zeros((TAG, LANES), jnp.int32)
    for t in range(slots):
        tag = jnp.where((lane == 2 * t) & (t < count), mu_in[t], tag)
        tag = jnp.where((lane == 2 * t + 1) & (t < count), nu_in[t], tag)
    tag = tag.astype(jnp.float32).astype(jnp.bfloat16)
    copies[0].wait()
    for t in range(slots):
        for j in range(wide):
            at = pl.ds((t * wide + j) * kets, kets)
            spread[at, :] = tiles[t, :, j * LANES : (j + 1) * LANES].astype(jnp.float32)
    tile_at, rows = orbitals // LANES * held, columns * SB
    for s in range(n_pair):
        dest = p ^ s
        for k in range(columns):
            column = dest * columns + k
            one = spread[pl.ds(column, wide, stride=kets), :]
            two = spread[pl.ds(wide * kets + column, wide, stride=kets), :]
            even = jnp.where(low, one, pltpu.roll(two, SB, axis=1))
            odd = jnp.where(low, pltpu.roll(one, SB, axis=1), two)
            begin = (s * columns + k) * SB
            woven[pl.ds(begin, wide, stride=2), :] = jnp.where(kept, even, 0.0)
            woven[pl.ds(begin + 1, wide, stride=2), :] = jnp.where(kept, odd, 0.0)
        outs[s][tile_at : tile_at + rows] = woven[pl.ds(s * rows, rows), :].astype(jnp.bfloat16)
        outs[s][tile_at + rows :] = tag
    copies[3].wait()
    for j in range(orbitals // LANES):
        lanes = shard[:, j * LANES : (j + 1) * LANES]
        for s in range(n_pair):
            outs[s][j * held : (j + 1) * held] = lanes


def pack(n_pair, integrals, mu, nu, counts, coeff):
    slots, kets, flat = integrals.shape
    rows = coeff.shape[0] * coeff.shape[1] // LANES + kets // n_pair * SB + TAG
    hbm, smem = pl.BlockSpec(memory_space=pltpu.HBM), pl.BlockSpec(memory_space=pltpu.SMEM)
    return pl.pallas_call(
        functools.partial(pack_kernel, n_pair),
        out_shape=[pltpu.VMEM((rows, LANES), jnp.bfloat16)] * n_pair,
        in_specs=[hbm, hbm, hbm, smem, hbm],
        out_specs=[pl.BlockSpec(memory_space=pltpu.VMEM)] * n_pair,
        scratch_shapes=[
            pltpu.VMEM(integrals.shape, jnp.bfloat16),
            pltpu.VMEM(coeff.shape, jnp.bfloat16),
            pltpu.SMEM(mu.shape, jnp.int32),
            pltpu.SMEM(nu.shape, jnp.int32),
            pltpu.VMEM((slots * kets * flat // LANES, LANES), jnp.float32),
            pltpu.VMEM((kets * SB, LANES), jnp.float32),
            pltpu.SemaphoreType.DMA((4,)),
        ],
        compiler_params=pltpu.CompilerParams(vmem_limit_bytes=56 << 20),
        name="pack",
    )(integrals, mu, nu, counts, coeff)


def transform_kernel(came, n_orb, orbitals, n_in, *refs):
    pieces = refs[:n_in]
    out, c_all, codes, index, half, left, sem = refs[n_in:]
    p, o = lax.axis_index("pair"), lax.axis_index("orb")
    devices = codes.shape[0]
    blocks = orbitals // LANES
    tile_at = pieces[0].shape[-2] - TAG - 2 * SB
    if came:
        for q, piece in enumerate(pieces):
            codes[q : q + 1, :] = piece[tile_at + 2 * SB :][:1].astype(jnp.float32).astype(jnp.int32)
    else:
        codes[...] = pieces[0][:, 2 * SB :, :][:, 0, :].astype(jnp.float32).astype(jnp.int32)
    to_scalars = pltpu.make_async_copy(codes, index, sem)
    to_scalars.start()
    if came:
        rows = c_all.shape[0] // devices
        for q, piece in enumerate(pieces):
            source = (p ^ came[q][0]) * n_orb + (o ^ came[q][1])
            place = pl.ds(pl.multiple_of(source * rows, rows), rows)
            for j in range(blocks):
                c_all[place, j * LANES : (j + 1) * LANES] = piece[j * rows : (j + 1) * rows, :]
    else:
        c_all = pieces[1]
    to_scalars.wait()

    mine = pl.ds(pl.multiple_of(o * LANES, LANES), LANES)
    low = lax.broadcasted_iota(jnp.int32, (SB, LANES), 1) < SB
    chunks = devices // CHUNK

    def rows_of(block):
        return pl.ds(pl.multiple_of(block * SB, SB), SB)

    def chunk_step(chunk, carry):
        part = None
        for d in range(CHUNK):
            device = chunk * CHUNK + d
            stacked = []
            for k in range(2):
                if came:
                    tile = pieces[d][tile_at + k * SB : tile_at + (k + 1) * SB, :]
                else:
                    tile = pieces[0][device, k * SB : (k + 1) * SB, :]
                stacked += [jnp.where(low, tile, jnp.zeros_like(tile)), jnp.where(low, jnp.zeros_like(tile), tile)]
            mu_one, nu_one, mu_two, nu_two = (index[device, n] for n in range(4))
            rows = jnp.concatenate([c_all[rows_of(nu_one)], c_all[rows_of(nu_two)]], 0)
            moved = jnp.dot(jnp.concatenate(stacked, 0), rows, preferred_element_type=jnp.float32)
            moved = moved.astype(jnp.bfloat16)
            at = pl.ds(d * 2 * SB, 2 * SB)
            half[at, :orbitals] = moved[: 2 * SB]
            half[at, orbitals:] = moved[2 * SB :]
            left[:, at] = jnp.concatenate([c_all[rows_of(mu_one), mine], c_all[rows_of(mu_two), mine]], 0).T
            if d % (CHUNK // 4) == CHUNK // 4 - 1:
                done = slice((d + 1 - CHUNK // 4) * 2 * SB, (d + 1) * 2 * SB)
                term = jnp.dot(left[:, done], half[done, :], preferred_element_type=jnp.float32)
                part = term if part is None else part + term
        for k in range(2):
            for j in range(blocks):
                at = pl.ds(2 * j + k, LANES, stride=2 * blocks)
                begin = k * orbitals + j * LANES
                value = part[:, begin : begin + LANES]
                out[at, :] = value if chunks == 1 else out[at, :] + value
        return carry

    if chunks == 1:
        chunk_step(0, 0)
    else:
        out[...] = jnp.zeros_like(out)
        lax.fori_loop(0, chunks, chunk_step, 0)


def transform(came, n_orb, devices, orbitals, pieces):
    wide = CHUNK * 2 * SB
    held = pieces[0].shape[0] - 2 * SB - TAG if came else TAG
    return pl.pallas_call(
        functools.partial(transform_kernel, came, n_orb, orbitals, len(pieces)),
        out_shape=jax.ShapeDtypeStruct((2 * orbitals // LANES * LANES, LANES), jnp.float32),
        in_specs=[pl.BlockSpec(memory_space=pltpu.VMEM)] * len(pieces),
        out_specs=pl.BlockSpec(memory_space=pltpu.VMEM),
        scratch_shapes=[
            pltpu.VMEM((held * LANES // orbitals * devices if came else TAG, orbitals), jnp.bfloat16),
            pltpu.VMEM((devices, LANES), jnp.int32),
            pltpu.SMEM((devices, LANES), jnp.int32),
            pltpu.VMEM((wide, 2 * orbitals), jnp.bfloat16),
            pltpu.VMEM((LANES, wide), jnp.bfloat16),
            pltpu.SemaphoreType.DMA,
        ],
        compiler_params=pltpu.CompilerParams(vmem_limit_bytes=40 << 20),
        name="transform",
    )(*pieces)


def flip(array, axis, size, bit):
    return lax.ppermute(array, axis, [(i, i ^ bit) for i in range(size)])


def body(n_pair, n_orb, integrals, mu_block, nu_block, counts, coeff):
    slots, kets, flat = integrals.shape
    columns = kets // n_pair
    orbitals = coeff.shape[1]
    if n_orb == 4 and n_pair == 4:
        packed = list(pack(n_pair, integrals, mu_block, nu_block, counts, coeff))
        lines = packed[:1] + [flip(packed[s], "pair", n_pair, s) for s in range(1, n_pair)]
        across = [flip(line, "orb", n_orb, 2) for line in lines[:3]]
        last, across[1] = lax.optimization_barrier((lines[3], across[1]))
        across.append(flip(last, "orb", n_orb, 2))
        first = list(lax.optimization_barrier((lines[0], lines[1], last)))[:2]
        swapped = [flip(piece, "orb", n_orb, 1) for piece in first]
        later = list(lax.optimization_barrier((lines[2], last, *across[:3]))) + across[3:]
        swapped += [flip(piece, "orb", n_orb, 1) for piece in later]
        pieces = first + later + swapped
        came = [(0, 0), (1, 0), (2, 0), (3, 0), (0, 2), (1, 2), (2, 2), (3, 2)]
        came += [(s, side ^ 1) for s, side in came]
    else:
        kept = jnp.arange(slots, dtype=jnp.int32) < counts[0]
        tiles = jnp.where(kept[:, None, None], integrals, jnp.zeros_like(integrals))
        tiles = tiles.reshape(slots, n_pair, columns, SB, SB).transpose(1, 2, 3, 0, 4)
        tiles = tiles.reshape(n_pair, columns * SB, slots * SB)
        tag = jnp.where(kept[:, None], jnp.stack([mu_block, nu_block], 1), 0).reshape(-1)
        tag = jnp.zeros((n_pair, TAG, LANES), jnp.bfloat16).at[:, :, : 2 * slots].set(tag.astype(jnp.bfloat16))
        packed = jnp.concatenate([tiles, tag], 1)
        line = lax.all_to_all(packed, "pair", split_axis=0, concat_axis=0, tiled=True)
        gathered = lax.all_gather(coeff, ("pair", "orb"), axis=0, tiled=True)
        pieces, came = [lax.all_gather(line, "orb", axis=0, tiled=True), gathered], None
    out = transform(came, n_orb, n_pair * n_orb, orbitals, pieces)
    out = out.reshape(orbitals // n_orb, orbitals // LANES, columns, LANES)
    return out.transpose(0, 2, 1, 3).reshape(orbitals // n_orb, columns, orbitals)


def solution(mesh):
    placed = (
        P(("grp", "pair", "orb"), None, None),
        P(("grp", "pair", "orb")),
        P(("grp", "pair", "orb")),
        P(("grp", "pair", "orb")),
        P(("grp", "pair", "orb"), None),
    )
    return jax.shard_map(
        functools.partial(body, mesh.shape["pair"], mesh.shape["orb"]),
        mesh=mesh,
        in_specs=placed,
        out_specs=P(("grp", "orb"), "pair", None),
        check_vma=False,
    )
```

```python
import functools

import jax
import jax.numpy as jnp
from jax import lax
from jax.experimental import pallas as pl
from jax.experimental.pallas import tpu as pltpu
from jax.sharding import PartitionSpec as P

SB = 64
LANES = 128
TAG = 16
CHUNK = 16


def pack_kernel(n_pair, integrals, mu, nu, counts, coeff, *refs):
    outs = refs[:n_pair]
    tiles, shard, mu_in, nu_in, spread, woven, sems = refs[n_pair:]
    p = lax.axis_index("pair")
    copies = [
        pltpu.make_async_copy(source, target, sems.at[n])
        for n, (source, target) in enumerate(((integrals, tiles), (mu, mu_in), (nu, nu_in), (coeff, shard)))
    ]
    for copy in copies:
        copy.start()
    slots, kets, flat = tiles.shape
    wide = flat // LANES
    columns = kets // n_pair
    held, orbitals = shard.shape
    for copy in copies[1:3]:
        copy.wait()
    count = counts[0]
    lane = lax.broadcasted_iota(jnp.int32, (wide, LANES), 1)
    low, kept = lane < SB, lane < SB * count
    lane = lax.broadcasted_iota(jnp.int32, (TAG, LANES), 1)
    tag = jnp.zeros((TAG, LANES), jnp.int32)
    for t in range(slots):
        tag = jnp.where((lane == 2 * t) & (t < count), mu_in[t], tag)
        tag = jnp.where((lane == 2 * t + 1) & (t < count), nu_in[t], tag)
    tag = tag.astype(jnp.float32).astype(jnp.bfloat16)
    copies[3].wait()
    for j in range(orbitals // LANES):
        lanes = shard[:, j * LANES : (j + 1) * LANES]
        for s in range(n_pair):
            outs[s][j * held : (j + 1) * held] = lanes
    copies[0].wait()
    for t in range(slots):
        for j in range(wide):
            at = pl.ds((t * wide + j) * kets, kets)
            spread[at, :] = tiles[t, :, j * LANES : (j + 1) * LANES].astype(jnp.float32)
    tile_at, rows = orbitals // LANES * held, columns * SB
    for s in range(n_pair):
        dest = p ^ s
        for k in range(columns):
            column = dest * columns + k
            one = spread[pl.ds(column, wide, stride=kets), :]
            two = spread[pl.ds(wide * kets + column, wide, stride=kets), :]
            even = jnp.where(low, one, pltpu.roll(two, SB, axis=1))
            odd = jnp.where(low, pltpu.roll(one, SB, axis=1), two)
            begin = (s * columns + k) * SB
            woven[pl.ds(begin, wide, stride=2), :] = jnp.where(kept, even, 0.0)
            woven[pl.ds(begin + 1, wide, stride=2), :] = jnp.where(kept, odd, 0.0)
        outs[s][tile_at : tile_at + rows] = woven[pl.ds(s * rows, rows), :].astype(jnp.bfloat16)
        outs[s][tile_at + rows :] = tag


def pack(n_pair, integrals, mu, nu, counts, coeff):
    slots, kets, flat = integrals.shape
    rows = coeff.shape[0] * coeff.shape[1] // LANES + kets // n_pair * SB + TAG
    hbm, smem = pl.BlockSpec(memory_space=pltpu.HBM), pl.BlockSpec(memory_space=pltpu.SMEM)
    return pl.pallas_call(
        functools.partial(pack_kernel, n_pair),
        out_shape=[pltpu.VMEM((rows, LANES), jnp.bfloat16)] * n_pair,
        in_specs=[hbm, hbm, hbm, smem, hbm],
        out_specs=[pl.BlockSpec(memory_space=pltpu.VMEM)] * n_pair,
        scratch_shapes=[
            pltpu.VMEM(integrals.shape, jnp.bfloat16),
            pltpu.VMEM(coeff.shape, jnp.bfloat16),
            pltpu.SMEM(mu.shape, jnp.int32),
            pltpu.SMEM(nu.shape, jnp.int32),
            pltpu.VMEM((slots * kets * flat // LANES, LANES), jnp.float32),
            pltpu.VMEM((kets * SB, LANES), jnp.float32),
            pltpu.SemaphoreType.DMA((4,)),
        ],
        compiler_params=pltpu.CompilerParams(vmem_limit_bytes=56 << 20),
        name="pack",
    )(integrals, mu, nu, counts, coeff)


def transform_kernel(came, n_orb, orbitals, n_in, *refs):
    pieces = refs[:n_in]
    out, c_all, codes, index, half, left, sem = refs[n_in:]
    p, o = lax.axis_index("pair"), lax.axis_index("orb")
    devices = codes.shape[0]
    blocks = orbitals // LANES
    tile_at = pieces[0].shape[-2] - TAG - 2 * SB
    if came:
        for q, piece in enumerate(pieces):
            codes[q : q + 1, :] = piece[tile_at + 2 * SB :][:1].astype(jnp.float32).astype(jnp.int32)
    else:
        codes[...] = pieces[0][:, 2 * SB :, :][:, 0, :].astype(jnp.float32).astype(jnp.int32)
    to_scalars = pltpu.make_async_copy(codes, index, sem)
    to_scalars.start()
    if came:
        rows = c_all.shape[0] // devices
        for q, piece in enumerate(pieces):
            source = (p ^ came[q][0]) * n_orb + (o ^ came[q][1])
            place = pl.ds(pl.multiple_of(source * rows, rows), rows)
            for j in range(blocks):
                c_all[place, j * LANES : (j + 1) * LANES] = piece[j * rows : (j + 1) * rows, :]
    else:
        c_all = pieces[1]
    to_scalars.wait()

    mine = pl.ds(pl.multiple_of(o * LANES, LANES), LANES)
    low = lax.broadcasted_iota(jnp.int32, (SB, LANES), 1) < SB
    chunks = devices // CHUNK

    def rows_of(block):
        return pl.ds(pl.multiple_of(block * SB, SB), SB)

    def chunk_step(chunk, carry):
        part = None
        for d in range(CHUNK):
            device = chunk * CHUNK + d
            stacked = []
            for k in range(2):
                if came:
                    tile = pieces[d][tile_at + k * SB : tile_at + (k + 1) * SB, :]
                else:
                    tile = pieces[0][device, k * SB : (k + 1) * SB, :]
                stacked += [jnp.where(low, tile, jnp.zeros_like(tile)), jnp.where(low, jnp.zeros_like(tile), tile)]
            mu_one, nu_one, mu_two, nu_two = (index[device, n] for n in range(4))
            rows = jnp.concatenate([c_all[rows_of(nu_one)], c_all[rows_of(nu_two)]], 0)
            moved = jnp.dot(jnp.concatenate(stacked, 0), rows, preferred_element_type=jnp.float32)
            moved = moved.astype(jnp.bfloat16)
            at = pl.ds(d * 2 * SB, 2 * SB)
            half[at, :orbitals] = moved[: 2 * SB]
            half[at, orbitals:] = moved[2 * SB :]
            left[:, at] = jnp.concatenate([c_all[rows_of(mu_one), mine], c_all[rows_of(mu_two), mine]], 0).T
            if d % (CHUNK // 2) == CHUNK // 2 - 1:
                done = slice((d + 1 - CHUNK // 2) * 2 * SB, (d + 1) * 2 * SB)
                term = jnp.dot(left[:, done], half[done, :], preferred_element_type=jnp.float32)
                part = term if part is None else part + term
        for k in range(2):
            for j in range(blocks):
                at = pl.ds(2 * j + k, LANES, stride=2 * blocks)
                begin = k * orbitals + j * LANES
                value = part[:, begin : begin + LANES]
                out[at, :] = value if chunks == 1 else out[at, :] + value
        return carry

    if chunks == 1:
        chunk_step(0, 0)
    else:
        out[...] = jnp.zeros_like(out)
        lax.fori_loop(0, chunks, chunk_step, 0)


def transform(came, n_orb, devices, orbitals, pieces):
    wide = CHUNK * 2 * SB
    held = pieces[0].shape[0] - 2 * SB - TAG if came else TAG
    return pl.pallas_call(
        functools.partial(transform_kernel, came, n_orb, orbitals, len(pieces)),
        out_shape=jax.ShapeDtypeStruct((2 * orbitals // LANES * LANES, LANES), jnp.float32),
        in_specs=[pl.BlockSpec(memory_space=pltpu.VMEM)] * len(pieces),
        out_specs=pl.BlockSpec(memory_space=pltpu.VMEM),
        scratch_shapes=[
            pltpu.VMEM((held * LANES // orbitals * devices if came else TAG, orbitals), jnp.bfloat16),
            pltpu.VMEM((devices, LANES), jnp.int32),
            pltpu.SMEM((devices, LANES), jnp.int32),
            pltpu.VMEM((wide, 2 * orbitals), jnp.bfloat16),
            pltpu.VMEM((LANES, wide), jnp.bfloat16),
            pltpu.SemaphoreType.DMA,
        ],
        compiler_params=pltpu.CompilerParams(vmem_limit_bytes=40 << 20),
        name="transform",
    )(*pieces)


def flip(array, axis, size, bit):
    return lax.ppermute(array, axis, [(i, i ^ bit) for i in range(size)])


def body(n_pair, n_orb, integrals, mu_block, nu_block, counts, coeff):
    slots, kets, flat = integrals.shape
    columns = kets // n_pair
    orbitals = coeff.shape[1]
    if n_orb == 4 and n_pair == 4:
        packed = list(pack(n_pair, integrals, mu_block, nu_block, counts, coeff))
        lines = packed[:1] + [flip(packed[s], "pair", n_pair, s) for s in range(1, n_pair)]
        across = [flip(line, "orb", n_orb, 2) for line in lines[:3]]
        last, across[1] = lax.optimization_barrier((lines[3], across[1]))
        across.append(flip(last, "orb", n_orb, 2))
        first = list(lax.optimization_barrier((lines[0], lines[1], last)))[:2]
        swapped = [flip(piece, "orb", n_orb, 1) for piece in first]
        later = list(lax.optimization_barrier((lines[2], last, *across[:3]))) + across[3:]
        swapped += [flip(piece, "orb", n_orb, 1) for piece in later]
        pieces = first + later + swapped
        came = [(0, 0), (1, 0), (2, 0), (3, 0), (0, 2), (1, 2), (2, 2), (3, 2)]
        came += [(s, side ^ 1) for s, side in came]
    else:
        kept = jnp.arange(slots, dtype=jnp.int32) < counts[0]
        tiles = jnp.where(kept[:, None, None], integrals, jnp.zeros_like(integrals))
        tiles = tiles.reshape(slots, n_pair, columns, SB, SB).transpose(1, 2, 3, 0, 4)
        tiles = tiles.reshape(n_pair, columns * SB, slots * SB)
        tag = jnp.where(kept[:, None], jnp.stack([mu_block, nu_block], 1), 0).reshape(-1)
        tag = jnp.zeros((n_pair, TAG, LANES), jnp.bfloat16).at[:, :, : 2 * slots].set(tag.astype(jnp.bfloat16))
        packed = jnp.concatenate([tiles, tag], 1)
        line = lax.all_to_all(packed, "pair", split_axis=0, concat_axis=0, tiled=True)
        gathered = lax.all_gather(coeff, ("pair", "orb"), axis=0, tiled=True)
        pieces, came = [lax.all_gather(line, "orb", axis=0, tiled=True), gathered], None
    out = transform(came, n_orb, n_pair * n_orb, orbitals, pieces)
    out = out.reshape(orbitals // n_orb, orbitals // LANES, columns, LANES)
    return out.transpose(0, 2, 1, 3).reshape(orbitals // n_orb, columns, orbitals)


def solution(mesh):
    placed = (
        P(("grp", "pair", "orb"), None, None),
        P(("grp", "pair", "orb")),
        P(("grp", "pair", "orb")),
        P(("grp", "pair", "orb")),
        P(("grp", "pair", "orb"), None),
    )
    return jax.shard_map(
        functools.partial(body, mesh.shape["pair"], mesh.shape["orb"]),
        mesh=mesh,
        in_specs=placed,
        out_specs=P(("grp", "orb"), "pair", None),
        check_vma=False,
    )
```

```python
import functools

import jax
import jax.numpy as jnp
from jax import lax
from jax.experimental import pallas as pl
from jax.experimental.pallas import tpu as pltpu
from jax.sharding import PartitionSpec as P

SB = 64
LANES = 128
TAG = 16
CHUNK = 16


def pack_kernel(n_pair, integrals, mu, nu, counts, coeff, *refs):
    outs = refs[:n_pair]
    tiles, shard, mu_in, nu_in, spread, woven, sems = refs[n_pair:]
    p = lax.axis_index("pair")
    copies = [
        pltpu.make_async_copy(source, target, sems.at[n])
        for n, (source, target) in enumerate(((integrals, tiles), (mu, mu_in), (nu, nu_in), (coeff, shard)))
    ]
    for copy in copies:
        copy.start()
    slots, kets, flat = tiles.shape
    wide = flat // LANES
    columns = kets // n_pair
    held, orbitals = shard.shape
    for copy in copies[1:3]:
        copy.wait()
    count = counts[0]
    lane = lax.broadcasted_iota(jnp.int32, (wide, LANES), 1)
    low, kept = lane < SB, lane < SB * count
    lane = lax.broadcasted_iota(jnp.int32, (TAG, LANES), 1)
    tag = jnp.zeros((TAG, LANES), jnp.int32)
    for t in range(slots):
        tag = jnp.where((lane == 2 * t) & (t < count), mu_in[t], tag)
        tag = jnp.where((lane == 2 * t + 1) & (t < count), nu_in[t], tag)
    tag = tag.astype(jnp.float32).astype(jnp.bfloat16)
    copies[0].wait()
    for t in range(slots):
        for j in range(wide):
            at = pl.ds((t * wide + j) * kets, kets)
            spread[at, :] = tiles[t, :, j * LANES : (j + 1) * LANES].astype(jnp.float32)
    tile_at, rows = orbitals // LANES * held, columns * SB
    for s in range(n_pair):
        dest = p ^ s
        for k in range(columns):
            column = dest * columns + k
            one = spread[pl.ds(column, wide, stride=kets), :]
            two = spread[pl.ds(wide * kets + column, wide, stride=kets), :]
            even = jnp.where(low, one, pltpu.roll(two, SB, axis=1))
            odd = jnp.where(low, pltpu.roll(one, SB, axis=1), two)
            begin = (s * columns + k) * SB
            woven[pl.ds(begin, wide, stride=2), :] = jnp.where(kept, even, 0.0)
            woven[pl.ds(begin + 1, wide, stride=2), :] = jnp.where(kept, odd, 0.0)
        outs[s][tile_at : tile_at + rows] = woven[pl.ds(s * rows, rows), :].astype(jnp.bfloat16)
        outs[s][tile_at + rows :] = tag
    copies[3].wait()
    for j in range(orbitals // LANES):
        lanes = shard[:, j * LANES : (j + 1) * LANES]
        for s in range(n_pair):
            outs[s][j * held : (j + 1) * held] = lanes


def pack(n_pair, integrals, mu, nu, counts, coeff):
    slots, kets, flat = integrals.shape
    rows = coeff.shape[0] * coeff.shape[1] // LANES + kets // n_pair * SB + TAG
    hbm, smem = pl.BlockSpec(memory_space=pltpu.HBM), pl.BlockSpec(memory_space=pltpu.SMEM)
    return pl.pallas_call(
        functools.partial(pack_kernel, n_pair),
        out_shape=[pltpu.VMEM((rows, LANES), jnp.bfloat16)] * n_pair,
        in_specs=[hbm, hbm, hbm, smem, hbm],
        out_specs=[pl.BlockSpec(memory_space=pltpu.VMEM)] * n_pair,
        scratch_shapes=[
            pltpu.VMEM(integrals.shape, jnp.bfloat16),
            pltpu.VMEM(coeff.shape, jnp.bfloat16),
            pltpu.SMEM(mu.shape, jnp.int32),
            pltpu.SMEM(nu.shape, jnp.int32),
            pltpu.VMEM((slots * kets * flat // LANES, LANES), jnp.float32),
            pltpu.VMEM((kets * SB, LANES), jnp.float32),
            pltpu.SemaphoreType.DMA((4,)),
        ],
        compiler_params=pltpu.CompilerParams(vmem_limit_bytes=56 << 20),
        name="pack",
    )(integrals, mu, nu, counts, coeff)


def transform_kernel(came, n_orb, orbitals, n_in, *refs):
    pieces = refs[:n_in]
    out, c_all, codes, index, half, left, sem = refs[n_in:]
    p, o = lax.axis_index("pair"), lax.axis_index("orb")
    devices = codes.shape[0]
    blocks = orbitals // LANES
    tile_at = pieces[0].shape[-2] - TAG - 2 * SB
    if came:
        for q, piece in enumerate(pieces):
            codes[q : q + 1, :] = piece[tile_at + 2 * SB :][:1].astype(jnp.float32).astype(jnp.int32)
    else:
        codes[...] = pieces[0][:, 2 * SB :, :][:, 0, :].astype(jnp.float32).astype(jnp.int32)
    to_scalars = pltpu.make_async_copy(codes, index, sem)
    to_scalars.start()
    if came:
        rows = c_all.shape[0] // devices
        for q, piece in enumerate(pieces):
            source = (p ^ came[q][0]) * n_orb + (o ^ came[q][1])
            place = pl.ds(pl.multiple_of(source * rows, rows), rows)
            for j in range(blocks):
                c_all[place, j * LANES : (j + 1) * LANES] = piece[j * rows : (j + 1) * rows, :]
    else:
        c_all = pieces[1]
    to_scalars.wait()

    mine = pl.ds(pl.multiple_of(o * LANES, LANES), LANES)
    low = lax.broadcasted_iota(jnp.int32, (SB, LANES), 1) < SB
    chunks = devices // CHUNK

    def rows_of(block):
        return pl.ds(pl.multiple_of(block * SB, SB), SB)

    def chunk_step(chunk, carry):
        part = None
        for d in range(CHUNK):
            device = chunk * CHUNK + d
            stacked = []
            for k in range(2):
                if came:
                    tile = pieces[d][tile_at + k * SB : tile_at + (k + 1) * SB, :]
                else:
                    tile = pieces[0][device, k * SB : (k + 1) * SB, :]
                stacked += [jnp.where(low, tile, jnp.zeros_like(tile)), jnp.where(low, jnp.zeros_like(tile), tile)]
            mu_one, nu_one, mu_two, nu_two = (index[device, n] for n in range(4))
            rows = jnp.concatenate([c_all[rows_of(nu_one)], c_all[rows_of(nu_two)]], 0)
            moved = jnp.dot(jnp.concatenate(stacked, 0), rows, preferred_element_type=jnp.float32)
            moved = moved.astype(jnp.bfloat16)
            at = pl.ds(d * 2 * SB, 2 * SB)
            half[at, :orbitals] = moved[: 2 * SB]
            half[at, orbitals:] = moved[2 * SB :]
            left[:, at] = jnp.concatenate([c_all[rows_of(mu_one), mine], c_all[rows_of(mu_two), mine]], 0).T
            if d % (CHUNK // 2) == CHUNK // 2 - 1:
                done = slice((d + 1 - CHUNK // 2) * 2 * SB, (d + 1) * 2 * SB)
                term = jnp.dot(left[:, done], half[done, :], preferred_element_type=jnp.float32)
                part = term if part is None else part + term
        for k in range(2):
            for j in range(blocks):
                at = pl.ds(2 * j + k, LANES, stride=2 * blocks)
                begin = k * orbitals + j * LANES
                value = part[:, begin : begin + LANES]
                out[at, :] = value if chunks == 1 else out[at, :] + value
        return carry

    if chunks == 1:
        chunk_step(0, 0)
    else:
        out[...] = jnp.zeros_like(out)
        lax.fori_loop(0, chunks, chunk_step, 0)


def transform(came, n_orb, devices, orbitals, pieces):
    wide = CHUNK * 2 * SB
    held = pieces[0].shape[0] - 2 * SB - TAG if came else TAG
    return pl.pallas_call(
        functools.partial(transform_kernel, came, n_orb, orbitals, len(pieces)),
        out_shape=jax.ShapeDtypeStruct((2 * orbitals // LANES * LANES, LANES), jnp.float32),
        in_specs=[pl.BlockSpec(memory_space=pltpu.VMEM)] * len(pieces),
        out_specs=pl.BlockSpec(memory_space=pltpu.VMEM),
        scratch_shapes=[
            pltpu.VMEM((held * LANES // orbitals * devices if came else TAG, orbitals), jnp.bfloat16),
            pltpu.VMEM((devices, LANES), jnp.int32),
            pltpu.SMEM((devices, LANES), jnp.int32),
            pltpu.VMEM((wide, 2 * orbitals), jnp.bfloat16),
            pltpu.VMEM((LANES, wide), jnp.bfloat16),
            pltpu.SemaphoreType.DMA,
        ],
        compiler_params=pltpu.CompilerParams(vmem_limit_bytes=40 << 20),
        name="transform",
    )(*pieces)


def flip(array, axis, size, bit):
    return lax.ppermute(array, axis, [(i, i ^ bit) for i in range(size)])


def body(n_pair, n_orb, integrals, mu_block, nu_block, counts, coeff):
    slots, kets, flat = integrals.shape
    columns = kets // n_pair
    orbitals = coeff.shape[1]
    if n_orb == 4 and n_pair == 4:
        packed = list(pack(n_pair, integrals, mu_block, nu_block, counts, coeff))
        lines = packed[:1] + [flip(packed[s], "pair", n_pair, s) for s in range(1, n_pair)]
        across = [flip(line, "orb", n_orb, 2) for line in lines[:3]]
        last, across[1] = lax.optimization_barrier((lines[3], across[1]))
        across.append(flip(last, "orb", n_orb, 2))
        first = list(lax.optimization_barrier((lines[0], lines[1], last)))[:2]
        swapped = [flip(piece, "orb", n_orb, 1) for piece in first]
        later = [*lax.optimization_barrier((lines[2], last)), *lax.optimization_barrier(tuple(across[:3])), across[3]]
        swapped += [flip(piece, "orb", n_orb, 1) for piece in later]
        pieces = first + later + swapped
        came = [(0, 0), (1, 0), (2, 0), (3, 0), (0, 2), (1, 2), (2, 2), (3, 2)]
        came += [(s, side ^ 1) for s, side in came]
    else:
        kept = jnp.arange(slots, dtype=jnp.int32) < counts[0]
        tiles = jnp.where(kept[:, None, None], integrals, jnp.zeros_like(integrals))
        tiles = tiles.reshape(slots, n_pair, columns, SB, SB).transpose(1, 2, 3, 0, 4)
        tiles = tiles.reshape(n_pair, columns * SB, slots * SB)
        tag = jnp.where(kept[:, None], jnp.stack([mu_block, nu_block], 1), 0).reshape(-1)
        tag = jnp.zeros((n_pair, TAG, LANES), jnp.bfloat16).at[:, :, : 2 * slots].set(tag.astype(jnp.bfloat16))
        packed = jnp.concatenate([tiles, tag], 1)
        line = lax.all_to_all(packed, "pair", split_axis=0, concat_axis=0, tiled=True)
        gathered = lax.all_gather(coeff, ("pair", "orb"), axis=0, tiled=True)
        pieces, came = [lax.all_gather(line, "orb", axis=0, tiled=True), gathered], None
    out = transform(came, n_orb, n_pair * n_orb, orbitals, pieces)
    out = out.reshape(orbitals // n_orb, orbitals // LANES, columns, LANES)
    return out.transpose(0, 2, 1, 3).reshape(orbitals // n_orb, columns, orbitals)


def solution(mesh):
    placed = (
        P(("grp", "pair", "orb"), None, None),
        P(("grp", "pair", "orb")),
        P(("grp", "pair", "orb")),
        P(("grp", "pair", "orb")),
        P(("grp", "pair", "orb"), None),
    )
    return jax.shard_map(
        functools.partial(body, mesh.shape["pair"], mesh.shape["orb"]),
        mesh=mesh,
        in_specs=placed,
        out_specs=P(("grp", "orb"), "pair", None),
        check_vma=False,
    )
```
